128 devices in a mesh: dp: 32 (over z, y, core), fsdp: 4 (over x).
Axes of the slice: x: 4, y: 4, z: 4, core: 2. Of those that a mesh axis runs over, the one named last changes fastest.
Arguments:
- enc_hidden: bfloat16 [65536, 2048], P(('dp', 'fsdp')), may hold values from -24 to 24
- kv_weights: bfloat16 [2048, 4096], P('dp', 'fsdp'), may hold values from -0.125 to 0.125
- queries: bfloat16 [65536, 2048], P(('dp', 'fsdp')), may hold values from -1000 to 1000
- cotangent: bfloat16 [65536, 2048], P(('dp', 'fsdp')), may hold values from -6 to 6
- enc_lengths: int32 [128, 4], replicated, may hold values from 1 to 160, as said below
- dec_lengths: int32 [128, 4], replicated, may hold values from 1 to 160, as said below
- dec_partner: int32 [128, 4], replicated, may hold values from 0 to 511, as said below
Outputs:
- context: bfloat16 [65536, 2048], P(('dp', 'fsdp'))
- grad_queries: bfloat16 [65536, 2048], P(('dp', 'fsdp'))
- grad_kv_weights: float32 [2048, 4096], P('dp', 'fsdp')
The draws below stay inside these ranges and needn't reach their ends.
Inputs may be any that keep to these rules, and one draw needn't show every extreme that they name: `enc_lengths`: each row sums to 512. `dec_lengths`: each row sums to 512. `dec_partner`: every encoder segment id is named exactly once. With device index = dp index * 4 + fsdp index, row b names segments of device b and of the devices with b's fsdp index whose dp index is one lower or one higher than b's, exactly one segment of each such neighbour.
All inputs are finite; a program needn't handle non-finite values.
Results may differ from the reference program's by a relative error of at most 0.034.
The reference program's roundings to bfloat16 on the way count: a program that leaves them out, or rounds other values in their place, can miss the bound.
Values may be sent and summed in bfloat16 or wider, within the bound.
No kernel may reach another device: no remote copies, remote signals or barrier semaphores. Data moves between devices by JAX's collectives and lax.ppermute only.
A program may use at most 192 MiB of HBM per device.

```python
import jax
import jax.numpy as jnp
from jax import lax

D = 2048
HEADS = 8
HEAD_DIM = 256
ENC_DEV = 512
DEC_DEV = 512
SEG_DEV = 4
INNER = 2048
ENC_MOST = 160
DEC_MOST = 160
ENC_TOKENS = 65536
DEC_TOKENS = 65536
N_DP = 32
N_FSDP = 4
DEVICES = 128


def split_lengths(key, total, most):
    rest = total - most
    spare = SEG_DEV - 1
    base = rest // spare
    extra = rest % spare
    tail = base + (jnp.arange(spare, dtype=jnp.int32) < extra).astype(jnp.int32)
    single = jnp.concatenate([jnp.full((1,), most, jnp.int32), tail])
    lengths = jnp.broadcast_to(single, (DEVICES, SEG_DEV))
    move_keys = jax.random.split(key, SEG_DEV)
    for position in range(1, SEG_DEV - 1):
        left_size = lengths[:, position]
        right_size = lengths[:, position + 1]
        lower_bound = -jnp.minimum(right_size - 1, most - left_size)
        upper_bound = jnp.minimum(left_size - 1, most - right_size)
        shifted_amount = jax.random.randint(move_keys[position], (DEVICES,), lower_bound, upper_bound + 1)
        lengths = lengths.at[:, position].add(-shifted_amount).at[:, position + 1].add(shifted_amount)
    return lengths.astype(jnp.int32)


def shuffle_rows(key, width):
    row_keys = jax.random.split(key, DEVICES)
    return jax.vmap(lambda single: jax.random.permutation(single, width))(row_keys).astype(jnp.int32)


def draw_plan(key):
    key_list = jax.random.split(key, 7)
    devices = jnp.arange(DEVICES, dtype=jnp.int32)
    dp_place = devices // N_FSDP
    enc_orig = split_lengths(key_list[0], ENC_DEV, ENC_MOST)
    dec_orig = split_lengths(key_list[1], DEC_DEV, DEC_MOST)
    enc_order = shuffle_rows(key_list[2], SEG_DEV)
    dec_order = shuffle_rows(key_list[3], SEG_DEV)
    enc_lengths = jnp.take_along_axis(enc_orig, enc_order, axis=1)
    dec_lengths = jnp.take_along_axis(dec_orig, dec_order, axis=1)
    enc_pos = jnp.argsort(enc_order, axis=1).astype(jnp.int32)
    coin_flip = jax.random.randint(key_list[4], (DEVICES,), 0, 2)
    coin_flip = jnp.where(dp_place == 0, 1, coin_flip)
    up_slot = jnp.where(coin_flip == 1, enc_pos[:, 0], enc_pos[:, 1])
    down_slot = jnp.where(coin_flip == 1, enc_pos[:, 1], enc_pos[:, 0])
    enc_base = devices * SEG_DEV
    lower_device = jnp.maximum(devices - N_FSDP, 0)
    upper_device = jnp.minimum(devices + N_FSDP, DEVICES - 1)
    extra_low = jnp.where(dp_place > 0, enc_base[lower_device] + up_slot[lower_device], enc_base + down_slot)
    extra_high = jnp.where(dp_place < N_DP - 1, enc_base[upper_device] + down_slot[upper_device], enc_base + up_slot)
    kept_ids = enc_base[:, None] + enc_pos[:, 2:]
    kept_ids = jnp.take_along_axis(kept_ids, shuffle_rows(key_list[5], SEG_DEV - 2), axis=1)
    pick_low = jax.random.randint(key_list[6], (DEVICES,), 0, 2)
    pick_low = jnp.where(dp_place == 1, 1, pick_low)
    first_pick = jnp.where(pick_low == 1, extra_low, extra_high)
    second_pick = jnp.where(pick_low == 1, extra_high, extra_low)
    assigned = jnp.concatenate([first_pick[:, None], second_pick[:, None], kept_ids], axis=1)
    partner = jnp.take_along_axis(assigned, dec_order, axis=1)
    return (enc_lengths.astype(jnp.int32), dec_lengths.astype(jnp.int32), partner.astype(jnp.int32))


def draw_enc_lengths(key, part):
    shared = draw_plan(key)
    return shared[0]


def draw_dec_lengths(key, part):
    shared = draw_plan(key)
    return shared[1]


def draw_dec_partner(key, part):
    shared = draw_plan(key)
    return shared[2]


def draw_queries(key, part):
    key = jax.random.fold_in(key, 29)
    base_key = jax.random.fold_in(key, 0)
    base = jax.random.normal(base_key, (DEC_TOKENS, INNER), jnp.float32)
    return jnp.clip(base, -6.0, 6.0).astype(jnp.bfloat16)


def spiked(entries, stream_key, source, target, shards_of, factor):
    def block_of(dim):
        return (jnp.arange(entries.shape[dim]) // (entries.shape[dim] // shards_of)).reshape((-1,) + (1,) * (entries.ndim - 1 - dim))

    first = jax.random.permutation(stream_key, shards_of)[block_of(target)]
    second = (block_of(target) + shards_of // 2) % shards_of
    return jnp.where((block_of(source) == first) | (block_of(source) == second), factor * entries, entries)


def level_of(key, shape, pieces, least, top_value):
    def one(axis_at, parts):
        heights = jax.random.uniform(jax.random.fold_in(jax.random.fold_in(key, 6), axis_at), (parts,), jnp.float32, least / len(pieces), top_value / len(pieces))
        return jnp.repeat(jnp.exp(heights), shape[axis_at] // parts).reshape((-1,) + (1,) * (len(shape) - axis_at - 1))

    level = one(*pieces[0])
    for cut in pieces[1:]:
        level = level * one(*cut)
    return level


def scatter_about(stream_key, extent, scale, bound, cuts=(), kind=jnp.bfloat16):
    drawn = jax.random.normal(stream_key, extent, jnp.float32) * scale
    if len(cuts) > 0:
        drawn = level_of(stream_key, extent, cuts, -0.22, 0.18) * drawn
    return jnp.clip(drawn, min=-bound, max=bound).astype(kind)


def noise_with(own_key, dims, scale, limit, pieces, heavy, kind=jnp.bfloat16):
    entries = scale * jax.random.normal(own_key, dims, jnp.float32)
    if pieces:
        entries = entries * level_of(own_key, dims, pieces, -0.22, 0.18)
    return jnp.clip(spiked(entries, jax.random.fold_in(own_key, 3), *heavy), -limit, limit).astype(kind)


def setup_inputs(seed: int = 0) -> dict:
    splits = jax.random.split(jax.random.key(seed), 8)
    return {
        "enc_hidden": noise_with(splits[0], (ENC_TOKENS, D), 1.0, 24.0, ((0, 128),), (0, 1, 128, 5.5)),
        "kv_weights": scatter_about(splits[1], (D, 2 * INNER), D ** -0.5, 0.125, ((0, 32), (1, 4))),
        "queries": draw_queries(jax.random.fold_in(splits[7], 71), 0),
        "cotangent": scatter_about(splits[3], (DEC_TOKENS, INNER), 1.0, 6.0, ((0, 128),)),
        "enc_lengths": draw_enc_lengths(jax.random.fold_in(splits[7], 71), 0),
        "dec_lengths": draw_dec_lengths(jax.random.fold_in(splits[7], 71), 0),
        "dec_partner": draw_dec_partner(jax.random.fold_in(splits[7], 71), 0),
    }


def segment_slots(lengths, token_total):
    seg_ends = jnp.cumsum(lengths).astype(jnp.int32)
    places = jnp.arange(token_total, dtype=jnp.int32)
    return jnp.sum((places[:, None] >= seg_ends[None, :]).astype(jnp.int32), axis=1).astype(jnp.int32)


def attend(query_rows, upstream, key_rows, key_alive):
    seg_total, row_total, inner_width = query_rows.shape
    key_total = key_rows.shape[1]
    score_scale = HEAD_DIM ** -0.5
    query_heads = query_rows.astype(jnp.float32).reshape(seg_total, row_total, HEADS, HEAD_DIM)
    key_heads = key_rows[:, :, :inner_width].astype(jnp.float32).reshape(seg_total, key_total, HEADS, HEAD_DIM)
    value_heads = key_rows[:, :, inner_width:].astype(jnp.float32).reshape(seg_total, key_total, HEADS, HEAD_DIM)
    upstream_heads = upstream.astype(jnp.float32).reshape(seg_total, row_total, HEADS, HEAD_DIM)
    scores = jnp.einsum("sqhd,skhd->shqk", query_heads, key_heads) * score_scale
    allowed = key_alive[:, None, None, :]
    top_score = jnp.max(jnp.where(allowed, scores, -jnp.inf), axis=3, keepdims=True)
    exponent = jnp.where(allowed, jnp.exp(scores - top_score), 0.0)
    weights = exponent / jnp.sum(exponent, axis=3, keepdims=True)
    weights_low = weights.astype(jnp.bfloat16).astype(jnp.float32)
    context = jnp.einsum("shqk,skhd->sqhd", weights_low, value_heads)
    grad_weights = jnp.einsum("sqhd,skhd->shqk", upstream_heads, value_heads)
    row_delta = jnp.sum(weights * grad_weights, axis=3, keepdims=True)
    grad_scores = (weights * (grad_weights - row_delta) * score_scale).astype(jnp.bfloat16).astype(jnp.float32)
    grad_query = jnp.einsum("shqk,skhd->sqhd", grad_scores, key_heads)
    grad_key = jnp.einsum("shqk,sqhd->skhd", grad_scores, query_heads)
    grad_value = jnp.einsum("shqk,sqhd->skhd", weights_low, upstream_heads)
    grad_pair = jnp.concatenate([grad_key.reshape(seg_total, key_total, inner_width),
                                 grad_value.reshape(seg_total, key_total, inner_width)], axis=2)
    return (context.reshape(seg_total, row_total, inner_width).astype(jnp.bfloat16),
            grad_query.reshape(seg_total, row_total, inner_width).astype(jnp.bfloat16),
            grad_pair.astype(jnp.bfloat16))


def reference(enc_hidden, kv_weights, queries, cotangent, enc_lengths, dec_lengths, dec_partner):
    stacked = jnp.concatenate([queries, cotangent], axis=1)
    flat_partner = dec_partner.reshape(-1)
    seg_total = flat_partner.shape[0]
    dec_place = jnp.zeros((seg_total,), jnp.int32).at[flat_partner].set(jnp.arange(seg_total, dtype=jnp.int32))
    dec_begins = (jnp.cumsum(dec_lengths, axis=1).astype(jnp.int32) - dec_lengths
                  + jnp.arange(DEVICES, dtype=jnp.int32)[:, None] * DEC_DEV).reshape(-1).astype(jnp.int32)
    dec_sizes = dec_lengths.reshape(-1)
    enc_offsets = jnp.arange(ENC_MOST, dtype=jnp.int32)
    dec_offsets = jnp.arange(DEC_MOST, dtype=jnp.int32)
    token_places = jnp.arange(ENC_DEV, dtype=jnp.int32)

    def one_device(carry, device):
        weight_sum, context_all, grad_query_all = carry
        hidden_block = lax.dynamic_slice_in_dim(enc_hidden, (device * ENC_DEV).astype(jnp.int32), ENC_DEV, 0)
        key_block = jnp.dot(hidden_block, kv_weights, preferred_element_type=jnp.float32).astype(jnp.bfloat16)
        lengths_row = lax.dynamic_index_in_dim(enc_lengths, device, 0, keepdims=False)
        enc_starts = (jnp.cumsum(lengths_row).astype(jnp.int32) - lengths_row).astype(jnp.int32)
        key_index = enc_starts[:, None] + enc_offsets[None, :]
        key_alive = enc_offsets[None, :] < lengths_row[:, None]
        key_rows = key_block[jnp.minimum(key_index, ENC_DEV - 1)]
        places = lax.dynamic_slice_in_dim(dec_place, (device * SEG_DEV).astype(jnp.int32), SEG_DEV, 0)
        query_index = (dec_begins[places][:, None] + dec_offsets[None, :]).astype(jnp.int32)
        query_alive = dec_offsets[None, :] < dec_sizes[places][:, None]
        query_rows = jnp.where(query_alive[:, :, None], stacked[jnp.minimum(query_index, DEC_TOKENS - 1)],
                               jnp.zeros((), stacked.dtype))
        context, grad_query, grad_pair = attend(query_rows[:, :, :INNER], query_rows[:, :, INNER:], key_rows, key_alive)
        token_slots = segment_slots(lengths_row, ENC_DEV)
        home = (token_slots * ENC_MOST + token_places - enc_starts[token_slots]).astype(jnp.int32)
        grad_block = grad_pair.reshape(-1, 2 * INNER)[home]
        product = lax.dot_general(hidden_block, grad_block, (((0,), (0,)), ((), ())), preferred_element_type=jnp.float32)
        rounded = lax.optimization_barrier(product.astype(jnp.bfloat16))
        targets = jnp.where(query_alive, query_index, DEC_TOKENS).reshape(-1).astype(jnp.int32)
        context_all = context_all.at[targets].set(context.reshape(-1, INNER), mode="drop")
        grad_query_all = grad_query_all.at[targets].set(grad_query.reshape(-1, INNER), mode="drop")
        return (weight_sum + rounded.astype(jnp.float32), context_all, grad_query_all), None

    initial = (jnp.zeros((D, 2 * INNER), jnp.float32),
               jnp.zeros((DEC_TOKENS, INNER), jnp.bfloat16),
               jnp.zeros((DEC_TOKENS, INNER), jnp.bfloat16))
    final, unused = lax.scan(one_device, initial, jnp.arange(DEVICES, dtype=jnp.int32))
    grad_kv_weights, context_all, grad_query_all = final
    return context_all, grad_query_all, grad_kv_weights
```

```python
import jax
import jax.numpy as jnp
from jax import lax
from jax.experimental import pallas as pl
from jax.experimental.pallas import tpu as pltpu
from jax.sharding import Mesh, PartitionSpec as P

HEADS = 8
HEAD_DIM = 256
SEGS = 4
TOK = 512
PAIR = 2 * TOK
WIN = 176
POOL = PAIR + 2 * WIN
D = 2048
CHIP = ("z", "y", "x")
ALL = ("z", "y", "c", "x")


def align(start, limit):
    return jnp.minimum((start // 16) * 16, limit - WIN)


def kernel(meta, x_ref, xt_ref, wk_ref, wv_ref, q_ref, ct_ref, ctx_ref, gq_ref, dw_ref, k_s, v_s, gk_s, gv_s):
    scale = HEAD_DIM ** -0.5
    x = x_ref[...]
    k_s[...] = jnp.dot(
        x, wk_ref[...].reshape(D, HEAD_DIM), preferred_element_type=jnp.float32
    ).astype(jnp.bfloat16)
    v_s[...] = jnp.dot(
        x, wv_ref[...].reshape(D, HEAD_DIM), preferred_element_type=jnp.float32
    ).astype(jnp.bfloat16)

    def mm(a, b, dims):
        return lax.dot_general(a, b, (dims, ((), ())), preferred_element_type=jnp.float32)

    col = lax.broadcasted_iota(jnp.int32, (WIN, WIN), 1)
    row = lax.broadcasted_iota(jnp.int32, (WIN, WIN), 0)
    row_wide = lax.broadcasted_iota(jnp.int32, (WIN, HEAD_DIM), 0)
    for e in range(2 * SEGS):
        es, el, ds, dl = meta[e, 0], meta[e, 1], meta[e, 2], meta[e, 3]
        ew = pl.multiple_of(align(es, PAIR), 16)
        dw = pl.multiple_of(align(ds, POOL), 16)
        elo, dlo = es - ew, ds - dw
        ewin, dwin = pl.ds(ew, WIN), pl.ds(dw, WIN)
        k, v = k_s[ewin, :], v_s[ewin, :]
        q, ct = q_ref[dwin, :], ct_ref[dwin, :]
        s = mm(q, k, ((1,), (1,))) * scale
        gw = mm(ct, v, ((1,), (1,)))
        k_live = (col >= elo) & (col < elo + el)
        live = k_live & (row >= dlo) & (row < dlo + dl)
        top = jnp.max(jnp.where(k_live, s, -jnp.inf), axis=1, keepdims=True)
        p = jnp.where(k_live, jnp.exp(s - top), 0.0)
        total = jnp.sum(p, axis=1, keepdims=True)
        w = jnp.where(live, p * (1.0 / total), 0.0)
        w_low = w.astype(jnp.bfloat16)
        delta = jnp.sum(w * gw, axis=1, keepdims=True)
        gs = (w * (gw - delta) * scale).astype(jnp.bfloat16)
        ctx = mm(w_low, v, ((1,), (0,))).astype(jnp.bfloat16)
        gq = mm(gs, k, ((1,), (0,))).astype(jnp.bfloat16)
        gk = mm(gs, q, ((0,), (0,))).astype(jnp.bfloat16)
        gv = mm(w_low, ct, ((0,), (0,))).astype(jnp.bfloat16)
        d_in = (row_wide >= dlo) & (row_wide < dlo + dl)
        e_in = (row_wide >= elo) & (row_wide < elo + el)
        ctx_ref[dwin, :] = jnp.where(d_in, ctx, ctx_ref[dwin, :])
        gq_ref[dwin, :] = jnp.where(d_in, gq, gq_ref[dwin, :])
        gk_s[ewin, :] = jnp.where(e_in, gk, gk_s[ewin, :])
        gv_s[ewin, :] = jnp.where(e_in, gv, gv_s[ewin, :])
    xt = xt_ref[...]
    dw_ref[:, 0, 0] = (
        jnp.dot(xt, gk_s[...], preferred_element_type=jnp.float32)
        .astype(jnp.bfloat16)
        .reshape(16, 128, HEAD_DIM)
    )
    dw_ref[:, 1, 0] = (
        jnp.dot(xt, gv_s[...], preferred_element_type=jnp.float32)
        .astype(jnp.bfloat16)
        .reshape(16, 128, HEAD_DIM)
    )


def run_kernel(meta, x, xt, weights, pool, core):
    col_of = core.reshape(1).astype(jnp.int32)

    def wrap(meta, core_ref, *refs):
        kernel(meta, *refs)

    grid_spec = pltpu.PrefetchScalarGridSpec(
        num_scalar_prefetch=2,
        grid=(4,),
        in_specs=[
            pl.BlockSpec((PAIR, D), lambda i, m, c: (0, 0)),
            pl.BlockSpec((D, PAIR), lambda i, m, c: (0, 0)),
            pl.BlockSpec((32, 1, 64, HEAD_DIM), lambda i, m, c: (0, i // 2, 0, c[0] * 2 + i % 2)),
            pl.BlockSpec((32, 1, 64, HEAD_DIM), lambda i, m, c: (0, 2 + i // 2, 0, c[0] * 2 + i % 2)),
            pl.BlockSpec((POOL, HEAD_DIM), lambda i, m, c: (0, i)),
            pl.BlockSpec((POOL, HEAD_DIM), lambda i, m, c: (0, 4 + i)),
        ],
        out_specs=[
            pl.BlockSpec((POOL, HEAD_DIM), lambda i, m, c: (0, i)),
            pl.BlockSpec((POOL, HEAD_DIM), lambda i, m, c: (0, i)),
            pl.BlockSpec((16, 2, 1, 128, HEAD_DIM), lambda i, m, c: (0, 0, i // 2, 0, i % 2)),
        ],
        scratch_shapes=[pltpu.VMEM((PAIR, HEAD_DIM), jnp.bfloat16)] * 4,
    )
    return pl.pallas_call(
        wrap,
        grid_spec=grid_spec,
        out_shape=[
            jax.ShapeDtypeStruct((POOL, 4 * HEAD_DIM), jnp.bfloat16),
            jax.ShapeDtypeStruct((POOL, 4 * HEAD_DIM), jnp.bfloat16),
            jax.ShapeDtypeStruct((16, 2, 2, 128, 512), jnp.bfloat16),
        ],
        compiler_params=pltpu.CompilerParams(vmem_limit_bytes=50 * 1024 * 1024),
        cost_estimate=pl.CostEstimate(flops=25_000_000_000, bytes_accessed=40_000_000, transcendentals=1_000_000),
    )(meta, col_of, x, xt, weights, weights, pool, pool)


def swap(value):
    return lax.ppermute(value, "c", [(0, 1), (1, 0)])


def send_up(value):
    return lax.ppermute(value, ("z", "y"), [(i, i + 1) for i in range(15)])


def send_down(value):
    return lax.ppermute(value, ("z", "y"), [(i + 1, i) for i in range(15)])


def plan(enc_lengths, dec_lengths, dec_partner, t, c, x):
    cores = jnp.stack([c, 1 - c])
    devices = (t * 2 + cores) * 4 + x
    ids = (devices[:, None] * SEGS + jnp.arange(SEGS, dtype=jnp.int32)).reshape(-1)
    dec_starts = (jnp.cumsum(dec_lengths, axis=1) - dec_lengths).reshape(-1)
    enc_starts = (jnp.cumsum(enc_lengths, axis=1) - enc_lengths).reshape(-1)
    places = jnp.arange(ids.shape[0] * 0 + enc_starts.shape[0], dtype=jnp.int32)
    own = places[None, :] == ids[:, None]
    hit = dec_partner.reshape(-1)[None, :] == ids[:, None]

    def pick(mask, table):
        return jnp.sum(jnp.where(mask, table[None, :], 0), axis=1)

    enc_len = pick(own, enc_lengths.reshape(-1))
    enc_start = pick(own, enc_starts) + jnp.repeat(jnp.arange(2, dtype=jnp.int32) * TOK, SEGS)
    dec_len = pick(hit, dec_lengths.reshape(-1))
    dec_start = pick(hit, dec_starts)
    owner_dp = pick(hit, places) // (SEGS * 4)
    base = jnp.where(owner_dp % 2 == c, 0, TOK)
    in_pool = base + dec_start
    window = align(in_pool, PAIR)
    chip = owner_dp // 2
    dec_at = jnp.where(
        chip == t,
        in_pool,
        in_pool - window + jnp.where(chip < t, PAIR, PAIR + WIN),
    )
    meta = jnp.stack([enc_start, enc_len, dec_at, dec_len], axis=1).astype(jnp.int32)

    def leaving(core, step):
        device = (t * 2 + core) * 4 + x
        at = places // SEGS == device
        goes = at & (dec_partner.reshape(-1) // (SEGS * 4) == t * 2 + core + step)
        length = jnp.sum(jnp.where(goes, dec_lengths.reshape(-1), 0))
        start = jnp.sum(jnp.where(goes, dec_starts, 0)) + jnp.where(core == c, 0, TOK)
        return start, length, align(start, PAIR)

    return meta, leaving(0, -1), leaving(1, 1)


def body(enc_hidden, kv_weights, queries, cotangent, enc_lengths, dec_lengths, dec_partner):
    z, y, c, x = (lax.axis_index(a) for a in ALL)
    t = z * 4 + y
    weights = lax.all_gather(kv_weights, ALL, axis=0).reshape(32, 4, 64, 1024)
    meta, below, above = plan(enc_lengths, dec_lengths, dec_partner, t, c, x)

    tokens = jnp.concatenate([enc_hidden, swap(enc_hidden)], axis=0)
    tokens_t = tokens.T
    stacked = jnp.concatenate([queries, cotangent], axis=1).reshape(TOK, 4, 2, 512)
    mine = lax.dynamic_index_in_dim(stacked, c, 2, keepdims=False).reshape(TOK, 2048)
    other = lax.dynamic_index_in_dim(stacked, 1 - c, 2, keepdims=False).reshape(TOK, 2048)
    pair = jnp.concatenate([mine, swap(other)], axis=0)
    to_below = lax.dynamic_slice_in_dim(pair, below[2], WIN, 0)
    to_above = lax.dynamic_slice_in_dim(pair, above[2], WIN, 0)
    pool = jnp.concatenate([pair, send_up(to_above), send_down(to_below)], axis=0)

    ctx, gq, dw = run_kernel(meta, tokens, tokens_t, weights, pool, c)

    parts = lax.all_to_all(dw.reshape(64, 128, 512), CHIP, 0, 0, tiled=True)
    summed = jnp.sum(parts.astype(jnp.float32), axis=0).reshape(2, 64, 512)
    kept = lax.dynamic_index_in_dim(summed, c, 0, keepdims=False)
    got = swap(lax.dynamic_index_in_dim(summed, 1 - c, 0, keepdims=False))
    grad = jnp.where(
        c == 0, jnp.concatenate([kept, got], axis=1), jnp.concatenate([got, kept], axis=1)
    )

    both = jnp.concatenate([ctx, gq], axis=1)
    from_above = send_down(both[PAIR : PAIR + WIN])
    from_below = send_up(both[PAIR + WIN :])
    out = both[:PAIR]
    offsets = jnp.arange(WIN, dtype=jnp.int32)[:, None]
    for (start, length, window), got in ((below, from_below), (above, from_above)):
        inside = (offsets + window >= start) & (offsets + window < start + length)
        now = lax.dynamic_slice_in_dim(out, window, WIN, 0)
        out = lax.dynamic_update_slice_in_dim(out, jnp.where(inside, got, now), window, 0)
    theirs = swap(out[TOK:]).reshape(TOK, 4, 1, 512)
    ours = out[:TOK].reshape(TOK, 4, 1, 512)
    full = jnp.where(
        c == 0, jnp.concatenate([ours, theirs], axis=2), jnp.concatenate([theirs, ours], axis=2)
    ).reshape(TOK, 4096)
    return full[:, :2048], full[:, 2048:], grad


def solution(mesh):
    fine = Mesh(mesh.devices.reshape(4, 4, 2, 4), ALL)
    rows = P(ALL, None)
    cut = P(("z", "y", "c"), "x")
    return jax.shard_map(
        body,
        mesh=fine,
        in_specs=(rows, cut, rows, rows, P(), P(), P()),
        out_specs=(rows, rows, cut),
        check_vma=False,
    )
```

```python
import jax
import jax.numpy as jnp
from jax import lax
from jax.experimental import pallas as pl
from jax.experimental.pallas import tpu as pltpu
from jax.sharding import Mesh, PartitionSpec as P

HEAD_DIM = 256
SEGS = 4
TOK = 512
PAIR = 2 * TOK
WIN = 176
POOL = PAIR + 2 * WIN
D = 2048
HALF = 512
DP = ("z", "y", "c")
ALL = ("z", "y", "c", "x")
MIB = 1024 * 1024
BF = jnp.bfloat16


def align(start, limit):
    return jnp.minimum((start // 16) * 16, limit - WIN)


def mm(a, b, dims):
    return lax.dot_general(a, b, (dims, ((), ())), preferred_element_type=jnp.float32)


def attend(meta, k_s, v_s, q_s, ct_s, ctx_s, gq_s, gk_s, gv_s):
    scale = HEAD_DIM ** -0.5
    col = lax.broadcasted_iota(jnp.int32, (WIN, WIN), 1)
    row = lax.broadcasted_iota(jnp.int32, (WIN, WIN), 0)
    row_wide = lax.broadcasted_iota(jnp.int32, (WIN, HEAD_DIM), 0)
    for e in range(2 * SEGS):
        es, el, ds, dl = meta[e, 0], meta[e, 1], meta[e, 2], meta[e, 3]
        ew = pl.multiple_of(align(es, PAIR), 16)
        dw = pl.multiple_of(align(ds, POOL), 16)
        elo, dlo = es - ew, ds - dw
        ewin, dwin = pl.ds(ew, WIN), pl.ds(dw, WIN)
        k, v = k_s[ewin, :], v_s[ewin, :]
        q, ct = q_s[dwin, :], ct_s[dwin, :]
        s = mm(q, k, ((1,), (1,))) * scale
        gw = mm(ct, v, ((1,), (1,)))
        k_live = (col >= elo) & (col < elo + el)
        live = k_live & (row >= dlo) & (row < dlo + dl)
        top = jnp.max(jnp.where(k_live, s, -jnp.inf), axis=1, keepdims=True)
        p = jnp.where(k_live, jnp.exp(s - top), 0.0)
        total = jnp.sum(p, axis=1, keepdims=True)
        w = jnp.where(live, p * (1.0 / total), 0.0)
        w_low = w.astype(BF)
        delta = jnp.sum(w * gw, axis=1, keepdims=True)
        gs = (w * (gw - delta) * scale).astype(BF)
        ctx = mm(w_low, v, ((1,), (0,))).astype(BF)
        gq = mm(gs, k, ((1,), (0,))).astype(BF)
        gk = mm(gs, q, ((0,), (0,))).astype(BF)
        gv = mm(w_low, ct, ((0,), (0,))).astype(BF)
        d_in = (row_wide >= dlo) & (row_wide < dlo + dl)
        e_in = (row_wide >= elo) & (row_wide < elo + el)
        ctx_s[dwin, :] = jnp.where(d_in, ctx, ctx_s[dwin, :])
        gq_s[dwin, :] = jnp.where(d_in, gq, gq_s[dwin, :])
        gk_s[ewin, :] = jnp.where(e_in, gk, gk_s[ewin, :])
        gv_s[ewin, :] = jnp.where(e_in, gv, gv_s[ewin, :])


def places(me):
    z, y, c, x = me[0], me[1], me[2], me[3]

    def block(ra, rb, rc):
        first = c == 0
        bx = (x + jnp.where(first, ra, rb)) & 3
        by = (y + jnp.where(first, rb, rc)) & 3
        bz = (z + jnp.where(first, rc, ra)) & 3
        return bx, bz * 4 + by

    return block


def main_kernel(meta, me, x_ref, xt_ref, wk_ref, wv_ref, qm, qo, qa, qb, cm, co, ca, cb,
                om, oo, oa, ob, d0, d1, d2, d3,
                k_s, v_s, gk_s, gv_s, q_s, ct_s, ctx_s, gq_s, dw_s):
    step = pl.program_id(0)
    x = x_ref[...]
    k_s[...] = jnp.dot(x, wk_ref[...].reshape(D, HEAD_DIM), preferred_element_type=jnp.float32).astype(BF)
    v_s[...] = jnp.dot(x, wv_ref[...].reshape(D, HEAD_DIM), preferred_element_type=jnp.float32).astype(BF)
    for pool, parts in ((q_s, (qm, qo, qa, qb)), (ct_s, (cm, co, ca, cb))):
        pool[0:TOK, :] = parts[0][...]
        pool[TOK:PAIR, :] = parts[1][...]
        pool[PAIR : PAIR + WIN, :] = parts[2][...]
        pool[PAIR + WIN :, :] = parts[3][...]
    attend(meta, k_s, v_s, q_s, ct_s, ctx_s, gq_s, gk_s, gv_s)
    for kind, pool in enumerate((ctx_s, gq_s)):
        om[kind] = pool[0:TOK, :]
        oo[kind] = pool[TOK:PAIR, :]
        oa[kind] = pool[PAIR : PAIR + WIN, :]
        ob[kind] = pool[PAIR + WIN :, :]
    xt = xt_ref[...]
    dw_s[step] = jnp.dot(xt, gk_s[...], preferred_element_type=jnp.float32).astype(BF)
    dw_s[2 + step] = jnp.dot(xt, gv_s[...], preferred_element_type=jnp.float32).astype(BF)

    @pl.when(step == 1)
    def _():
        block = places(me)

        def put(n, carry):
            rb, rc = n // 4, n % 4
            for ra, out in enumerate((d0, d1, d2, d3)):
                bx, bzy = block(ra, rb, rc)
                out[rb, rc] = dw_s[bx, pl.ds(pl.multiple_of(bzy * 128, 128), 128), :]
            return carry

        lax.fori_loop(0, 16, put, 0)


def run_main(chunk, meta, me, x, xt, weights, q, q_other, ct, ct_other, sent_a, sent_b):
    def fixed(*shape):
        return pl.BlockSpec(shape, lambda i, m, e: (0,) * len(shape), pipeline_mode=pl.Buffered(1))

    def wide(rows):
        return pl.BlockSpec((rows, HEAD_DIM), lambda i, m, e: (0, i * 4 + e[2] * 2 + chunk))

    def narrow(kind):
        return pl.BlockSpec((WIN, HEAD_DIM), lambda i, m, e: (0, kind * 4 + i * 2 + chunk))

    def weight(kind):
        return pl.BlockSpec((32, 1, 64, HEAD_DIM), lambda i, m, e: (0, kind * 2 + i, 0, e[2] * 2 + chunk))

    def out(rows):
        return pl.BlockSpec((2, rows, HEAD_DIM), lambda i, m, e: (0, 0, i))

    part = pl.BlockSpec((4, 4, 128, HEAD_DIM), lambda i, m, e: (0, 0, 0, 0))
    pair = pltpu.VMEM((PAIR, HEAD_DIM), BF)
    pool = pltpu.VMEM((POOL, HEAD_DIM), BF)
    return pl.pallas_call(
        main_kernel,
        grid_spec=pltpu.PrefetchScalarGridSpec(
            num_scalar_prefetch=2,
            grid=(2,),
            in_specs=[fixed(PAIR, D), fixed(D, PAIR), weight(0), weight(1),
                      wide(TOK), wide(TOK), narrow(0), narrow(0),
                      wide(TOK), wide(TOK), narrow(1), narrow(1)],
            out_specs=[out(TOK), out(TOK), out(WIN), out(WIN), part, part, part, part],
            scratch_shapes=[pair, pair, pair, pair, pool, pool, pool, pool,
                            pltpu.VMEM((4, D, HEAD_DIM), BF)],
        ),
        out_shape=[jax.ShapeDtypeStruct((2, rows, HALF), BF) for rows in (TOK, TOK, WIN, WIN)]
        + [jax.ShapeDtypeStruct((4, 4, 128, HEAD_DIM), BF)] * 4,
        compiler_params=pltpu.CompilerParams(vmem_limit_bytes=52 * MIB),
        cost_estimate=pl.CostEstimate(flops=12_000_000_000, bytes_accessed=24_000_000, transcendentals=500_000),
    )(meta, me, x, xt, weights, weights, q, q_other, sent_a, sent_b, ct, ct_other, sent_a, sent_b)


def add_kernel(*refs):
    ins, outs = refs[:4], refs[-4:]
    total = sum(ref[...].astype(jnp.float32) for ref in ins).astype(BF)
    for n, out in enumerate(outs):
        out[...] = total[n]


def add_parts(parts, after=None):
    extra = [] if after is None else [after]
    shape = parts[0].shape
    rank = len(shape)
    if rank == 4:
        grid = (4,)
        source = pl.BlockSpec((4, 1, 128, HEAD_DIM), lambda i: (0, i, 0, 0))
        target = pl.BlockSpec((1, 128, HEAD_DIM), lambda i: (i, 0, 0))
    else:
        grid = (1,)
        source = pl.BlockSpec(shape, lambda i: (0, 0, 0))
        target = pl.BlockSpec(shape[1:], lambda i: (0, 0))
    return pl.pallas_call(
        add_kernel,
        grid=grid,
        in_specs=[source] * 4 + [pl.BlockSpec(memory_space=pl.ANY)] * len(extra),
        out_specs=[target] * 4,
        out_shape=[jax.ShapeDtypeStruct(shape[1:], BF)] * 4,
        compiler_params=pltpu.CompilerParams(vmem_limit_bytes=16 * MIB),
    )(*parts, *extra)


def depart_kernel(info, q_ref, ct_ref, a_ref, b_ref):
    rows = pl.ds(pl.multiple_of(info[0], 16), WIN)
    core = info[1]
    for n in range(4):
        source = (q_ref, ct_ref)[n // 2]
        for side, out in ((core, a_ref), (1 - core, b_ref)):
            start = pl.multiple_of((n % 2) * 1024 + side * HALF, HALF)
            out[:, n * HALF : (n + 1) * HALF] = source[rows, pl.ds(start, HALF)]


def depart(info, q, ct):
    whole = pl.BlockSpec(memory_space=pltpu.VMEM)
    return pl.pallas_call(
        depart_kernel,
        in_specs=[pl.BlockSpec(memory_space=pltpu.SMEM), whole, whole],
        out_specs=[whole, whole],
        out_shape=[jax.ShapeDtypeStruct((WIN, 2048), BF)] * 2,
        compiler_params=pltpu.CompilerParams(vmem_limit_bytes=16 * MIB),
    )(info, q, ct)


def finish_kernel(info, *refs):
    ins, outs = refs[:8], refs[8:]
    win = pl.multiple_of(info[0], 16)
    core, start, length = info[1], info[2] - info[0], info[3]
    rows = pl.ds(win, WIN)
    place = lax.broadcasted_iota(jnp.int32, (WIN, HEAD_DIM), 0)
    inside = (place >= start) & (place < start + length)
    for chunk in range(2):
        mine, theirs, back_a, back_b = ins[chunk * 4 : chunk * 4 + 4]
        for side, base, back in ((core, mine, back_a), (1 - core, theirs, back_b)):
            cols = pl.ds(pl.multiple_of(side * HALF + chunk * HEAD_DIM, HEAD_DIM), HEAD_DIM)
            for kind, out in enumerate(outs):
                out[:, cols] = base[kind]
                out[rows, cols] = jnp.where(inside, back[kind], out[rows, cols])


def finish(info, pieces):
    def source(rows):
        return pl.BlockSpec((2, rows, HEAD_DIM), lambda i, e: (0, 0, i))

    out = pl.BlockSpec((TOK, 1024), lambda i, e: (0, i))
    return pl.pallas_call(
        finish_kernel,
        grid_spec=pltpu.PrefetchScalarGridSpec(
            num_scalar_prefetch=1,
            grid=(2,),
            in_specs=[source(TOK), source(TOK), source(WIN), source(WIN)] * 2,
            out_specs=[out, out],
        ),
        out_shape=[jax.ShapeDtypeStruct((TOK, 2048), BF)] * 2,
        compiler_params=pltpu.CompilerParams(vmem_limit_bytes=32 * MIB),
    )(info, *pieces)


def swap(value):
    return lax.ppermute(value, "c", [(0, 1), (1, 0)])


SEND_A = [(2 * t, 2 * t - 2) for t in range(1, 16)] + [(2 * t + 1, 2 * t + 3) for t in range(15)]
SEND_B = [(2 * t, 2 * t - 1) for t in range(1, 16)] + [(2 * t + 1, 2 * t + 2) for t in range(15)]


def back(pairs):
    return [(b, a) for a, b in pairs]


def shift(phase, amount):
    pairs = []
    for z in range(4):
        for y in range(4):
            for c in range(2):
                for x in range(4):
                    to = {"z": z, "y": y, "x": x}
                    axis = ("xyz", "zxy")[c][phase]
                    to[axis] = (to[axis] + amount) % 4
                    pairs.append((((z * 4 + y) * 2 + c) * 4 + x, ((to["z"] * 4 + to["y"]) * 2 + c) * 4 + to["x"]))
    return pairs


def exchange(parts, phase):
    return [parts[0]] + [lax.ppermute(parts[r], ALL, shift(phase, r)) for r in (1, 3, 2)]


def plan(enc_lengths, dec_lengths, dec_partner, t, c, x):
    device = (t * 2 + c) * 4 + x
    cores = jnp.stack([c, 1 - c])
    devices = (t * 2 + cores) * 4 + x
    ids = (devices[:, None] * SEGS + jnp.arange(SEGS, dtype=jnp.int32)).reshape(-1)
    dec_starts = (jnp.cumsum(dec_lengths, axis=1) - dec_lengths).reshape(-1)
    enc_starts = (jnp.cumsum(enc_lengths, axis=1) - enc_lengths).reshape(-1)
    flat_dec = dec_lengths.reshape(-1)
    flat_partner = dec_partner.reshape(-1)
    entries = jnp.arange(enc_starts.shape[0], dtype=jnp.int32)
    own = entries[None, :] == ids[:, None]
    hit = flat_partner[None, :] == ids[:, None]

    def pick(mask, table):
        return jnp.sum(jnp.where(mask, table[None, :], 0), axis=1)

    enc_len = pick(own, enc_lengths.reshape(-1))
    enc_start = pick(own, enc_starts) + jnp.repeat(jnp.arange(2, dtype=jnp.int32) * TOK, SEGS)
    dec_len = pick(hit, flat_dec)
    dec_start = pick(hit, dec_starts)
    owner = pick(hit, entries) // (SEGS * 4)
    same = owner % 2 == c
    dec_at = jnp.where(
        owner // 2 == t,
        dec_start + jnp.where(same, 0, TOK),
        dec_start - align(dec_start, TOK) + PAIR + jnp.where(same, 0, WIN),
    )
    meta = jnp.stack([enc_start, enc_len, dec_at, dec_len], axis=1).astype(jnp.int32)

    goes = (entries // SEGS == device) & (flat_partner // (SEGS * 4) == t * 2 + c + jnp.where(c == 0, -1, 1))
    length = jnp.sum(jnp.where(goes, flat_dec, 0))
    start = jnp.sum(jnp.where(goes, dec_starts, 0))
    info = jnp.stack([align(start, TOK), c, start, length]).astype(jnp.int32)
    return meta, info


def body(enc_hidden, kv_weights, queries, cotangent, enc_lengths, dec_lengths, dec_partner):
    z, y, c, x = (lax.axis_index(a) for a in ALL)
    me = jnp.stack([z, y, c, x]).astype(jnp.int32)
    weights = lax.all_gather(kv_weights, ALL, axis=0).reshape(32, 4, 64, 1024)
    meta, info = plan(enc_lengths, dec_lengths, dec_partner, z * 4 + y, c, x)
    leave_a, leave_b = depart(info, queries, cotangent)
    sent_a = lax.ppermute(leave_a, DP, SEND_A)
    sent_b = lax.ppermute(leave_b, DP, SEND_B)
    tokens = jnp.concatenate([enc_hidden, swap(enc_hidden)], axis=0)
    tokens_t = tokens.T
    q_other, ct_other = swap(queries), swap(cotangent)

    pieces, grads = [], []
    for chunk in range(2):
        mine, other, far_a, far_b, *parts = run_main(
            chunk, meta, me, tokens, tokens_t, weights, queries, q_other, cotangent, ct_other, sent_a, sent_b
        )
        grads.append(exchange(parts, 0))
        pieces += [mine, swap(other), lax.ppermute(far_a, DP, back(SEND_A)), lax.ppermute(far_b, DP, back(SEND_B))]

    last = []
    for chunk, parts in enumerate(grads):
        after = grads[1][0] if chunk == 0 else None
        second = exchange(add_parts(parts, after), 1)
        last.append(exchange(add_parts(second), 2))
    summed = jnp.concatenate(
        [sum(part.astype(jnp.float32) for part in parts) for parts in last], axis=1
    )
    low, high = summed[:64], summed[64:]
    got = swap(jnp.where(c == 0, high, low))
    kept = jnp.where(c == 0, low, high)
    grad = jnp.concatenate([jnp.where(c == 0, kept, got), jnp.where(c == 0, got, kept)], axis=1)
    context, grad_queries = finish(info, pieces)
    return context, grad_queries, grad


def solution(mesh):
    fine = Mesh(mesh.devices.reshape(4, 4, 2, 4), ALL)
    rows = P(ALL, None)
    cut = P(DP, "x")
    return jax.shard_map(
        body,
        mesh=fine,
        in_specs=(rows, cut, rows, rows, P(), P(), P()),
        out_specs=(rows, rows, cut),
        check_vma=False,
    )
```

```python
import jax
import jax.numpy as jnp
from jax import lax
from jax.experimental import pallas as pl
from jax.experimental.pallas import tpu as pltpu
from jax.sharding import Mesh, PartitionSpec as P

HEAD_DIM = 256
SEGS = 4
TOK = 512
PAIR = 2 * TOK
WIN = 176
POOL = PAIR + 2 * WIN
D = 2048
HALF = 512
GROUP = 4
DP = ("z", "y", "c")
ALL = ("z", "y", "c", "x")
MIB = 1024 * 1024
BF = jnp.bfloat16


def align(start, limit):
    return jnp.minimum((start // 16) * 16, limit - WIN)


def mm(a, b, dims):
    return lax.dot_general(a, b, (dims, ((), ())), preferred_element_type=jnp.float32)


def attend(meta, k_s, v_s, q_s, ct_s, ctx_s, gq_s, gk_s, gv_s):
    scale = HEAD_DIM ** -0.5
    col = lax.broadcasted_iota(jnp.int32, (WIN, WIN), 1)
    row = lax.broadcasted_iota(jnp.int32, (WIN, WIN), 0)
    row_wide = lax.broadcasted_iota(jnp.int32, (WIN, HEAD_DIM), 0)
    for first in range(0, 2 * SEGS, GROUP):
        spots, loaded, scores = [], [], []
        for e in range(first, first + GROUP):
            es, el, ds, dl = meta[e, 0], meta[e, 1], meta[e, 2], meta[e, 3]
            ew = pl.multiple_of(align(es, PAIR), 16)
            dw = pl.multiple_of(align(ds, POOL), 16)
            spots.append((pl.ds(ew, WIN), pl.ds(dw, WIN), es - ew, el, ds - dw, dl))
        for ewin, dwin, *_ in spots:
            k, v, q, ct = k_s[ewin, :], v_s[ewin, :], q_s[dwin, :], ct_s[dwin, :]
            loaded.append((k, v, q, ct))
            scores.append((mm(q, k, ((1,), (1,))), mm(ct, v, ((1,), (1,)))))
        weights = []
        for (_, _, elo, el, dlo, dl), (s, gw) in zip(spots, scores):
            k_live = (col >= elo) & (col < elo + el)
            q_live = (row[:, :1] >= dlo) & (row[:, :1] < dlo + dl)
            s = jnp.where(k_live, s * scale, -jnp.inf)
            p = jnp.exp(s - jnp.max(s, axis=1, keepdims=True))
            share = jnp.where(q_live, 1.0 / jnp.sum(p, axis=1, keepdims=True), 0.0)
            w = p * share
            delta = jnp.sum(w * gw, axis=1, keepdims=True)
            weights.append((w.astype(BF), (w * (gw - delta) * scale).astype(BF)))
        results = []
        for (k, v, q, ct), (w_low, gs) in zip(loaded, weights):
            results.append((
                mm(w_low, v, ((1,), (0,))).astype(BF),
                mm(gs, k, ((1,), (0,))).astype(BF),
                mm(gs, q, ((0,), (0,))).astype(BF),
                mm(w_low, ct, ((0,), (0,))).astype(BF),
            ))
        for (ewin, dwin, elo, el, dlo, dl), (ctx, gq, gk, gv) in zip(spots, results):
            d_in = (row_wide >= dlo) & (row_wide < dlo + dl)
            e_in = (row_wide >= elo) & (row_wide < elo + el)
            ctx_s[dwin, :] = jnp.where(d_in, ctx, ctx_s[dwin, :])
            gq_s[dwin, :] = jnp.where(d_in, gq, gq_s[dwin, :])
            gk_s[ewin, :] = jnp.where(e_in, gk, gk_s[ewin, :])
            gv_s[ewin, :] = jnp.where(e_in, gv, gv_s[ewin, :])


def places(me):
    z, y, c, x = me[0], me[1], me[2], me[3]

    def block(ra, rb, rc):
        first = c == 0
        bx = (x + jnp.where(first, ra, rb)) & 3
        by = (y + jnp.where(first, rb, rc)) & 3
        bz = (z + jnp.where(first, rc, ra)) & 3
        return bx, bz * 4 + by

    return block


def main_kernel(meta, me, x_ref, xt_ref, w0, w1, w3, w2a, w2b, qm, qo, qa, qb, cm, co, ca, cb,
                om, oo, oa, ob, d0, d1, d2, d3,
                k_s, v_s, gk_s, gv_s, q_s, ct_s, ctx_s, gq_s, dw_s, w_s):
    step = pl.program_id(0)
    block = places(me)

    @pl.when(step == 0)
    def _():
        def take(rc, carry):
            for rb in range(4):
                far = w2a[rb, rc] if rb < 2 else w2b[rb - 2, rc]
                for ra, value in enumerate((w0[rb, rc], w1[rb, rc], far, w3[rb, rc])):
                    bx, bzy = block(ra, rb, rc)
                    w_s[bx, pl.ds(pl.multiple_of(bzy * 128, 128), 128), :] = value
            return carry

        lax.fori_loop(0, 4, take, 0)

    x = x_ref[...]
    k_s[...] = jnp.dot(x, w_s[step], preferred_element_type=jnp.float32).astype(BF)
    v_s[...] = jnp.dot(x, w_s[2 + step], preferred_element_type=jnp.float32).astype(BF)
    for pool, parts in ((q_s, (qm, qo, qa, qb)), (ct_s, (cm, co, ca, cb))):
        pool[0:TOK, :] = parts[0][...]
        pool[TOK:PAIR, :] = parts[1][...]
        pool[PAIR : PAIR + WIN, :] = parts[2][...]
        pool[PAIR + WIN :, :] = parts[3][...]
    attend(meta, k_s, v_s, q_s, ct_s, ctx_s, gq_s, gk_s, gv_s)
    for kind, pool in enumerate((ctx_s, gq_s)):
        om[kind] = pool[0:TOK, :]
        oo[kind] = pool[TOK:PAIR, :]
        oa[kind] = pool[PAIR : PAIR + WIN, :]
        ob[kind] = pool[PAIR + WIN :, :]
    xt = xt_ref[...]
    dw_s[step] = jnp.dot(xt, gk_s[...], preferred_element_type=jnp.float32).astype(BF)
    dw_s[2 + step] = jnp.dot(xt, gv_s[...], preferred_element_type=jnp.float32).astype(BF)

    @pl.when(step == 1)
    def _():
        def put(n, carry):
            rb, rc = n // 4, n % 4
            for ra, out in enumerate((d0, d1, d2, d3)):
                bx, bzy = block(ra, rb, rc)
                out[rb, rc] = dw_s[bx, pl.ds(pl.multiple_of(bzy * 128, 128), 128), :]
            return carry

        lax.fori_loop(0, 16, put, 0)


def run_main(chunk, meta, me, x, xt, weights, q, q_other, ct, ct_other, sent_a, sent_b):
    def fixed(*shape):
        return pl.BlockSpec(shape, lambda i, m, e: (0,) * len(shape), pipeline_mode=pl.Buffered(1))

    def wide(rows):
        return pl.BlockSpec((rows, HEAD_DIM), lambda i, m, e: (0, i * 4 + e[2] * 2 + chunk))

    def narrow(kind):
        return pl.BlockSpec((WIN, HEAD_DIM), lambda i, m, e: (0, kind * 4 + i * 2 + chunk))

    def out(rows):
        return pl.BlockSpec((2, rows, HEAD_DIM), lambda i, m, e: (0, 0, i))

    part = pl.BlockSpec((4, 4, 128, HEAD_DIM), lambda i, m, e: (0, 0, 0, 0))
    pair = pltpu.VMEM((PAIR, HEAD_DIM), BF)
    pool = pltpu.VMEM((POOL, HEAD_DIM), BF)
    return pl.pallas_call(
        main_kernel,
        grid_spec=pltpu.PrefetchScalarGridSpec(
            num_scalar_prefetch=2,
            grid=(2,),
            in_specs=[fixed(PAIR, D), fixed(D, PAIR), *[fixed(*w.shape) for w in weights],
                      wide(TOK), wide(TOK), narrow(0), narrow(0),
                      wide(TOK), wide(TOK), narrow(1), narrow(1)],
            out_specs=[out(TOK), out(TOK), out(WIN), out(WIN), part, part, part, part],
            scratch_shapes=[pair, pair, pair, pair, pool, pool, pool, pool,
                            pltpu.VMEM((4, D, HEAD_DIM), BF)] + [pltpu.VMEM((4, D, HEAD_DIM), BF)],
        ),
        out_shape=[jax.ShapeDtypeStruct((2, rows, HALF), BF) for rows in (TOK, TOK, WIN, WIN)]
        + [jax.ShapeDtypeStruct((4, 4, 128, HEAD_DIM), BF)] * 4,
        compiler_params=pltpu.CompilerParams(vmem_limit_bytes=52 * MIB),
        cost_estimate=pl.CostEstimate(flops=12_000_000_000, bytes_accessed=24_000_000, transcendentals=500_000),
    )(meta, me, x, xt, *weights, q, q_other, sent_a, sent_b, ct, ct_other, sent_a, sent_b)


def add_kernel(*refs):
    ins, outs = refs[:4], refs[-4:]
    total = sum(ref[...].astype(jnp.float32) for ref in ins).astype(BF)
    for n, out in enumerate(outs):
        out[...] = total[n]


def add_parts(parts, after=None):
    extra = [] if after is None else [after]
    shape = parts[0].shape
    rank = len(shape)
    if rank == 4:
        grid = (4,)
        source = pl.BlockSpec((4, 1, 128, HEAD_DIM), lambda i: (0, i, 0, 0))
        target = pl.BlockSpec((1, 128, HEAD_DIM), lambda i: (i, 0, 0))
    else:
        grid = (1,)
        source = pl.BlockSpec(shape, lambda i: (0, 0, 0))
        target = pl.BlockSpec(shape[1:], lambda i: (0, 0))
    return pl.pallas_call(
        add_kernel,
        grid=grid,
        in_specs=[source] * 4 + [pl.BlockSpec(memory_space=pl.ANY)] * len(extra),
        out_specs=[target] * 4,
        out_shape=[jax.ShapeDtypeStruct(shape[1:], BF)] * 4,
        compiler_params=pltpu.CompilerParams(vmem_limit_bytes=16 * MIB),
    )(*parts, *extra)


def depart_kernel(me, enc_len, dec_len, partner, q_ref, ct_ref, meta, info, a_ref, b_ref):
    core, x = me[2], me[3]
    t = me[0] * 4 + me[1]

    for side in range(2):
        device = (t * 2 + (core if side == 0 else 1 - core)) * 4 + x
        start = jnp.int32(side * TOK)
        for slot in range(SEGS):
            meta[side * SEGS + slot, 0] = start
            meta[side * SEGS + slot, 1] = enc_len[device, slot]
            start = start + enc_len[device, slot]
    for n in range(4):
        info[n] = jnp.int32(0)
    info[1] = core
    for near in range(4):
        dp = t * 2 - 1 + near
        device = jnp.clip(dp, 0, 31) * 4 + x
        real = (dp >= 0) & (dp < 32)
        same = (dp & 1) == core
        start = jnp.int32(0)
        for slot in range(SEGS):
            begin, length = start, dec_len[device, slot]
            owner = partner[device, slot] >> 4
            here = real & ((owner >> 1) == t)
            window = align(begin, TOK)
            if near in (1, 2):
                at = begin + jnp.where(same, 0, TOK)
            else:
                at = begin - window + PAIR + jnp.where(same, 0, WIN)

            @pl.when(here)
            def _():
                entry = jnp.where((owner & 1) == core, 0, SEGS) + (partner[device, slot] & 3)
                meta[entry, 2] = at
                meta[entry, 3] = length

            if near in (1, 2):

                @pl.when(same & jnp.logical_not(here))
                def _():
                    info[0] = window
                    info[2] = begin
                    info[3] = length

            start = start + length

    rows = pl.ds(pl.multiple_of(info[0], 16), WIN)
    for n in range(4):
        source = (q_ref, ct_ref)[n // 2]
        for side, out in ((core, a_ref), (1 - core, b_ref)):
            begin = pl.multiple_of((n % 2) * 1024 + side * HALF, HALF)
            out[:, n * HALF : (n + 1) * HALF] = source[rows, pl.ds(begin, HALF)]


def depart(me, enc_lengths, dec_lengths, dec_partner, q, ct):
    whole = pl.BlockSpec(memory_space=pltpu.VMEM)
    scalar = pl.BlockSpec(memory_space=pltpu.SMEM)
    return pl.pallas_call(
        depart_kernel,
        in_specs=[scalar, scalar, scalar, scalar, whole, whole],
        out_specs=[scalar, scalar, whole, whole],
        out_shape=[jax.ShapeDtypeStruct((2 * SEGS, 4), jnp.int32), jax.ShapeDtypeStruct((4,), jnp.int32)]
        + [jax.ShapeDtypeStruct((WIN, 2048), BF)] * 2,
        compiler_params=pltpu.CompilerParams(vmem_limit_bytes=16 * MIB),
    )(me, enc_lengths, dec_lengths, dec_partner, q, ct)


def turn_kernel(a_ref, b_ref, x_ref, xt_ref):
    for n, ref in enumerate((a_ref, b_ref)):
        value = ref[...]
        x_ref[n * TOK : (n + 1) * TOK, :] = value
        xt_ref[:, n * TOK : (n + 1) * TOK] = value.T


def turn(a, b):
    part = pl.BlockSpec((TOK, 512), lambda i: (0, i))
    return pl.pallas_call(
        turn_kernel,
        grid=(D // 512,),
        in_specs=[part, part],
        out_specs=[pl.BlockSpec((PAIR, 512), lambda i: (0, i)), pl.BlockSpec((512, PAIR), lambda i: (i, 0))],
        out_shape=[jax.ShapeDtypeStruct((PAIR, D), BF), jax.ShapeDtypeStruct((D, PAIR), BF)],
        compiler_params=pltpu.CompilerParams(vmem_limit_bytes=16 * MIB),
    )(a, b)


def finish_kernel(info, *refs):
    ins, outs = refs[:8], refs[8:]
    win = pl.multiple_of(info[0], 16)
    core, start, length = info[1], info[2] - info[0], info[3]
    rows = pl.ds(win, WIN)
    place = lax.broadcasted_iota(jnp.int32, (WIN, HEAD_DIM), 0)
    inside = (place >= start) & (place < start + length)
    for chunk in range(2):
        mine, theirs, back_a, back_b = ins[chunk * 4 : chunk * 4 + 4]
        for side, base, back in ((core, mine, back_a), (1 - core, theirs, back_b)):
            cols = pl.ds(pl.multiple_of(side * HALF + chunk * HEAD_DIM, HEAD_DIM), HEAD_DIM)
            for kind, out in enumerate(outs):
                out[:, cols] = base[kind]
                out[rows, cols] = jnp.where(inside, back[kind], out[rows, cols])


def finish(info, pieces):
    def source(rows):
        return pl.BlockSpec((2, rows, HEAD_DIM), lambda i, e: (0, 0, i))

    out = pl.BlockSpec((TOK, 1024), lambda i, e: (0, i))
    return pl.pallas_call(
        finish_kernel,
        grid_spec=pltpu.PrefetchScalarGridSpec(
            num_scalar_prefetch=1,
            grid=(2,),
            in_specs=[source(TOK), source(TOK), source(WIN), source(WIN)] * 2,
            out_specs=[out, out],
        ),
        out_shape=[jax.ShapeDtypeStruct((TOK, 2048), BF)] * 2,
        compiler_params=pltpu.CompilerParams(vmem_limit_bytes=32 * MIB),
    )(info, *pieces)


def swap(value):
    return lax.ppermute(value, "c", [(0, 1), (1, 0)])


SEND_A = [(2 * t, 2 * t - 2) for t in range(1, 16)] + [(2 * t + 1, 2 * t + 3) for t in range(15)]
SEND_B = [(2 * t, 2 * t - 1) for t in range(1, 16)] + [(2 * t + 1, 2 * t + 2) for t in range(15)]


def back(pairs):
    return [(b, a) for a, b in pairs]


def shift(phase, amount):
    pairs = []
    for z in range(4):
        for y in range(4):
            for c in range(2):
                for x in range(4):
                    to = {"z": z, "y": y, "x": x}
                    axis = ("xyz", "zxy")[c][phase]
                    to[axis] = (to[axis] + amount) % 4
                    pairs.append((((z * 4 + y) * 2 + c) * 4 + x, ((to["z"] * 4 + to["y"]) * 2 + c) * 4 + to["x"]))
    return pairs


def exchange(parts, phase):
    return [parts[0]] + [lax.ppermute(parts[r], ALL, shift(phase, r)) for r in (1, 3, 2)]


def join_kernel(*refs):
    for n in range(4):
        refs[-1][n] = refs[n][...]


def join(parts, after):
    whole = pl.BlockSpec(memory_space=pltpu.VMEM)
    return pl.pallas_call(
        join_kernel,
        in_specs=[whole] * 4 + [pl.BlockSpec(memory_space=pl.ANY)] * len(after),
        out_specs=whole,
        out_shape=jax.ShapeDtypeStruct((4,) + parts[0].shape, BF),
        compiler_params=pltpu.CompilerParams(vmem_limit_bytes=16 * MIB),
    )(*parts, *after)


def ring(value, phase, amount):
    return lax.ppermute(value, ALL, shift(phase, -amount))


def gather(kv_weights, c):
    low, high = kv_weights[:, :HALF], kv_weights[:, HALF:]
    mine, got = jnp.where(c == 0, low, high), swap(jnp.where(c == 0, high, low))
    own = jnp.where(c == 0, jnp.concatenate([mine, got]), jnp.concatenate([got, mine]))
    first = [own] + [ring(own, 2, n) for n in (1, 2, 3)]
    chunks = []
    for chunk in range(2):
        cols = slice(chunk * HEAD_DIM, (chunk + 1) * HEAD_DIM)
        part = jnp.stack([piece[:, cols] for piece in first])
        part = join([part] + [ring(part, 1, n) for n in (1, 2, 3)], chunks[0][1:3] if chunk else [])
        ahead, behind = ring(part, 0, 1), ring(part, 0, -1)
        far_a, far_b = ring(behind[:2], 0, -1), ring(ahead[2:], 0, 1)
        chunks.append([part, ahead, behind, far_a, far_b])
    return chunks


def body(enc_hidden, kv_weights, queries, cotangent, enc_lengths, dec_lengths, dec_partner):
    z, y, c, x = (lax.axis_index(a) for a in ALL)
    me = jnp.stack([z, y, c, x]).astype(jnp.int32)
    weights = gather(kv_weights, c)
    meta, info, leave_a, leave_b = depart(me, enc_lengths, dec_lengths, dec_partner, queries, cotangent)
    sent_a = lax.ppermute(leave_a, DP, SEND_A)
    sent_b = lax.ppermute(leave_b, DP, SEND_B)
    tokens, tokens_t = turn(enc_hidden, swap(enc_hidden))
    q_other, ct_other = swap(queries), swap(cotangent)

    pieces, grads = [], []
    for chunk in range(2):
        mine, other, far_a, far_b, *parts = run_main(
            chunk, meta, me, tokens, tokens_t, weights[chunk], queries, q_other, cotangent, ct_other, sent_a, sent_b
        )
        grads.append(exchange(parts, 0))
        pieces += [mine, swap(other), lax.ppermute(far_a, DP, back(SEND_A)), lax.ppermute(far_b, DP, back(SEND_B))]

    last = []
    for chunk, parts in enumerate(grads):
        after = grads[1][0] if chunk == 0 else None
        second = exchange(add_parts(parts, after), 1)
        last.append(exchange(add_parts(second), 2))
    summed = jnp.concatenate(
        [sum(part.astype(jnp.float32) for part in parts) for parts in last], axis=1
    )
    low, high = summed[:64], summed[64:]
    got = swap(jnp.where(c == 0, high, low))
    kept = jnp.where(c == 0, low, high)
    grad = jnp.concatenate([jnp.where(c == 0, kept, got), jnp.where(c == 0, got, kept)], axis=1)
    context, grad_queries = finish(info, pieces)
    return context, grad_queries, grad


def solution(mesh):
    fine = Mesh(mesh.devices.reshape(4, 4, 2, 4), ALL)
    rows = P(ALL, None)
    cut = P(DP, "x")
    return jax.shard_map(
        body,
        mesh=fine,
        in_specs=(rows, cut, rows, rows, P(), P(), P()),
        out_specs=(rows, rows, cut),
        check_vma=False,
    )
```

```python
import functools

import jax
import jax.numpy as jnp
from jax import lax
from jax.experimental import pallas as pl
from jax.experimental.pallas import tpu as pltpu
from jax.sharding import Mesh, PartitionSpec as P

HEAD_DIM = 256
SEGS = 4
TOK = 512
PAIR = 2 * TOK
WIN = 176
POOL = PAIR + 2 * WIN
D = 2048
HALF = 512
GROUP = 4
DP = ("z", "y", "c")
ALL = ("z", "y", "c", "x")
MIB = 1024 * 1024
BF = jnp.bfloat16


def align(start, limit):
    return jnp.minimum((start // 16) * 16, limit - WIN)


def mm(a, b, dims):
    return lax.dot_general(a, b, (dims, ((), ())), preferred_element_type=jnp.float32)


def attend(meta, k_s, v_s, q_s, ct_s, ctx_s, gq_s, gk_s, gv_s):
    scale = HEAD_DIM ** -0.5
    col = lax.broadcasted_iota(jnp.int32, (WIN, WIN), 1)
    row = lax.broadcasted_iota(jnp.int32, (WIN, WIN), 0)
    row_wide = lax.broadcasted_iota(jnp.int32, (WIN, HEAD_DIM), 0)
    for first in range(0, 2 * SEGS, GROUP):
        spots, loaded, scores = [], [], []
        for e in range(first, first + GROUP):
            es, el, ds, dl = meta[e, 0], meta[e, 1], meta[e, 2], meta[e, 3]
            ew = pl.multiple_of(align(es, PAIR), 16)
            dw = pl.multiple_of(align(ds, POOL), 16)
            spots.append((pl.ds(ew, WIN), pl.ds(dw, WIN), es - ew, el, ds - dw, dl))
        for ewin, dwin, *_ in spots:
            k, v, q, ct = k_s[ewin, :], v_s[ewin, :], q_s[dwin, :], ct_s[dwin, :]
            loaded.append((k, v, q, ct))
            scores.append((mm(q, k, ((1,), (1,))), mm(ct, v, ((1,), (1,)))))
        weights = []
        for (_, _, elo, el, dlo, dl), (s, gw) in zip(spots, scores):
            k_live = (col >= elo) & (col < elo + el)
            q_live = (row[:, :1] >= dlo) & (row[:, :1] < dlo + dl)
            s = jnp.where(k_live, s * scale, -jnp.inf)
            p = jnp.exp(s - jnp.max(s, axis=1, keepdims=True))
            share = jnp.where(q_live, 1.0 / jnp.sum(p, axis=1, keepdims=True), 0.0)
            w = p * share
            delta = jnp.sum(w * gw, axis=1, keepdims=True)
            weights.append((w.astype(BF), (w * (gw - delta) * scale).astype(BF)))
        results = []
        for (k, v, q, ct), (w_low, gs) in zip(loaded, weights):
            results.append((
                mm(w_low, v, ((1,), (0,))).astype(BF),
                mm(gs, k, ((1,), (0,))).astype(BF),
                mm(gs, q, ((0,), (0,))).astype(BF),
                mm(w_low, ct, ((0,), (0,))).astype(BF),
            ))
        for (ewin, dwin, elo, el, dlo, dl), (ctx, gq, gk, gv) in zip(spots, results):
            d_in = (row_wide >= dlo) & (row_wide < dlo + dl)
            e_in = (row_wide >= elo) & (row_wide < elo + el)
            ctx_s[dwin, :] = jnp.where(d_in, ctx, ctx_s[dwin, :])
            gq_s[dwin, :] = jnp.where(d_in, gq, gq_s[dwin, :])
            gk_s[ewin, :] = jnp.where(e_in, gk, gk_s[ewin, :])
            gv_s[ewin, :] = jnp.where(e_in, gv, gv_s[ewin, :])


def places(me):
    z, y, c, x = me[0], me[1], me[2], me[3]

    def block(ra, rb, rc):
        first = c == 0
        bx = (x + jnp.where(first, ra, rb)) & 3
        by = (y + jnp.where(first, rb, rc)) & 3
        bz = (z + jnp.where(first, rc, ra)) & 3
        return bx, bz * 4 + by

    return block


def main_kernel(extra, meta, me, x_ref, xt_ref, w0, w1, w3, w2a, w2b,
                qm, qo, qa, qb, cm, co, ca, cb, *refs):
    om, oo, oa, ob, d0, d1, d2, d3 = refs[extra : extra + 8]
    k_s, v_s, gk_s, gv_s, q_s, ct_s, ctx_s, gq_s, dw_s, w_s = refs[extra + 8 :]
    step = pl.program_id(0)
    block = places(me)

    @pl.when(step == 0)
    def _():
        def take(rc, carry):
            for rb in range(4):
                far = w2a[rb, rc] if rb < 2 else w2b[rb - 2, rc]
                for ra, value in enumerate((w0[rb, rc], w1[rb, rc], far, w3[rb, rc])):
                    bx, bzy = block(ra, rb, rc)
                    w_s[bx, pl.ds(pl.multiple_of(bzy * 128, 128), 128), :] = value
            return carry

        lax.fori_loop(0, 4, take, 0)

    x = x_ref[...]
    k_s[...] = jnp.dot(x, w_s[step], preferred_element_type=jnp.float32).astype(BF)
    v_s[...] = jnp.dot(x, w_s[2 + step], preferred_element_type=jnp.float32).astype(BF)
    for pool, parts in ((q_s, (qm, qo, qa, qb)), (ct_s, (cm, co, ca, cb))):
        pool[0:TOK, :] = parts[0][...]
        pool[TOK:PAIR, :] = parts[1][...]
        pool[PAIR : PAIR + WIN, :] = parts[2][...]
        pool[PAIR + WIN :, :] = parts[3][...]
    attend(meta, k_s, v_s, q_s, ct_s, ctx_s, gq_s, gk_s, gv_s)
    for kind, pool in enumerate((ctx_s, gq_s)):
        om[kind] = pool[0:TOK, :]
        oo[kind] = pool[TOK:PAIR, :]
        oa[kind] = pool[PAIR : PAIR + WIN, :]
        ob[kind] = pool[PAIR + WIN :, :]
    xt = xt_ref[...]
    dw_s[step] = jnp.dot(xt, gk_s[...], preferred_element_type=jnp.float32).astype(BF)
    dw_s[2 + step] = jnp.dot(xt, gv_s[...], preferred_element_type=jnp.float32).astype(BF)

    @pl.when(step == 1)
    def _():
        def put(n, carry):
            rb, rc = n // 4, n % 4
            for ra, out in enumerate((d0, d1, d2, d3)):
                bx, bzy = block(ra, rb, rc)
                out[rb, rc] = dw_s[bx, pl.ds(pl.multiple_of(bzy * 128, 128), 128), :]
            return carry

        lax.fori_loop(0, 16, put, 0)


def run_main(chunk, meta, me, x, xt, weights, q, ct, given, sent_a, sent_b, before=(), after=()):
    def fixed(*shape):
        return pl.BlockSpec(shape, lambda i, m, e: (0,) * len(shape), pipeline_mode=pl.Buffered(1))

    def wide():
        return pl.BlockSpec((TOK, HEAD_DIM), lambda i, m, e: (0, i * 4 + e[2] * 2 + chunk))

    def narrow(rows, kind):
        return pl.BlockSpec((rows, HEAD_DIM), lambda i, m, e: (0, kind * 4 + i * 2 + chunk))

    def out(rows):
        return pl.BlockSpec((2, rows, HEAD_DIM), lambda i, m, e: (0, 0, i * 2 + chunk))

    part = pl.BlockSpec((4, 4, 128, HEAD_DIM), lambda i, m, e: (0, 0, 0, 0))
    anywhere = pl.BlockSpec(memory_space=pl.ANY)
    pair = pltpu.VMEM((PAIR, HEAD_DIM), BF)
    pool = pltpu.VMEM((POOL, HEAD_DIM), BF)
    extra = [*before, *after]
    return pl.pallas_call(
        functools.partial(main_kernel, len(extra)),
        grid_spec=pltpu.PrefetchScalarGridSpec(
            num_scalar_prefetch=2,
            grid=(2,),
            in_specs=[fixed(PAIR, D), fixed(D, PAIR), *[fixed(*w.shape) for w in weights],
                      wide(), narrow(TOK, 0), narrow(WIN, 0), narrow(WIN, 0),
                      wide(), narrow(TOK, 1), narrow(WIN, 1), narrow(WIN, 1)]
            + [anywhere] * len(extra),
            out_specs=[out(TOK), out(TOK), out(WIN), out(WIN), part, part, part, part],
            scratch_shapes=[pair, pair, pair, pair, pool, pool, pool, pool,
                            pltpu.VMEM((4, D, HEAD_DIM), BF), pltpu.VMEM((4, D, HEAD_DIM), BF)],
        ),
        out_shape=[jax.ShapeDtypeStruct((2, rows, 2 * HALF), BF) for rows in (TOK, TOK, WIN, WIN)]
        + [jax.ShapeDtypeStruct((4, 4, 128, HEAD_DIM), BF)] * 4,
        input_output_aliases={17 + n: n for n in range(len(before))},
        compiler_params=pltpu.CompilerParams(vmem_limit_bytes=52 * MIB),
        cost_estimate=pl.CostEstimate(flops=12_000_000_000, bytes_accessed=24_000_000, transcendentals=500_000),
    )(meta, me, x, xt, *weights, q, given, sent_a, sent_b, ct, given, sent_a, sent_b, *extra)


def add_kernel(*refs):
    ins, outs = refs[:4], refs[-4:]
    total = sum(ref[...].astype(jnp.float32) for ref in ins).astype(BF)
    for n, out in enumerate(outs):
        out[...] = total[n]


def add_parts(parts, after=()):
    extra = list(after)
    shape = parts[0].shape
    rank = len(shape)
    if rank == 4:
        grid = (4,)
        source = pl.BlockSpec((4, 1, 128, HEAD_DIM), lambda i: (0, i, 0, 0))
        target = pl.BlockSpec((1, 128, HEAD_DIM), lambda i: (i, 0, 0))
    else:
        grid = (1,)
        source = pl.BlockSpec(shape, lambda i: (0, 0, 0))
        target = pl.BlockSpec(shape[1:], lambda i: (0, 0))
    return pl.pallas_call(
        add_kernel,
        grid=grid,
        in_specs=[source] * 4 + [pl.BlockSpec(memory_space=pl.ANY)] * len(extra),
        out_specs=[target] * 4,
        out_shape=[jax.ShapeDtypeStruct(shape[1:], BF)] * 4,
        compiler_params=pltpu.CompilerParams(vmem_limit_bytes=16 * MIB),
    )(*parts, *extra)


def depart_kernel(me, enc_len, dec_len, partner, q_ref, ct_ref, meta, info, a_ref, b_ref, give_ref):
    core, x = me[2], me[3]
    t = me[0] * 4 + me[1]

    for side in range(2):
        device = (t * 2 + (core if side == 0 else 1 - core)) * 4 + x
        start = jnp.int32(side * TOK)
        for slot in range(SEGS):
            meta[side * SEGS + slot, 0] = start
            meta[side * SEGS + slot, 1] = enc_len[device, slot]
            start = start + enc_len[device, slot]
    for n in range(4):
        info[n] = jnp.int32(0)
    info[1] = core
    for near in range(4):
        dp = t * 2 - 1 + near
        device = jnp.clip(dp, 0, 31) * 4 + x
        real = (dp >= 0) & (dp < 32)
        same = (dp & 1) == core
        start = jnp.int32(0)
        for slot in range(SEGS):
            begin, length = start, dec_len[device, slot]
            owner = partner[device, slot] >> 4
            here = real & ((owner >> 1) == t)
            window = align(begin, TOK)
            if near in (1, 2):
                at = begin + jnp.where(same, 0, TOK)
            else:
                at = begin - window + PAIR + jnp.where(same, 0, WIN)

            @pl.when(here)
            def _():
                entry = jnp.where((owner & 1) == core, 0, SEGS) + (partner[device, slot] & 3)
                meta[entry, 2] = at
                meta[entry, 3] = length

            if near in (1, 2):

                @pl.when(same & jnp.logical_not(here))
                def _():
                    info[0] = window
                    info[2] = begin
                    info[3] = length

            start = start + length

    rows = pl.ds(pl.multiple_of(info[0], 16), WIN)
    for n in range(4):
        source = (q_ref, ct_ref)[n // 2]
        for side, out in ((core, a_ref), (1 - core, b_ref)):
            begin = pl.multiple_of((n % 2) * 1024 + side * HALF, HALF)
            out[:, n * HALF : (n + 1) * HALF] = source[rows, pl.ds(begin, HALF)]
        give_ref[:, n * HALF : (n + 1) * HALF] = source[:, pl.ds(begin, HALF)]


def depart(me, enc_lengths, dec_lengths, dec_partner, q, ct):
    whole = pl.BlockSpec(memory_space=pltpu.VMEM)
    scalar = pl.BlockSpec(memory_space=pltpu.SMEM)
    return pl.pallas_call(
        depart_kernel,
        in_specs=[scalar, scalar, scalar, scalar, whole, whole],
        out_specs=[scalar, scalar, whole, whole, whole],
        out_shape=[jax.ShapeDtypeStruct((2 * SEGS, 4), jnp.int32), jax.ShapeDtypeStruct((4,), jnp.int32)]
        + [jax.ShapeDtypeStruct((rows, 2048), BF) for rows in (WIN, WIN, TOK)],
        compiler_params=pltpu.CompilerParams(vmem_limit_bytes=16 * MIB),
    )(me, enc_lengths, dec_lengths, dec_partner, q, ct)


def turn_kernel(a_ref, b_ref, x_ref, xt_ref):
    for n, ref in enumerate((a_ref, b_ref)):
        value = ref[...]
        x_ref[n * TOK : (n + 1) * TOK, :] = value
        xt_ref[:, n * TOK : (n + 1) * TOK] = value.T


def turn(a, b):
    part = pl.BlockSpec((TOK, 512), lambda i: (0, i))
    return pl.pallas_call(
        turn_kernel,
        grid=(D // 512,),
        in_specs=[part, part],
        out_specs=[pl.BlockSpec((PAIR, 512), lambda i: (0, i)), pl.BlockSpec((512, PAIR), lambda i: (i, 0))],
        out_shape=[jax.ShapeDtypeStruct((PAIR, D), BF), jax.ShapeDtypeStruct((D, PAIR), BF)],
        compiler_params=pltpu.CompilerParams(vmem_limit_bytes=16 * MIB),
    )(a, b)


def finish_kernel(info, *refs):
    ins, outs = refs[:4], refs[4:]
    win = pl.multiple_of(info[0], 16)
    core, start, length = info[1], info[2] - info[0], info[3]
    rows = pl.ds(win, WIN)
    place = lax.broadcasted_iota(jnp.int32, (WIN, HALF), 0)
    inside = (place >= start) & (place < start + length)
    mine, theirs, back_a, back_b = ins
    for side, base, back in ((core, mine, back_a), (1 - core, theirs, back_b)):
        cols = pl.ds(pl.multiple_of(side * HALF, HALF), HALF)
        for kind, out in enumerate(outs):
            out[:, cols] = base[kind]
            out[rows, cols] = jnp.where(inside, back[kind], out[rows, cols])


def finish(info, pieces):
    def source(rows):
        return pl.BlockSpec((2, rows, HALF), lambda i, e: (0, 0, i))

    out = pl.BlockSpec((TOK, 1024), lambda i, e: (0, i))
    return pl.pallas_call(
        finish_kernel,
        grid_spec=pltpu.PrefetchScalarGridSpec(
            num_scalar_prefetch=1,
            grid=(2,),
            in_specs=[source(TOK), source(TOK), source(WIN), source(WIN)],
            out_specs=[out, out],
        ),
        out_shape=[jax.ShapeDtypeStruct((TOK, 2048), BF)] * 2,
        compiler_params=pltpu.CompilerParams(vmem_limit_bytes=32 * MIB),
    )(info, *pieces)


def swap(value):
    return lax.ppermute(value, "c", [(0, 1), (1, 0)])


SEND_A = [(2 * t, 2 * t - 2) for t in range(1, 16)] + [(2 * t + 1, 2 * t + 3) for t in range(15)]
SEND_B = [(2 * t, 2 * t - 1) for t in range(1, 16)] + [(2 * t + 1, 2 * t + 2) for t in range(15)]


def back(pairs):
    return [(b, a) for a, b in pairs]


def shift(phase, amount):
    pairs = []
    for z in range(4):
        for y in range(4):
            for c in range(2):
                for x in range(4):
                    to = {"z": z, "y": y, "x": x}
                    axis = ("xyz", "zxy")[c][phase]
                    to[axis] = (to[axis] + amount) % 4
                    pairs.append((((z * 4 + y) * 2 + c) * 4 + x, ((to["z"] * 4 + to["y"]) * 2 + c) * 4 + to["x"]))
    return pairs


def exchange(parts, phase):
    return [parts[0]] + [lax.ppermute(parts[r], ALL, shift(phase, r)) for r in (1, 3, 2)]


def join_kernel(cols, *refs):
    for n in range(4):
        refs[-1][n] = refs[n][..., cols]


def join(parts, after, cols=slice(0, HEAD_DIM)):
    whole = pl.BlockSpec(memory_space=pltpu.VMEM)
    return pl.pallas_call(
        functools.partial(join_kernel, cols),
        in_specs=[whole] * 4 + [pl.BlockSpec(memory_space=pl.ANY)] * len(after),
        out_specs=whole,
        out_shape=jax.ShapeDtypeStruct((4,) + parts[0].shape[:-1] + (HEAD_DIM,), BF),
        compiler_params=pltpu.CompilerParams(vmem_limit_bytes=16 * MIB),
    )(*parts, *after)


def ring(value, phase, amount):
    return lax.ppermute(value, ALL, shift(phase, -amount))


def gather(kv_weights, c, ready, turned):
    low, high = kv_weights[:, :HALF], kv_weights[:, HALF:]
    mine, got = jnp.where(c == 0, low, high), swap(jnp.where(c == 0, high, low))
    own = jnp.where(c == 0, jnp.concatenate([mine, got]), jnp.concatenate([got, mine]))
    first = [own] + [ring(own, 2, n) for n in (1, 2, 3)]
    chunks = []
    for chunk in range(2):
        cols = slice(chunk * HEAD_DIM, (chunk + 1) * HEAD_DIM)
        part = join(first, chunks[0][:1] if chunk else [ready], cols)
        part = join([part] + [ring(part, 1, n) for n in (1, 2, 3)], [] if chunk else [turned])
        ahead, behind = ring(part, 0, 1), ring(part, 0, -1)
        far_a, far_b = ring(behind[:2], 0, -1), ring(ahead[2:], 0, 1)
        chunks.append([part, ahead, behind, far_a, far_b])
    return chunks


def body(enc_hidden, kv_weights, queries, cotangent, enc_lengths, dec_lengths, dec_partner):
    z, y, c, x = (lax.axis_index(a) for a in ALL)
    me = jnp.stack([z, y, c, x]).astype(jnp.int32)
    meta, info, leave_a, leave_b, give = depart(me, enc_lengths, dec_lengths, dec_partner, queries, cotangent)
    tokens, tokens_t = turn(enc_hidden, swap(enc_hidden))
    weights = gather(kv_weights, c, leave_a, tokens_t)
    sent_a = lax.ppermute(leave_a, DP, SEND_A)
    sent_b = lax.ppermute(leave_b, DP, SEND_B)
    shared = (meta, me, tokens, tokens_t)
    inputs = (queries, cotangent, swap(give), sent_a, sent_b)

    results, parts = [], []
    for chunk in range(2):
        done = run_main(chunk, *shared, weights[chunk], *inputs, before=results, after=() if chunk else weights[1][1:3])
        results = done[:4]
        parts.append(exchange(done[4:], 0))
    mine, other, far_a, far_b = results
    context, grad_queries = finish(
        info,
        [mine, swap(other), lax.ppermute(far_a, DP, back(SEND_A)), lax.ppermute(far_b, DP, back(SEND_B))],
    )

    second = add_parts(exchange(add_parts(parts[0], [mine]), 1))
    last = [exchange(second, 2)]
    second = add_parts(exchange(add_parts(parts[1], [second[0]]), 1), [context])
    last.append(exchange(second, 2))
    summed = jnp.concatenate(
        [sum(part.astype(jnp.float32) for part in parts) for parts in last], axis=1
    )
    low, high = summed[:64], summed[64:]
    got = swap(jnp.where(c == 0, high, low))
    kept = jnp.where(c == 0, low, high)
    grad = jnp.concatenate([jnp.where(c == 0, kept, got), jnp.where(c == 0, got, kept)], axis=1)
    return context, grad_queries, grad


def solution(mesh):
    fine = Mesh(mesh.devices.reshape(4, 4, 2, 4), ALL)
    rows = P(ALL, None)
    cut = P(DP, "x")
    return jax.shard_map(
        body,
        mesh=fine,
        in_specs=(rows, cut, rows, rows, P(), P(), P()),
        out_specs=(rows, rows, cut),
        check_vma=False,
    )
```

```python
import functools

import jax
import jax.numpy as jnp
from jax import lax
from jax.experimental import pallas as pl
from jax.experimental.pallas import tpu as pltpu
from jax.sharding import Mesh, PartitionSpec as P

HEAD_DIM = 256
SEGS = 4
TOK = 512
PAIR = 2 * TOK
WIN = 176
POOL = PAIR + 2 * WIN
D = 2048
HALF = 512
GROUP = 4
DP = ("z", "y", "c")
ALL = ("z", "y", "c", "x")
MIB = 1024 * 1024
BF = jnp.bfloat16


def align(start, limit):
    return jnp.minimum((start // 16) * 16, limit - WIN)


def mm(a, b, dims):
    return lax.dot_general(a, b, (dims, ((), ())), preferred_element_type=jnp.float32)


def attend(meta, k_s, v_s, q_s, ct_s, ctx_s, gq_s, gk_s, gv_s):
    scale = HEAD_DIM ** -0.5
    col = lax.broadcasted_iota(jnp.int32, (WIN, WIN), 1)
    row = lax.broadcasted_iota(jnp.int32, (WIN, WIN), 0)
    row_wide = lax.broadcasted_iota(jnp.int32, (WIN, HEAD_DIM), 0)
    for first in range(0, 2 * SEGS, GROUP):
        spots, loaded, scores = [], [], []
        for e in range(first, first + GROUP):
            es, el, ds, dl = meta[e, 0], meta[e, 1], meta[e, 2], meta[e, 3]
            ew = pl.multiple_of(align(es, PAIR), 16)
            dw = pl.multiple_of(align(ds, POOL), 16)
            spots.append((pl.ds(ew, WIN), pl.ds(dw, WIN), es - ew, el, ds - dw, dl))
        for ewin, dwin, *_ in spots:
            k, v, q, ct = k_s[ewin, :], v_s[ewin, :], q_s[dwin, :], ct_s[dwin, :]
            loaded.append((k, v, q, ct))
            scores.append((mm(q, k, ((1,), (1,))), mm(ct, v, ((1,), (1,)))))
        weights = []
        for (_, _, elo, el, dlo, dl), (s, gw) in zip(spots, scores):
            k_live = (col >= elo) & (col < elo + el)
            q_live = (row[:, :1] >= dlo) & (row[:, :1] < dlo + dl)
            s = jnp.where(k_live, s * scale, -jnp.inf)
            p = jnp.exp(s - jnp.max(s, axis=1, keepdims=True))
            share = jnp.where(q_live, 1.0 / jnp.sum(p, axis=1, keepdims=True), 0.0)
            w = p * share
            delta = jnp.sum(w * gw, axis=1, keepdims=True)
            weights.append((w.astype(BF), (w * (gw - delta) * scale).astype(BF)))
        results = []
        for (k, v, q, ct), (w_low, gs) in zip(loaded, weights):
            results.append((
                mm(w_low, v, ((1,), (0,))).astype(BF),
                mm(gs, k, ((1,), (0,))).astype(BF),
                mm(gs, q, ((0,), (0,))).astype(BF),
                mm(w_low, ct, ((0,), (0,))).astype(BF),
            ))
        for (ewin, dwin, elo, el, dlo, dl), (ctx, gq, gk, gv) in zip(spots, results):
            d_in = (row_wide >= dlo) & (row_wide < dlo + dl)
            e_in = (row_wide >= elo) & (row_wide < elo + el)
            ctx_s[dwin, :] = jnp.where(d_in, ctx, ctx_s[dwin, :])
            gq_s[dwin, :] = jnp.where(d_in, gq, gq_s[dwin, :])
            gk_s[ewin, :] = jnp.where(e_in, gk, gk_s[ewin, :])
            gv_s[ewin, :] = jnp.where(e_in, gv, gv_s[ewin, :])


def places(me):
    z, y, c, x = me[0], me[1], me[2], me[3]

    def block(ra, rb, rc):
        first = c == 0
        bx = (x + jnp.where(first, ra, rb)) & 3
        by = (y + jnp.where(first, rb, rc)) & 3
        bz = (z + jnp.where(first, rc, ra)) & 3
        return bx, bz * 4 + by

    return block


def main_kernel(weights, extra, meta, me, x_ref, xt_ref, *refs):
    w0, w1, w3, *w2 = refs[:weights]
    qm, qo, qa, qb, cm, co, ca, cb = refs[weights : weights + 8]
    om, oo, oa, ob, d0, d1, d3, *d2 = refs[weights + 8 + extra : -10]
    k_s, v_s, gk_s, gv_s, q_s, ct_s, ctx_s, gq_s, dw_s, w_s = refs[-10:]
    step = pl.program_id(0)
    block = places(me)

    @pl.when(step == 0)
    def _():
        def take(rc, carry):
            for rb in range(4):
                far = w2[rb * len(w2) // 4][rb % (4 // len(w2)), rc]
                for ra, value in enumerate((w0[rb, rc], w1[rb, rc], far, w3[rb, rc])):
                    bx, bzy = block(ra, rb, rc)
                    w_s[bx, pl.ds(pl.multiple_of(bzy * 128, 128), 128), :] = value
            return carry

        lax.fori_loop(0, 4, take, 0)

    x = x_ref[...]
    k_s[...] = jnp.dot(x, w_s[step], preferred_element_type=jnp.float32).astype(BF)
    v_s[...] = jnp.dot(x, w_s[2 + step], preferred_element_type=jnp.float32).astype(BF)
    for pool, parts in ((q_s, (qm, qo, qa, qb)), (ct_s, (cm, co, ca, cb))):
        pool[0:TOK, :] = parts[0][...]
        pool[TOK:PAIR, :] = parts[1][...]
        pool[PAIR : PAIR + WIN, :] = parts[2][...]
        pool[PAIR + WIN :, :] = parts[3][...]
    attend(meta, k_s, v_s, q_s, ct_s, ctx_s, gq_s, gk_s, gv_s)
    for kind, pool in enumerate((ctx_s, gq_s)):
        om[kind] = pool[0:TOK, :]
        oo[kind] = pool[TOK:PAIR, :]
        oa[kind] = pool[PAIR : PAIR + WIN, :]
        ob[kind] = pool[PAIR + WIN :, :]
    xt = xt_ref[...]
    dw_s[step] = jnp.dot(xt, gk_s[...], preferred_element_type=jnp.float32).astype(BF)
    dw_s[2 + step] = jnp.dot(xt, gv_s[...], preferred_element_type=jnp.float32).astype(BF)

    @pl.when(step == 1)
    def _():
        def put(rc, carry):
            for rb in range(4):
                for ra, out in ((0, d0), (1, d1), (3, d3), (2, d2[rb * len(d2) // 4])):
                    bx, bzy = block(ra, rb, rc)
                    at = rb % (4 // len(d2)) if ra == 2 else rb
                    out[at, rc] = dw_s[bx, pl.ds(pl.multiple_of(bzy * 128, 128), 128), :]
            return carry

        lax.fori_loop(0, 4, put, 0)


def run_main(chunk, meta, me, x, xt, weights, q, ct, given, sent_a, sent_b, before=()):
    def fixed(*shape):
        return pl.BlockSpec(shape, lambda i, m, e: (0,) * len(shape), pipeline_mode=pl.Buffered(1))

    def wide():
        return pl.BlockSpec((TOK, HEAD_DIM), lambda i, m, e: (0, i * 4 + e[2] * 2 + chunk))

    def narrow(rows, kind):
        return pl.BlockSpec((rows, HEAD_DIM), lambda i, m, e: (0, kind * 4 + i * 2 + chunk))

    def out(rows):
        return pl.BlockSpec((2, rows, HEAD_DIM), lambda i, m, e: (0, 0, i * 2 + chunk))

    def part(shape):
        return pl.BlockSpec(shape, lambda i, m, e: (0, 0, 0, 0))

    parts = [(4, 4, 128, HEAD_DIM)] * 4 if chunk == 0 else [(4, 4, 128, HEAD_DIM)] * 3 + [(2, 4, 128, HEAD_DIM)] * 2
    anywhere = pl.BlockSpec(memory_space=pl.ANY)
    pair = pltpu.VMEM((PAIR, HEAD_DIM), BF)
    pool = pltpu.VMEM((POOL, HEAD_DIM), BF)
    return pl.pallas_call(
        functools.partial(main_kernel, len(weights), len(before)),
        grid_spec=pltpu.PrefetchScalarGridSpec(
            num_scalar_prefetch=2,
            grid=(2,),
            in_specs=[fixed(PAIR, D), fixed(D, PAIR), *[fixed(*w.shape) for w in weights],
                      wide(), narrow(TOK, 0), narrow(WIN, 0), narrow(WIN, 0),
                      wide(), narrow(TOK, 1), narrow(WIN, 1), narrow(WIN, 1)]
            + [anywhere] * len(before),
            out_specs=[out(TOK), out(TOK), out(WIN), out(WIN), *[part(shape) for shape in parts]],
            scratch_shapes=[pair, pair, pair, pair, pool, pool, pool, pool,
                            pltpu.VMEM((4, D, HEAD_DIM), BF), pltpu.VMEM((4, D, HEAD_DIM), BF)],
        ),
        out_shape=[jax.ShapeDtypeStruct((2, rows, 2 * HALF), BF) for rows in (TOK, TOK, WIN, WIN)]
        + [jax.ShapeDtypeStruct(shape, BF) for shape in parts],
        input_output_aliases={12 + len(weights) + n: n for n in range(len(before))},
        compiler_params=pltpu.CompilerParams(vmem_limit_bytes=52 * MIB),
        cost_estimate=pl.CostEstimate(flops=12_000_000_000, bytes_accessed=24_000_000, transcendentals=500_000),
    )(meta, me, x, xt, *weights, q, given, sent_a, sent_b, ct, given, sent_a, sent_b, *before)


def add_kernel(count, *refs):
    ins, outs = refs[:count], refs[-4:]
    total = sum(ref[...].astype(jnp.float32) for ref in ins).astype(BF)
    for n, out in enumerate(outs):
        out[...] = total[n]


def add_parts(parts, after=()):
    extra = list(after)
    shape = parts[0].shape
    rank = len(shape)
    if rank == 4:
        grid = (4,)
        source = pl.BlockSpec((4, 1, 128, HEAD_DIM), lambda i: (0, i, 0, 0))
        target = pl.BlockSpec((1, 128, HEAD_DIM), lambda i: (i, 0, 0))
    else:
        grid = (1,)
        source = pl.BlockSpec(shape, lambda i: (0, 0, 0))
        target = pl.BlockSpec(shape[1:], lambda i: (0, 0))
    return pl.pallas_call(
        functools.partial(add_kernel, len(parts)),
        grid=grid,
        in_specs=[source] * len(parts) + [pl.BlockSpec(memory_space=pl.ANY)] * len(extra),
        out_specs=[target] * 4,
        out_shape=[jax.ShapeDtypeStruct(shape[1:], BF)] * 4,
        compiler_params=pltpu.CompilerParams(vmem_limit_bytes=16 * MIB),
    )(*parts, *extra)


def depart_kernel(me, enc_len, dec_len, partner, q_ref, ct_ref, meta, info, a_ref, b_ref, give_ref, sems):
    core, x = me[2], me[3]
    t = me[0] * 4 + me[1]

    for side in range(2):
        device = (t * 2 + (core if side == 0 else 1 - core)) * 4 + x
        start = jnp.int32(side * TOK)
        for slot in range(SEGS):
            meta[side * SEGS + slot, 0] = start
            meta[side * SEGS + slot, 1] = enc_len[device, slot]
            start = start + enc_len[device, slot]
    for n in range(4):
        info[n] = jnp.int32(0)
    info[1] = core
    for near in range(4):
        dp = t * 2 - 1 + near
        device = jnp.clip(dp, 0, 31) * 4 + x
        real = (dp >= 0) & (dp < 32)
        same = (dp & 1) == core
        start = jnp.int32(0)
        for slot in range(SEGS):
            begin, length = start, dec_len[device, slot]
            owner = partner[device, slot] >> 4
            here = real & ((owner >> 1) == t)
            window = align(begin, TOK)
            if near in (1, 2):
                at = begin + jnp.where(same, 0, TOK)
            else:
                at = begin - window + PAIR + jnp.where(same, 0, WIN)

            @pl.when(here)
            def _():
                entry = jnp.where((owner & 1) == core, 0, SEGS) + (partner[device, slot] & 3)
                meta[entry, 2] = at
                meta[entry, 3] = length

            if near in (1, 2):

                @pl.when(same & jnp.logical_not(here))
                def _():
                    info[0] = window
                    info[2] = begin
                    info[3] = length

            start = start + length

    rows = pl.ds(pl.multiple_of(info[0], 16), WIN)
    copies = []
    for n in range(4):
        source = (q_ref, ct_ref)[n // 2]
        cols = pl.ds(n * HALF, HALF)
        for side, out in ((core, a_ref), (1 - core, b_ref)):
            begin = pl.ds(pl.multiple_of((n % 2) * 1024 + side * HALF, HALF), HALF)
            copies.append((source.at[rows, begin], out.at[:, cols]))
        copies.append((source.at[:, begin], give_ref.at[:, cols]))
    copies = [pltpu.make_async_copy(a, b, sems.at[n]) for n, (a, b) in enumerate(copies)]
    for copy in copies:
        copy.start()
    for copy in copies:
        copy.wait()


def depart(me, enc_lengths, dec_lengths, dec_partner, q, ct):
    whole = pl.BlockSpec(memory_space=pl.ANY)
    scalar = pl.BlockSpec(memory_space=pltpu.SMEM)
    return pl.pallas_call(
        depart_kernel,
        in_specs=[scalar, scalar, scalar, scalar, whole, whole],
        out_specs=[scalar, scalar, whole, whole, whole],
        scratch_shapes=[pltpu.SemaphoreType.DMA((12,))],
        out_shape=[jax.ShapeDtypeStruct((2 * SEGS, 4), jnp.int32), jax.ShapeDtypeStruct((4,), jnp.int32)]
        + [jax.ShapeDtypeStruct((rows, 2048), BF) for rows in (WIN, WIN, TOK)],
        compiler_params=pltpu.CompilerParams(vmem_limit_bytes=16 * MIB),
    )(me, enc_lengths, dec_lengths, dec_partner, q, ct)


def turn_kernel(a_ref, b_ref, *refs):
    x_ref, xt_ref = refs[-2:]
    for n, ref in enumerate((a_ref, b_ref)):
        value = ref[...]
        x_ref[n * TOK : (n + 1) * TOK, :] = value
        xt_ref[:, n * TOK : (n + 1) * TOK] = value.T


def turn(a, b, after):
    part = pl.BlockSpec((TOK, 512), lambda i: (0, i))
    return pl.pallas_call(
        turn_kernel,
        grid=(D // 512,),
        in_specs=[part, part] + [pl.BlockSpec(memory_space=pl.ANY)] * len(after),
        out_specs=[pl.BlockSpec((PAIR, 512), lambda i: (0, i)), pl.BlockSpec((512, PAIR), lambda i: (i, 0))],
        out_shape=[jax.ShapeDtypeStruct((PAIR, D), BF), jax.ShapeDtypeStruct((D, PAIR), BF)],
        compiler_params=pltpu.CompilerParams(vmem_limit_bytes=16 * MIB),
    )(a, b, *after)


def finish_kernel(info, *refs):
    ins, outs = refs[:4], refs[4:]
    win = pl.multiple_of(info[0], 16)
    core, start, length = info[1], info[2] - info[0], info[3]
    rows = pl.ds(win, WIN)
    place = lax.broadcasted_iota(jnp.int32, (WIN, HALF), 0)
    inside = (place >= start) & (place < start + length)
    mine, theirs, back_a, back_b = ins
    for side, base, back in ((core, mine, back_a), (1 - core, theirs, back_b)):
        cols = pl.ds(pl.multiple_of(side * HALF, HALF), HALF)
        for kind, out in enumerate(outs):
            out[:, cols] = base[kind]
            out[rows, cols] = jnp.where(inside, back[kind], out[rows, cols])


def finish(info, pieces):
    def source(rows):
        return pl.BlockSpec((2, rows, HALF), lambda i, e: (0, 0, i))

    out = pl.BlockSpec((TOK, 1024), lambda i, e: (0, i))
    return pl.pallas_call(
        finish_kernel,
        grid_spec=pltpu.PrefetchScalarGridSpec(
            num_scalar_prefetch=1,
            grid=(2,),
            in_specs=[source(TOK), source(TOK), source(WIN), source(WIN)],
            out_specs=[out, out],
        ),
        out_shape=[jax.ShapeDtypeStruct((TOK, 2048), BF)] * 2,
        compiler_params=pltpu.CompilerParams(vmem_limit_bytes=32 * MIB),
    )(info, *pieces)


def swap(value):
    return lax.ppermute(value, "c", [(0, 1), (1, 0)])


SEND_A = [(2 * t, 2 * t - 2) for t in range(1, 16)] + [(2 * t + 1, 2 * t + 3) for t in range(15)]
SEND_B = [(2 * t, 2 * t - 1) for t in range(1, 16)] + [(2 * t + 1, 2 * t + 2) for t in range(15)]


def back(pairs):
    return [(b, a) for a, b in pairs]


def shift(phase, amount):
    pairs = []
    for z in range(4):
        for y in range(4):
            for c in range(2):
                for x in range(4):
                    to = {"z": z, "y": y, "x": x}
                    axis = ("xyz", "zxy")[c][phase]
                    to[axis] = (to[axis] + amount) % 4
                    pairs.append((((z * 4 + y) * 2 + c) * 4 + x, ((to["z"] * 4 + to["y"]) * 2 + c) * 4 + to["x"]))
    return pairs


def exchange(parts, phase):
    return [parts[0]] + [lax.ppermute(parts[r], ALL, shift(phase, r)) for r in (1, 3, 2)]


def join_kernel(cols, *refs):
    for n in range(4):
        refs[-1][n] = refs[n][..., cols]


def join(parts, after, cols):
    whole = pl.BlockSpec(memory_space=pltpu.VMEM)
    return pl.pallas_call(
        functools.partial(join_kernel, cols),
        in_specs=[whole] * 4 + [pl.BlockSpec(memory_space=pl.ANY)] * len(after),
        out_specs=whole,
        out_shape=jax.ShapeDtypeStruct((4,) + parts[0].shape[:-1] + (cols.stop - cols.start,), BF),
        compiler_params=pltpu.CompilerParams(vmem_limit_bytes=16 * MIB),
    )(*parts, *after)


def pick_kernel(me, w_ref, got_ref, *refs):
    mine = w_ref[:, pl.ds(pl.multiple_of(me[2] * HALF, HALF), HALF)]
    for core in range(2):

        @pl.when(me[2] == core)
        def _():
            refs[-1][core * 64 : core * 64 + 64, :] = mine
            refs[-1][64 - core * 64 : 128 - core * 64, :] = got_ref[...]


def pick(me, weights, got, after):
    whole = pl.BlockSpec(memory_space=pltpu.VMEM)
    return pl.pallas_call(
        pick_kernel,
        in_specs=[pl.BlockSpec(memory_space=pltpu.SMEM), whole, whole]
        + [pl.BlockSpec(memory_space=pl.ANY)] * len(after),
        out_specs=whole,
        out_shape=jax.ShapeDtypeStruct((128, HALF), BF),
    )(me, weights, got, *after)


def ring(value, phase, amount):
    return lax.ppermute(value, ALL, shift(phase, -amount))


def fold_kernel(a_ref, b_ref, got_a, got_b, after, out_a, out_b):
    for ref, got, out in ((a_ref, got_a, out_a), (b_ref, got_b, out_b)):
        out[...] = (ref[...].astype(jnp.float32) + got[...].astype(jnp.float32)).astype(BF)


def fold(ahead, behind, got_a, got_b, after):
    def block(start):
        return pl.BlockSpec((1, 4, 128, HEAD_DIM), lambda i: (i + start, 0, 0, 0))

    whole = jax.ShapeDtypeStruct(ahead.shape, BF)
    return pl.pallas_call(
        fold_kernel,
        grid=(2,),
        in_specs=[block(0), block(2), block(0), block(0), pl.BlockSpec(memory_space=pl.ANY)],
        out_specs=[block(0), block(2)],
        out_shape=[whole, whole],
        input_output_aliases={0: 0, 1: 1},
        compiler_params=pltpu.CompilerParams(vmem_limit_bytes=16 * MIB),
    )(ahead, behind, got_a, got_b, after)


def scatter_ring(own, ahead, behind, far_a, far_b, after):
    got_a = lax.ppermute(far_a, ALL, shift(0, 1))
    got_b = lax.ppermute(far_b, ALL, shift(0, -1))
    ahead, behind = fold(ahead, behind, got_a, got_b, after)
    return [own, lax.ppermute(ahead, ALL, shift(0, 1)), lax.ppermute(behind, ALL, shift(0, -1))]


def body(enc_hidden, kv_weights, queries, cotangent, enc_lengths, dec_lengths, dec_partner):
    z, y, c, x = (lax.axis_index(a) for a in ALL)
    me = jnp.stack([z, y, c, x]).astype(jnp.int32)
    swapped = swap(enc_hidden)
    meta, info, leave_a, leave_b, give = depart(me, enc_lengths, dec_lengths, dec_partner, queries, cotangent)
    sent_a = lax.ppermute(leave_a, DP, SEND_A)
    sent_b = lax.ppermute(leave_b, DP, SEND_B)

    got = swap(jnp.where(c == 0, kv_weights[:, HALF:], kv_weights[:, :HALF]))
    own = pick(me, kv_weights, got, [leave_a, swapped])
    first = [own] + [ring(own, 2, n) for n in (1, 2, 3)]
    part = join(first, [], slice(0, HALF))
    second = [part] + [ring(part, 1, n) for n in (1, 2, 3)]
    part = join(second, [], slice(0, HEAD_DIM))
    tokens, tokens_t = turn(enc_hidden, swapped, [part])
    ahead, behind = ring(part, 0, 1), ring(part, 0, -1)
    weights = [[part, ahead, behind, ring(behind[:2], 0, -1), ring(ahead[2:], 0, 1)]]
    part = join(second, [ahead, behind, sent_a, sent_b], slice(HEAD_DIM, HALF))
    weights.append([part, ring(part, 0, 1), ring(part, 0, -1), ring(part, 0, 2)])

    shared = (meta, me, tokens, tokens_t)
    inputs = (queries, cotangent, swap(give), sent_a, sent_b)

    *results, d0, d1, d3, d2 = run_main(0, *shared, weights[0], *inputs)
    parts = exchange([d0, d1, d2, d3], 0)
    *results, d0, d1, d3, far_a, far_b = run_main(1, *shared, weights[1], *inputs, before=results)
    mine, other, back_a, back_b = results
    context, grad_queries = finish(
        info,
        [mine, swap(other), lax.ppermute(back_a, DP, back(SEND_A)), lax.ppermute(back_b, DP, back(SEND_B))],
    )

    first = add_parts(parts, [mine])
    parts = scatter_ring(d0, d1, d3, far_a, far_b, first[0])
    second = add_parts(exchange(first, 1))
    last = [exchange(second, 2)]
    second = add_parts(exchange(add_parts(parts, [second[0]]), 1), [context])
    last.append(exchange(second, 2))
    summed = jnp.concatenate(
        [sum(part.astype(jnp.float32) for part in parts) for parts in last], axis=1
    )
    low, high = summed[:64], summed[64:]
    got = swap(jnp.where(c == 0, high, low))
    kept = jnp.where(c == 0, low, high)
    grad = jnp.concatenate([jnp.where(c == 0, kept, got), jnp.where(c == 0, got, kept)], axis=1)
    return context, grad_queries, grad


def solution(mesh):
    fine = Mesh(mesh.devices.reshape(4, 4, 2, 4), ALL)
    rows = P(ALL, None)
    cut = P(DP, "x")
    return jax.shard_map(
        body,
        mesh=fine,
        in_specs=(rows, cut, rows, rows, P(), P(), P()),
        out_specs=(rows, rows, cut),
        check_vma=False,
    )
```

```python
import functools

import jax
import jax.numpy as jnp
from jax import lax
from jax.experimental import pallas as pl
from jax.experimental.pallas import tpu as pltpu
from jax.sharding import Mesh, PartitionSpec as P

HEAD_DIM = 256
SEGS = 4
TOK = 512
PAIR = 2 * TOK
WIN = 176
POOL = PAIR + 2 * WIN
D = 2048
HALF = 512
GROUP = 4
DP = ("z", "y", "c")
ALL = ("z", "y", "c", "x")
MIB = 1024 * 1024
BF = jnp.bfloat16


def align(start, limit):
    return jnp.minimum((start // 16) * 16, limit - WIN)


def mm(a, b, dims):
    return lax.dot_general(a, b, (dims, ((), ())), preferred_element_type=jnp.float32)


def attend(meta, k_s, v_s, q_s, ct_s, ctx_s, gq_s, gk_s, gv_s):
    scale = HEAD_DIM ** -0.5
    col = lax.broadcasted_iota(jnp.int32, (WIN, WIN), 1)
    row = lax.broadcasted_iota(jnp.int32, (WIN, WIN), 0)
    row_wide = lax.broadcasted_iota(jnp.int32, (WIN, HEAD_DIM), 0)
    for first in range(0, 2 * SEGS, GROUP):
        spots, loaded, scores = [], [], []
        for e in range(first, first + GROUP):
            es, el, ds, dl = meta[e, 0], meta[e, 1], meta[e, 2], meta[e, 3]
            ew = pl.multiple_of(align(es, PAIR), 16)
            dw = pl.multiple_of(align(ds, POOL), 16)
            spots.append((pl.ds(ew, WIN), pl.ds(dw, WIN), es - ew, el, ds - dw, dl))
        for ewin, dwin, *_ in spots:
            k, v, q, ct = k_s[ewin, :], v_s[ewin, :], q_s[dwin, :], ct_s[dwin, :]
            loaded.append((k, v, q, ct))
            scores.append((mm(q, k, ((1,), (1,))), mm(ct, v, ((1,), (1,)))))
        weights = []
        for (_, _, elo, el, dlo, dl), (s, gw) in zip(spots, scores):
            k_live = (col >= elo) & (col < elo + el)
            q_live = (row[:, :1] >= dlo) & (row[:, :1] < dlo + dl)
            s = jnp.where(k_live, s * scale, -jnp.inf)
            p = jnp.exp(s - jnp.max(s, axis=1, keepdims=True))
            share = jnp.where(q_live, 1.0 / jnp.sum(p, axis=1, keepdims=True), 0.0)
            w = p * share
            delta = jnp.sum(w * gw, axis=1, keepdims=True)
            weights.append((w.astype(BF), (w * (gw - delta) * scale).astype(BF)))
        results = []
        for (k, v, q, ct), (w_low, gs) in zip(loaded, weights):
            results.append((
                mm(w_low, v, ((1,), (0,))).astype(BF),
                mm(gs, k, ((1,), (0,))).astype(BF),
                mm(gs, q, ((0,), (0,))).astype(BF),
                mm(w_low, ct, ((0,), (0,))).astype(BF),
            ))
        for (ewin, dwin, elo, el, dlo, dl), (ctx, gq, gk, gv) in zip(spots, results):
            d_in = (row_wide >= dlo) & (row_wide < dlo + dl)
            e_in = (row_wide >= elo) & (row_wide < elo + el)
            ctx_s[dwin, :] = jnp.where(d_in, ctx, ctx_s[dwin, :])
            gq_s[dwin, :] = jnp.where(d_in, gq, gq_s[dwin, :])
            gk_s[ewin, :] = jnp.where(e_in, gk, gk_s[ewin, :])
            gv_s[ewin, :] = jnp.where(e_in, gv, gv_s[ewin, :])


def places(me):
    z, y, c, x = me[0], me[1], me[2], me[3]

    def block(ra, rb, rc):
        first = c == 0
        bx = (x + jnp.where(first, ra, rb)) & 3
        by = (y + jnp.where(first, rb, rc)) & 3
        bz = (z + jnp.where(first, rc, ra)) & 3
        return bx, bz * 4 + by

    return block


def main_kernel(weights, extra, meta, me, x_ref, xt_ref, *refs):
    w0, w1, w3, *w2 = refs[:weights]
    qm, qo, qa, qb, cm, co, ca, cb = refs[weights : weights + 8]
    om, oo, oa, ob, d0, d1, d3, *d2 = refs[weights + 8 + extra : -10]
    k_s, v_s, gk_s, gv_s, q_s, ct_s, ctx_s, gq_s, dw_s, w_s = refs[-10:]
    step = pl.program_id(0)
    block = places(me)

    @pl.when(step == 0)
    def _():
        def take(rc, carry):
            for rb in range(4):
                far = w2[rb * len(w2) // 4][rb % (4 // len(w2)), rc]
                for ra, value in enumerate((w0[rb, rc], w1[rb, rc], far, w3[rb, rc])):
                    bx, bzy = block(ra, rb, rc)
                    w_s[bx, pl.ds(pl.multiple_of(bzy * 128, 128), 128), :] = value
            return carry

        lax.fori_loop(0, 4, take, 0)

    x = x_ref[...]
    k_s[...] = jnp.dot(x, w_s[step], preferred_element_type=jnp.float32).astype(BF)
    v_s[...] = jnp.dot(x, w_s[2 + step], preferred_element_type=jnp.float32).astype(BF)
    for pool, parts in ((q_s, (qm, qo, qa, qb)), (ct_s, (cm, co, ca, cb))):
        pool[0:TOK, :] = parts[0][...]
        pool[TOK:PAIR, :] = parts[1][...]
        pool[PAIR : PAIR + WIN, :] = parts[2][...]
        pool[PAIR + WIN :, :] = parts[3][...]
    attend(meta, k_s, v_s, q_s, ct_s, ctx_s, gq_s, gk_s, gv_s)
    for kind, pool in enumerate((ctx_s, gq_s)):
        om[kind] = pool[0:TOK, :]
        oo[kind] = pool[TOK:PAIR, :]
        oa[kind] = pool[PAIR : PAIR + WIN, :]
        ob[kind] = pool[PAIR + WIN :, :]
    xt = xt_ref[...]
    dw_s[step] = jnp.dot(xt, gk_s[...], preferred_element_type=jnp.float32).astype(BF)
    dw_s[2 + step] = jnp.dot(xt, gv_s[...], preferred_element_type=jnp.float32).astype(BF)

    @pl.when(step == 1)
    def _():
        def put(rc, carry):
            for rb in range(4):
                for ra, out in ((0, d0), (1, d1), (3, d3), (2, d2[rb * len(d2) // 4])):
                    bx, bzy = block(ra, rb, rc)
                    at = rb % (4 // len(d2)) if ra == 2 else rb
                    out[at, rc] = dw_s[bx, pl.ds(pl.multiple_of(bzy * 128, 128), 128), :]
            return carry

        lax.fori_loop(0, 4, put, 0)


def run_main(chunk, meta, me, x, xt, weights, q, ct, given, sent_a, sent_b, before=()):
    def fixed(*shape):
        return pl.BlockSpec(shape, lambda i, m, e: (0,) * len(shape), pipeline_mode=pl.Buffered(1))

    def wide():
        return pl.BlockSpec((TOK, HEAD_DIM), lambda i, m, e: (0, i * 4 + e[2] * 2 + chunk))

    def narrow(rows, kind):
        return pl.BlockSpec((rows, HEAD_DIM), lambda i, m, e: (0, kind * 4 + i * 2 + chunk))

    def handed(kind):
        return pl.BlockSpec((TOK, HEAD_DIM), lambda i, m, e: (0, i * 4 + kind * 2 + chunk))

    def out(rows):
        return pl.BlockSpec((2, rows, HEAD_DIM), lambda i, m, e: (0, 0, i * 2 + chunk))

    def out_far():
        return pl.BlockSpec((2, WIN, HEAD_DIM), lambda i, m, e: (0, 0, i))

    def part(shape):
        return pl.BlockSpec(shape, lambda i, m, e: (0, 0, 0, 0))

    parts = [(4, 4, 128, HEAD_DIM)] * 4 if chunk == 0 else [(4, 4, 128, HEAD_DIM)] * 3 + [(2, 4, 128, HEAD_DIM)] * 2
    anywhere = pl.BlockSpec(memory_space=pl.ANY)
    pair = pltpu.VMEM((PAIR, HEAD_DIM), BF)
    pool = pltpu.VMEM((POOL, HEAD_DIM), BF)
    return pl.pallas_call(
        functools.partial(main_kernel, len(weights), len(before)),
        grid_spec=pltpu.PrefetchScalarGridSpec(
            num_scalar_prefetch=2,
            grid=(2,),
            in_specs=[fixed(PAIR, D), fixed(D, PAIR), *[fixed(*w.shape) for w in weights],
                      wide(), handed(0), narrow(WIN, 0), narrow(WIN, 0),
                      wide(), handed(1), narrow(WIN, 1), narrow(WIN, 1)]
            + [anywhere] * len(before),
            out_specs=[out(TOK), out(TOK), out_far(), out_far(), *[part(shape) for shape in parts]],
            scratch_shapes=[pair, pair, pair, pair, pool, pool, pool, pool,
                            pltpu.VMEM((4, D, HEAD_DIM), BF), pltpu.VMEM((4, D, HEAD_DIM), BF)],
        ),
        out_shape=[jax.ShapeDtypeStruct((2, TOK, 2 * HALF), BF)] * 2
        + [jax.ShapeDtypeStruct((2, WIN, HALF), BF)] * 2
        + [jax.ShapeDtypeStruct(shape, BF) for shape in parts],
        input_output_aliases={12 + len(weights) + n: n for n in range(len(before))},
        compiler_params=pltpu.CompilerParams(vmem_limit_bytes=52 * MIB),
        cost_estimate=pl.CostEstimate(flops=12_000_000_000, bytes_accessed=24_000_000, transcendentals=500_000),
    )(meta, me, x, xt, *weights, q, given, sent_a, sent_b, ct, given, sent_a, sent_b, *before)


def add(refs):
    return sum(ref[...].astype(jnp.float32) for ref in refs)


def add_kernel(count, *refs):
    total = add(refs[:count]).astype(BF)
    for n, out in enumerate(refs[-4:]):
        out[...] = total[n]


def add_parts(parts, after):
    return pl.pallas_call(
        functools.partial(add_kernel, len(parts)),
        grid=(4,),
        in_specs=[pl.BlockSpec((4, 1, 128, HEAD_DIM), lambda i: (0, i, 0, 0))] * len(parts)
        + [pl.BlockSpec(memory_space=pl.ANY)] * len(after),
        out_specs=[pl.BlockSpec((1, 128, HEAD_DIM), lambda i: (i, 0, 0))] * 4,
        out_shape=[jax.ShapeDtypeStruct((4, 128, HEAD_DIM), BF)] * 4,
        compiler_params=pltpu.CompilerParams(vmem_limit_bytes=16 * MIB),
    )(*parts, *after)


def add_both_kernel(*refs):
    for chunk in range(2):
        total = add(refs[chunk * 4 : chunk * 4 + 4]).astype(BF)
        for n, out in enumerate(refs[8:]):
            out[:, chunk * HEAD_DIM : (chunk + 1) * HEAD_DIM] = total[n]


def add_both(first, second):
    whole = pl.BlockSpec(memory_space=pltpu.VMEM)
    return pl.pallas_call(
        add_both_kernel,
        in_specs=[whole] * 8,
        out_specs=[whole] * 4,
        out_shape=[jax.ShapeDtypeStruct((128, HALF), BF)] * 4,
        compiler_params=pltpu.CompilerParams(vmem_limit_bytes=16 * MIB),
    )(*first, *second)


def add_last_kernel(me, *refs):
    kept, given = refs[-2:]
    for row, out in ((me[2], kept), (1 - me[2], given)):
        rows = pl.ds(pl.multiple_of(row * 64, 64), 64)
        out[...] = sum(ref[rows, :].astype(jnp.float32) for ref in refs[:4])


def add_last(me, parts, after):
    whole = pl.BlockSpec(memory_space=pltpu.VMEM)
    return pl.pallas_call(
        add_last_kernel,
        in_specs=[pl.BlockSpec(memory_space=pltpu.SMEM)] + [whole] * 4
        + [pl.BlockSpec(memory_space=pl.ANY)] * len(after),
        out_specs=[whole] * 2,
        out_shape=[jax.ShapeDtypeStruct((64, HALF), jnp.float32)] * 2,
        compiler_params=pltpu.CompilerParams(vmem_limit_bytes=16 * MIB),
    )(me, *parts, *after)


def depart_kernel(me, enc_len, dec_len, partner, q_ref, ct_ref, meta, info, a_ref, b_ref, sems):
    core, x = me[2], me[3]
    t = me[0] * 4 + me[1]

    info[0], info[1], info[2], info[3] = jnp.int32(0), core, jnp.int32(0), jnp.int32(0)
    device = (t * 2 + core) * 4 + x
    start = jnp.int32(0)
    for slot in range(SEGS):
        begin, length = start, dec_len[device, slot]

        @pl.when((partner[device, slot] >> 5) != t)
        def _():
            info[0] = align(begin, TOK)
            info[2] = begin
            info[3] = length

        start = start + length

    rows = pl.ds(pl.multiple_of(info[0], 16), WIN)
    copies = []
    for n in range(4):
        source = (q_ref, ct_ref)[n // 2]
        for side, out in ((core, a_ref), (1 - core, b_ref)):
            begin = pl.ds(pl.multiple_of((n % 2) * 1024 + side * HALF, HALF), HALF)
            copies.append((source.at[rows, begin], out.at[:, pl.ds(n * HALF, HALF)]))
    copies = [pltpu.make_async_copy(a, b, sems.at[n]) for n, (a, b) in enumerate(copies)]
    for copy in copies:
        copy.start()

    for side in range(2):
        device = (t * 2 + (core if side == 0 else 1 - core)) * 4 + x
        start = jnp.int32(side * TOK)
        for slot in range(SEGS):
            meta[side * SEGS + slot, 0] = start
            meta[side * SEGS + slot, 1] = enc_len[device, slot]
            start = start + enc_len[device, slot]
    for near in range(4):
        dp = t * 2 - 1 + near
        device = jnp.clip(dp, 0, 31) * 4 + x
        real = (dp >= 0) & (dp < 32)
        same = (dp & 1) == core
        start = jnp.int32(0)
        for slot in range(SEGS):
            begin, length = start, dec_len[device, slot]
            owner = partner[device, slot] >> 4
            if near in (1, 2):
                at = begin + jnp.where(same, 0, TOK)
            else:
                at = begin - align(begin, TOK) + PAIR + jnp.where(same, 0, WIN)

            @pl.when(real & ((owner >> 1) == t))
            def _():
                entry = jnp.where((owner & 1) == core, 0, SEGS) + (partner[device, slot] & 3)
                meta[entry, 2] = at
                meta[entry, 3] = length

            start = start + length
    for copy in copies:
        copy.wait()


def depart(me, enc_lengths, dec_lengths, dec_partner, q, ct):
    whole = pl.BlockSpec(memory_space=pl.ANY)
    scalar = pl.BlockSpec(memory_space=pltpu.SMEM)
    return pl.pallas_call(
        depart_kernel,
        in_specs=[scalar, scalar, scalar, scalar, whole, whole],
        out_specs=[scalar, scalar, whole, whole],
        scratch_shapes=[pltpu.SemaphoreType.DMA((8,))],
        out_shape=[jax.ShapeDtypeStruct((2 * SEGS, 4), jnp.int32), jax.ShapeDtypeStruct((4,), jnp.int32)]
        + [jax.ShapeDtypeStruct((WIN, 2048), BF)] * 2,
        compiler_params=pltpu.CompilerParams(vmem_limit_bytes=60 * MIB),
    )(me, enc_lengths, dec_lengths, dec_partner, q, ct)


def hand_kernel(me, q_ref, ct_ref, *refs):
    refs[-1][:, :HALF] = q_ref[...]
    refs[-1][:, HALF:] = ct_ref[...]


def hand(me, q, ct, after):
    def half(i, me):
        return (0, i * 2 + 1 - me[2])

    part = pl.BlockSpec((TOK, HALF), half)
    return pl.pallas_call(
        hand_kernel,
        grid_spec=pltpu.PrefetchScalarGridSpec(
            num_scalar_prefetch=1,
            grid=(2,),
            in_specs=[part, part] + [pl.BlockSpec(memory_space=pl.ANY)] * len(after),
            out_specs=pl.BlockSpec((TOK, 2 * HALF), lambda i, me: (0, i)),
        ),
        out_shape=jax.ShapeDtypeStruct((TOK, 2048), BF),
        compiler_params=pltpu.CompilerParams(vmem_limit_bytes=16 * MIB),
    )(me, q, ct, *after)


def turn_kernel(a_ref, b_ref, *refs):
    x_ref, xt_ref = refs[-2:]
    for n, ref in enumerate((a_ref, b_ref)):
        value = ref[...]
        x_ref[n * TOK : (n + 1) * TOK, :] = value
        xt_ref[:, n * TOK : (n + 1) * TOK] = value.T


def turn(a, b, after):
    part = pl.BlockSpec((TOK, 512), lambda i: (0, i))
    return pl.pallas_call(
        turn_kernel,
        grid=(D // 512,),
        in_specs=[part, part] + [pl.BlockSpec(memory_space=pl.ANY)] * len(after),
        out_specs=[pl.BlockSpec((PAIR, 512), lambda i: (0, i)), pl.BlockSpec((512, PAIR), lambda i: (i, 0))],
        out_shape=[jax.ShapeDtypeStruct((PAIR, D), BF), jax.ShapeDtypeStruct((D, PAIR), BF)],
        compiler_params=pltpu.CompilerParams(vmem_limit_bytes=16 * MIB),
    )(a, b, *after)


def finish_kernel(info, *refs):
    ins, outs = refs[:6], refs[6:]
    win = pl.multiple_of(info[0], 16)
    core, start, length = info[1], info[2] - info[0], info[3]
    rows = pl.ds(win, WIN)
    place = lax.broadcasted_iota(jnp.int32, (WIN, HEAD_DIM), 0)
    inside = (place >= start) & (place < start + length)
    mine, theirs, *returned = ins
    for side, base, first in ((core, mine, 0), (1 - core, theirs, 1)):
        for chunk in range(2):
            cols = pl.ds(pl.multiple_of(side * HALF + chunk * HEAD_DIM, HEAD_DIM), HEAD_DIM)
            for kind, out in enumerate(outs):
                out[:, cols] = base[kind, :, chunk * HEAD_DIM : (chunk + 1) * HEAD_DIM]
                out[rows, cols] = jnp.where(inside, returned[chunk * 2 + first][kind], out[rows, cols])


def finish(info, pieces):
    def source(rows, cols):
        return pl.BlockSpec((2, rows, cols), lambda i, e: (0, 0, i))

    out = pl.BlockSpec((TOK, 1024), lambda i, e: (0, i))
    return pl.pallas_call(
        finish_kernel,
        grid_spec=pltpu.PrefetchScalarGridSpec(
            num_scalar_prefetch=1,
            grid=(2,),
            in_specs=[source(TOK, HALF)] * 2 + [source(WIN, HEAD_DIM)] * 4,
            out_specs=[out, out],
        ),
        out_shape=[jax.ShapeDtypeStruct((TOK, 2048), BF)] * 2,
        compiler_params=pltpu.CompilerParams(vmem_limit_bytes=32 * MIB),
    )(info, *pieces)


def swap(value):
    return lax.ppermute(value, "c", [(0, 1), (1, 0)])


SEND_A = [(2 * t, 2 * t - 2) for t in range(1, 16)] + [(2 * t + 1, 2 * t + 3) for t in range(15)]
SEND_B = [(2 * t, 2 * t - 1) for t in range(1, 16)] + [(2 * t + 1, 2 * t + 2) for t in range(15)]


def back(pairs):
    return [(b, a) for a, b in pairs]


def shift(phase, amount):
    pairs = []
    for z in range(4):
        for y in range(4):
            for c in range(2):
                for x in range(4):
                    to = {"z": z, "y": y, "x": x}
                    axis = ("xyz", "zxy")[c][phase]
                    to[axis] = (to[axis] + amount) % 4
                    pairs.append((((z * 4 + y) * 2 + c) * 4 + x, ((to["z"] * 4 + to["y"]) * 2 + c) * 4 + to["x"]))
    return pairs


def exchange(parts, phase):
    return [parts[0]] + [lax.ppermute(parts[r], ALL, shift(phase, r)) for r in (1, 3, 2)]


def join_kernel(cols, *refs):
    for n in range(4):
        refs[-1][n] = refs[n][..., cols]


def join(parts, after, cols):
    whole = pl.BlockSpec(memory_space=pltpu.VMEM)
    return pl.pallas_call(
        functools.partial(join_kernel, cols),
        in_specs=[whole] * 4 + [pl.BlockSpec(memory_space=pl.ANY)] * len(after),
        out_specs=whole,
        out_shape=jax.ShapeDtypeStruct((4,) + parts[0].shape[:-1] + (cols.stop - cols.start,), BF),
        compiler_params=pltpu.CompilerParams(vmem_limit_bytes=16 * MIB),
    )(*parts, *after)


def pick_kernel(me, w_ref, got_ref, *refs):
    mine = w_ref[:, pl.ds(pl.multiple_of(me[2] * HALF, HALF), HALF)]
    for core in range(2):

        @pl.when(me[2] == core)
        def _():
            refs[-1][core * 64 : core * 64 + 64, :] = mine
            refs[-1][64 - core * 64 : 128 - core * 64, :] = got_ref[...]


def pick(me, weights, got, after):
    whole = pl.BlockSpec(memory_space=pltpu.VMEM)
    return pl.pallas_call(
        pick_kernel,
        in_specs=[pl.BlockSpec(memory_space=pltpu.SMEM), whole, whole]
        + [pl.BlockSpec(memory_space=pl.ANY)] * len(after),
        out_specs=whole,
        out_shape=jax.ShapeDtypeStruct((128, HALF), BF),
        compiler_params=pltpu.CompilerParams(vmem_limit_bytes=16 * MIB),
    )(me, weights, got, *after)


def ring(value, phase, amount):
    return lax.ppermute(value, ALL, shift(phase, -amount))


def fold_kernel(a_ref, b_ref, got_a, got_b, after, out_a, out_b):
    for ref, got, out in ((a_ref, got_a, out_a), (b_ref, got_b, out_b)):
        out[...] = (ref[...].astype(jnp.float32) + got[...].astype(jnp.float32)).astype(BF)


def fold(ahead, behind, got_a, got_b, after):
    def block(start):
        return pl.BlockSpec((1, 4, 128, HEAD_DIM), lambda i: (i + start, 0, 0, 0))

    whole = jax.ShapeDtypeStruct(ahead.shape, BF)
    return pl.pallas_call(
        fold_kernel,
        grid=(2,),
        in_specs=[block(0), block(2), block(0), block(0), pl.BlockSpec(memory_space=pl.ANY)],
        out_specs=[block(0), block(2)],
        out_shape=[whole, whole],
        input_output_aliases={0: 0, 1: 1},
        compiler_params=pltpu.CompilerParams(vmem_limit_bytes=16 * MIB),
    )(ahead, behind, got_a, got_b, after)


def scatter_ring(own, ahead, behind, far_a, far_b, after):
    got_a = lax.ppermute(far_a, ALL, shift(0, 1))
    got_b = lax.ppermute(far_b, ALL, shift(0, -1))
    ahead, behind = fold(ahead, behind, got_a, got_b, after)
    return [own, lax.ppermute(ahead, ALL, shift(0, 1)), lax.ppermute(behind, ALL, shift(0, -1))]


def body(enc_hidden, kv_weights, queries, cotangent, enc_lengths, dec_lengths, dec_partner):
    z, y, c, x = (lax.axis_index(a) for a in ALL)
    me = jnp.stack([z, y, c, x]).astype(jnp.int32)
    swapped = swap(enc_hidden)
    meta, info, leave_a, leave_b = depart(me, enc_lengths, dec_lengths, dec_partner, queries, cotangent)
    sent_a = lax.ppermute(leave_a, DP, SEND_A)
    sent_b = lax.ppermute(leave_b, DP, SEND_B)

    got = swap(jnp.where(c == 0, kv_weights[:, HALF:], kv_weights[:, :HALF]))
    own = pick(me, kv_weights, got, [leave_a, swapped])
    first = [own] + [ring(own, 2, n) for n in (1, 2, 3)]
    part = join(first, [sent_a], slice(0, HALF))
    second = [part] + [ring(part, 1, n) for n in (1, 2, 3)]
    tokens, tokens_t = turn(enc_hidden, swapped, [second[1]])
    given = hand(me, queries, cotangent, [tokens_t])
    part = join(second, [given], slice(0, HEAD_DIM))
    ahead, behind = ring(part, 0, 1), ring(part, 0, -1)
    weights = [[part, ahead, behind, ring(behind[:2], 0, -1), ring(ahead[2:], 0, 1)]]
    part = join(second, [ahead, behind], slice(HEAD_DIM, HALF))
    weights.append([part, ring(part, 0, 1), ring(part, 0, -1), ring(part, 0, 2)])

    shared = (meta, me, tokens, tokens_t)
    inputs = (queries, cotangent, swap(given), sent_a, sent_b)
    home = [back(SEND_A), back(SEND_B)]

    *results, d0, d1, d3, d2 = run_main(0, *shared, weights[0], *inputs)
    returned = [lax.ppermute(part, DP, pairs) for part, pairs in zip(results[2:], home)]
    parts = exchange([d0, d1, d2, d3], 0)
    *results, d0, d1, d3, far_a, far_b = run_main(1, *shared, weights[1], *inputs, before=results[:2])
    mine, other = results[:2]
    late = [lax.ppermute(part, DP, pairs) for part, pairs in zip(results[2:], home)]

    first = add_parts(parts, [mine, *returned])
    parts = scatter_ring(d0, d1, d3, far_a, far_b, first[0])
    first = exchange(first, 1)
    second = exchange(add_parts(parts, late), 1)
    context, grad_queries = finish(info, [mine, swap(other), *returned, *late])
    kept, given = add_last(me, exchange(add_both(first, second), 2), [context])
    got = swap(given)
    grad = jnp.concatenate([jnp.where(c == 0, kept, got), jnp.where(c == 0, got, kept)], axis=1)
    return context, grad_queries, grad


def solution(mesh):
    fine = Mesh(mesh.devices.reshape(4, 4, 2, 4), ALL)
    rows = P(ALL, None)
    cut = P(DP, "x")
    return jax.shard_map(
        body,
        mesh=fine,
        in_specs=(rows, cut, rows, rows, P(), P(), P()),
        out_specs=(rows, rows, cut),
        check_vma=False,
    )
```

```python
import functools

import jax
import jax.numpy as jnp
from jax import lax
from jax.experimental import pallas as pl
from jax.experimental.pallas import tpu as pltpu
from jax.sharding import Mesh, PartitionSpec as P

HEAD_DIM = 256
SEGS = 4
TOK = 512
PAIR = 2 * TOK
WIN = 176
POOL = PAIR + 2 * WIN
D = 2048
HALF = 512
GROUP = 4
DP = ("z", "y", "c")
ALL = ("z", "y", "c", "x")
MIB = 1024 * 1024
BF = jnp.bfloat16


def align(start, limit):
    return jnp.minimum((start // 16) * 16, limit - WIN)


def mm(a, b, dims):
    return lax.dot_general(a, b, (dims, ((), ())), preferred_element_type=jnp.float32)


def attend(meta, k_s, v_s, q_s, ct_s, ctx_s, gq_s, gk_s, gv_s):
    scale = HEAD_DIM ** -0.5
    col = lax.broadcasted_iota(jnp.int32, (WIN, WIN), 1)
    row = lax.broadcasted_iota(jnp.int32, (WIN, WIN), 0)
    row_wide = lax.broadcasted_iota(jnp.int32, (WIN, HEAD_DIM), 0)
    for first in range(0, 2 * SEGS, GROUP):
        spots, loaded, scores = [], [], []
        for e in range(first, first + GROUP):
            es, el, ds, dl = meta[e, 0], meta[e, 1], meta[e, 2], meta[e, 3]
            ew = pl.multiple_of(align(es, PAIR), 16)
            dw = pl.multiple_of(align(ds, POOL), 16)
            spots.append((pl.ds(ew, WIN), pl.ds(dw, WIN), es - ew, el, ds - dw, dl))
        for ewin, dwin, *_ in spots:
            k, v, q, ct = k_s[ewin, :], v_s[ewin, :], q_s[dwin, :], ct_s[dwin, :]
            loaded.append((k, v, q, ct))
            scores.append((mm(q, k, ((1,), (1,))), mm(ct, v, ((1,), (1,)))))
        weights = []
        for (_, _, elo, el, dlo, dl), (s, gw) in zip(spots, scores):
            k_live = (col >= elo) & (col < elo + el)
            q_live = (row[:, :1] >= dlo) & (row[:, :1] < dlo + dl)
            s = jnp.where(k_live, s * scale, -jnp.inf)
            p = jnp.exp(s - jnp.max(s, axis=1, keepdims=True))
            share = jnp.where(q_live, 1.0 / jnp.sum(p, axis=1, keepdims=True), 0.0)
            w = p * share
            delta = jnp.sum(w * gw, axis=1, keepdims=True)
            weights.append((w.astype(BF), (w * (gw - delta) * scale).astype(BF)))
        results = []
        for (k, v, q, ct), (w_low, gs) in zip(loaded, weights):
            results.append((
                mm(w_low, v, ((1,), (0,))).astype(BF),
                mm(gs, k, ((1,), (0,))).astype(BF),
                mm(gs, q, ((0,), (0,))).astype(BF),
                mm(w_low, ct, ((0,), (0,))).astype(BF),
            ))
        for (ewin, dwin, elo, el, dlo, dl), (ctx, gq, gk, gv) in zip(spots, results):
            d_in = (row_wide >= dlo) & (row_wide < dlo + dl)
            e_in = (row_wide >= elo) & (row_wide < elo + el)
            ctx_s[dwin, :] = jnp.where(d_in, ctx, ctx_s[dwin, :])
            gq_s[dwin, :] = jnp.where(d_in, gq, gq_s[dwin, :])
            gk_s[ewin, :] = jnp.where(e_in, gk, gk_s[ewin, :])
            gv_s[ewin, :] = jnp.where(e_in, gv, gv_s[ewin, :])


def places(me):
    z, y, c, x = me[0], me[1], me[2], me[3]

    def block(ra, rb, rc):
        first = c == 0
        bx = (x + jnp.where(first, ra, rb)) & 3
        by = (y + jnp.where(first, rb, rc)) & 3
        bz = (z + jnp.where(first, rc, ra)) & 3
        return bx, bz * 4 + by

    return block


def main_kernel(weights, extra, meta, me, x_ref, xt_ref, *refs):
    qm, qo, qa, qb, cm, co, ca, cb = refs[weights : weights + 8]
    om, oo, oa, ob, d0, d1, d3, *d2 = refs[weights + 8 + extra : -10]
    k_s, v_s, gk_s, gv_s, q_s, ct_s, ctx_s, gq_s, dw_s, w_s = refs[-10:]
    step = pl.program_id(0)
    block = places(me)

    if weights == 2:
        wk, wv = (ref[...].reshape(D, HEAD_DIM) for ref in refs[:2])
    else:
        w0, w1, w3, *w2 = refs[:weights]

        @pl.when(step == 0)
        def _():
            def take(rc, carry):
                for rb in range(4):
                    far = w2[rb // 2][rb % 2, rc]
                    for ra, value in enumerate((w0[rb, rc], w1[rb, rc], far, w3[rb, rc])):
                        bx, bzy = block(ra, rb, rc)
                        w_s[bx, pl.ds(pl.multiple_of(bzy * 128, 128), 128), :] = value
                return carry

            lax.fori_loop(0, 4, take, 0)

        wk, wv = w_s[step], w_s[2 + step]
    x = x_ref[...]
    k_s[...] = jnp.dot(x, wk, preferred_element_type=jnp.float32).astype(BF)
    v_s[...] = jnp.dot(x, wv, preferred_element_type=jnp.float32).astype(BF)
    for pool, parts in ((q_s, (qm, qo, qa, qb)), (ct_s, (cm, co, ca, cb))):
        pool[0:TOK, :] = parts[0][...]
        pool[TOK:PAIR, :] = parts[1][...]
        pool[PAIR : PAIR + WIN, :] = parts[2][...]
        pool[PAIR + WIN :, :] = parts[3][...]
    attend(meta, k_s, v_s, q_s, ct_s, ctx_s, gq_s, gk_s, gv_s)
    for kind, pool in enumerate((ctx_s, gq_s)):
        om[kind] = pool[0:TOK, :]
        oo[kind] = pool[TOK:PAIR, :]
        oa[kind] = pool[PAIR : PAIR + WIN, :]
        ob[kind] = pool[PAIR + WIN :, :]
    xt = xt_ref[...]
    dw_s[step] = jnp.dot(xt, gk_s[...], preferred_element_type=jnp.float32).astype(BF)
    dw_s[2 + step] = jnp.dot(xt, gv_s[...], preferred_element_type=jnp.float32).astype(BF)

    @pl.when(step == 1)
    def _():
        def put(rc, carry):
            for rb in range(4):
                for ra, out in ((0, d0), (1, d1), (3, d3), (2, d2[rb * len(d2) // 4])):
                    bx, bzy = block(ra, rb, rc)
                    at = rb % (4 // len(d2)) if ra == 2 else rb
                    out[at, rc] = dw_s[bx, pl.ds(pl.multiple_of(bzy * 128, 128), 128), :]
            return carry

        lax.fori_loop(0, 4, put, 0)


def run_main(chunk, meta, me, x, xt, weights, q, ct, given, sent_a, sent_b, before=()):
    def fixed(*shape):
        return pl.BlockSpec(shape, lambda i, m, e: (0,) * len(shape), pipeline_mode=pl.Buffered(1))

    def wide():
        return pl.BlockSpec((TOK, HEAD_DIM), lambda i, m, e: (0, i * 4 + e[2] * 2 + chunk))

    def narrow(rows, kind):
        return pl.BlockSpec((rows, HEAD_DIM), lambda i, m, e: (0, kind * 4 + i * 2 + chunk))

    def gathered(kind):
        return pl.BlockSpec((32, 1, 64, HEAD_DIM), lambda i, m, e: (0, kind * 2 + i, 0, e[2]))

    def handed(kind):
        return pl.BlockSpec((TOK, HEAD_DIM), lambda i, m, e: (0, i * 4 + kind * 2 + chunk))

    def out(rows):
        return pl.BlockSpec((2, rows, HEAD_DIM), lambda i, m, e: (0, 0, i * 2 + chunk))

    def out_far():
        return pl.BlockSpec((2, WIN, HEAD_DIM), lambda i, m, e: (0, 0, i))

    def part(shape):
        return pl.BlockSpec(shape, lambda i, m, e: (0, 0, 0, 0))

    parts = [(4, 4, 128, HEAD_DIM)] * 4 if chunk == 0 else [(4, 4, 128, HEAD_DIM)] * 3 + [(2, 4, 128, HEAD_DIM)] * 2
    anywhere = pl.BlockSpec(memory_space=pl.ANY)
    if len(weights) == 1:
        weights = [*weights, *weights]
        weight_specs = [gathered(0), gathered(1)]
    else:
        weight_specs = [fixed(*w.shape) for w in weights]
    pair = pltpu.VMEM((PAIR, HEAD_DIM), BF)
    pool = pltpu.VMEM((POOL, HEAD_DIM), BF)
    return pl.pallas_call(
        functools.partial(main_kernel, len(weights), len(before)),
        grid_spec=pltpu.PrefetchScalarGridSpec(
            num_scalar_prefetch=2,
            grid=(2,),
            in_specs=[fixed(PAIR, D), fixed(D, PAIR), *weight_specs,
                      wide(), handed(0), narrow(WIN, 0), narrow(WIN, 0),
                      wide(), handed(1), narrow(WIN, 1), narrow(WIN, 1)]
            + [anywhere] * len(before),
            out_specs=[out(TOK), out(TOK), out_far(), out_far(), *[part(shape) for shape in parts]],
            scratch_shapes=[pair, pair, pair, pair, pool, pool, pool, pool,
                            pltpu.VMEM((4, D, HEAD_DIM), BF), pltpu.VMEM((4, D, HEAD_DIM), BF)],
        ),
        out_shape=[jax.ShapeDtypeStruct((2, TOK, 2 * HALF), BF)] * 2
        + [jax.ShapeDtypeStruct((2, WIN, HALF), BF)] * 2
        + [jax.ShapeDtypeStruct(shape, BF) for shape in parts],
        input_output_aliases={12 + len(weights) + n: n for n in range(len(before))},
        compiler_params=pltpu.CompilerParams(vmem_limit_bytes=44 * MIB),
        cost_estimate=pl.CostEstimate(flops=12_000_000_000, bytes_accessed=24_000_000, transcendentals=500_000),
    )(meta, me, x, xt, *weights, q, given, sent_a, sent_b, ct, given, sent_a, sent_b, *before)


def add(refs):
    return sum(ref[...].astype(jnp.float32) for ref in refs)


def add_kernel(count, *refs):
    total = add(refs[:count]).astype(BF)
    for n, out in enumerate(refs[-4:]):
        out[...] = total[n]


def add_parts(parts, after):
    return pl.pallas_call(
        functools.partial(add_kernel, len(parts)),
        grid=(4,),
        in_specs=[pl.BlockSpec((4, 1, 128, HEAD_DIM), lambda i: (0, i, 0, 0))] * len(parts)
        + [pl.BlockSpec(memory_space=pl.ANY)] * len(after),
        out_specs=[pl.BlockSpec((1, 128, HEAD_DIM), lambda i: (i, 0, 0))] * 4,
        out_shape=[jax.ShapeDtypeStruct((4, 128, HEAD_DIM), BF)] * 4,
        compiler_params=pltpu.CompilerParams(vmem_limit_bytes=16 * MIB),
    )(*parts, *after)


def add_both_kernel(*refs):
    for chunk in range(2):
        total = add(refs[chunk * 4 : chunk * 4 + 4]).astype(BF)
        for n, out in enumerate(refs[8:]):
            out[:, chunk * HEAD_DIM : (chunk + 1) * HEAD_DIM] = total[n]


def add_both(first, second):
    whole = pl.BlockSpec(memory_space=pltpu.VMEM)
    return pl.pallas_call(
        add_both_kernel,
        in_specs=[whole] * 8,
        out_specs=[whole] * 4,
        out_shape=[jax.ShapeDtypeStruct((128, HALF), BF)] * 4,
        compiler_params=pltpu.CompilerParams(vmem_limit_bytes=16 * MIB),
    )(*first, *second)


def add_last_kernel(me, *refs):
    kept, given = refs[-2:]
    for row, out in ((me[2], kept), (1 - me[2], given)):
        rows = pl.ds(pl.multiple_of(row * 64, 64), 64)
        out[...] = sum(ref[rows, :].astype(jnp.float32) for ref in refs[:4])


def add_last(me, parts, after):
    whole = pl.BlockSpec(memory_space=pltpu.VMEM)
    return pl.pallas_call(
        add_last_kernel,
        in_specs=[pl.BlockSpec(memory_space=pltpu.SMEM)] + [whole] * 4
        + [pl.BlockSpec(memory_space=pl.ANY)] * len(after),
        out_specs=[whole] * 2,
        out_shape=[jax.ShapeDtypeStruct((64, HALF), jnp.float32)] * 2,
        compiler_params=pltpu.CompilerParams(vmem_limit_bytes=16 * MIB),
    )(me, *parts, *after)


def depart_kernel(me, enc_len, dec_len, partner, q_ref, ct_ref, meta, info, a_ref, b_ref, sems):
    core, x = me[2], me[3]
    t = me[0] * 4 + me[1]

    info[0], info[1], info[2], info[3] = jnp.int32(0), core, jnp.int32(0), jnp.int32(0)
    device = (t * 2 + core) * 4 + x
    start = jnp.int32(0)
    for slot in range(SEGS):
        begin, length = start, dec_len[slot, device]

        @pl.when((partner[slot, device] >> 5) != t)
        def _():
            info[0] = align(begin, TOK)
            info[2] = begin
            info[3] = length

        start = start + length

    rows = pl.ds(pl.multiple_of(info[0], 16), WIN)
    copies = []
    for n in range(4):
        source = (q_ref, ct_ref)[n // 2]
        for side, out in ((core, a_ref), (1 - core, b_ref)):
            begin = pl.ds(pl.multiple_of((n % 2) * 1024 + side * HALF, HALF), HALF)
            copies.append((source.at[rows, begin], out.at[:, pl.ds(n * HALF, HALF)]))
    copies = [pltpu.make_async_copy(a, b, sems.at[n]) for n, (a, b) in enumerate(copies)]
    for copy in copies:
        copy.start()

    for side in range(2):
        device = (t * 2 + (core if side == 0 else 1 - core)) * 4 + x
        start = jnp.int32(side * TOK)
        for slot in range(SEGS):
            meta[side * SEGS + slot, 0] = start
            meta[side * SEGS + slot, 1] = enc_len[slot, device]
            start = start + enc_len[slot, device]
    for near in range(4):
        dp = t * 2 - 1 + near
        device = jnp.clip(dp, 0, 31) * 4 + x
        real = (dp >= 0) & (dp < 32)
        same = (dp & 1) == core
        start = jnp.int32(0)
        for slot in range(SEGS):
            begin, length = start, dec_len[slot, device]
            owner = partner[slot, device] >> 4
            if near in (1, 2):
                at = begin + jnp.where(same, 0, TOK)
            else:
                at = begin - align(begin, TOK) + PAIR + jnp.where(same, 0, WIN)

            @pl.when(real & ((owner >> 1) == t))
            def _():
                entry = jnp.where((owner & 1) == core, 0, SEGS) + (partner[slot, device] & 3)
                meta[entry, 2] = at
                meta[entry, 3] = length

            start = start + length
    for copy in copies:
        copy.wait()


def depart(me, enc_lengths, dec_lengths, dec_partner, q, ct):
    whole = pl.BlockSpec(memory_space=pl.ANY)
    scalar = pl.BlockSpec(memory_space=pltpu.SMEM)
    return pl.pallas_call(
        depart_kernel,
        in_specs=[scalar, scalar, scalar, scalar, whole, whole],
        out_specs=[scalar, scalar, pl.BlockSpec(memory_space=pltpu.VMEM), pl.BlockSpec(memory_space=pltpu.VMEM)],
        scratch_shapes=[pltpu.SemaphoreType.DMA((8,))],
        out_shape=[jax.ShapeDtypeStruct((2 * SEGS, 4), jnp.int32), jax.ShapeDtypeStruct((4,), jnp.int32)]
        + [jax.ShapeDtypeStruct((WIN, 2048), BF)] * 2,
        compiler_params=pltpu.CompilerParams(vmem_limit_bytes=59 * MIB),
    )(me, enc_lengths.T, dec_lengths.T, dec_partner.T, q, ct)


def hand_kernel(me, q_ref, ct_ref, *refs):
    refs[-1][:, :HALF] = q_ref[...]
    refs[-1][:, HALF:] = ct_ref[...]


def hand(me, q, ct, after):
    def half(i, me):
        return (0, i * 2 + 1 - me[2])

    part = pl.BlockSpec((TOK, HALF), half)
    return pl.pallas_call(
        hand_kernel,
        grid_spec=pltpu.PrefetchScalarGridSpec(
            num_scalar_prefetch=1,
            grid=(2,),
            in_specs=[part, part] + [pl.BlockSpec(memory_space=pl.ANY)] * len(after),
            out_specs=pl.BlockSpec((TOK, 2 * HALF), lambda i, me: (0, i)),
        ),
        out_shape=jax.ShapeDtypeStruct((TOK, 2048), BF),
        compiler_params=pltpu.CompilerParams(vmem_limit_bytes=16 * MIB),
    )(me, q, ct, *after)


def turn_kernel(a_ref, b_ref, *refs):
    x_ref, xt_ref = refs[-2:]
    for n, ref in enumerate((a_ref, b_ref)):
        value = ref[...]
        x_ref[n * TOK : (n + 1) * TOK, :] = value
        xt_ref[:, n * TOK : (n + 1) * TOK] = value.T


def turn(a, b, after):
    part = pl.BlockSpec((TOK, 512), lambda i: (0, i))
    return pl.pallas_call(
        turn_kernel,
        grid=(D // 512,),
        in_specs=[part, part] + [pl.BlockSpec(memory_space=pl.ANY)] * len(after),
        out_specs=[pl.BlockSpec((PAIR, 512), lambda i: (0, i)), pl.BlockSpec((512, PAIR), lambda i: (i, 0))],
        out_shape=[jax.ShapeDtypeStruct((PAIR, D), BF), jax.ShapeDtypeStruct((D, PAIR), BF)],
        compiler_params=pltpu.CompilerParams(vmem_limit_bytes=16 * MIB),
    )(a, b, *after)


def finish_kernel(info, *refs):
    ins, outs = refs[:6], refs[6:]
    win = pl.multiple_of(info[0], 16)
    core, start, length = info[1], info[2] - info[0], info[3]
    rows = pl.ds(win, WIN)
    place = lax.broadcasted_iota(jnp.int32, (WIN, HEAD_DIM), 0)
    inside = (place >= start) & (place < start + length)
    mine, theirs, *returned = ins
    for side, base, first in ((core, mine, 0), (1 - core, theirs, 1)):
        for chunk in range(2):
            cols = pl.ds(pl.multiple_of(side * HALF + chunk * HEAD_DIM, HEAD_DIM), HEAD_DIM)
            for kind, out in enumerate(outs):
                out[:, cols] = base[kind, :, chunk * HEAD_DIM : (chunk + 1) * HEAD_DIM]
                out[rows, cols] = jnp.where(inside, returned[chunk * 2 + first][kind], out[rows, cols])


def finish(info, pieces):
    def source(rows, cols):
        return pl.BlockSpec((2, rows, cols), lambda i, e: (0, 0, i))

    out = pl.BlockSpec((TOK, 1024), lambda i, e: (0, i))
    return pl.pallas_call(
        finish_kernel,
        grid_spec=pltpu.PrefetchScalarGridSpec(
            num_scalar_prefetch=1,
            grid=(2,),
            in_specs=[source(TOK, HALF)] * 2 + [source(WIN, HEAD_DIM)] * 4,
            out_specs=[out, out],
        ),
        out_shape=[jax.ShapeDtypeStruct((TOK, 2048), BF)] * 2,
        compiler_params=pltpu.CompilerParams(vmem_limit_bytes=32 * MIB),
    )(info, *pieces)


def swap(value):
    return lax.ppermute(value, "c", [(0, 1), (1, 0)])


SEND_A = [(2 * t, 2 * t - 2) for t in range(1, 16)] + [(2 * t + 1, 2 * t + 3) for t in range(15)]
SEND_B = [(2 * t, 2 * t - 1) for t in range(1, 16)] + [(2 * t + 1, 2 * t + 2) for t in range(15)]


def back(pairs):
    return [(b, a) for a, b in pairs]


def shift(phase, amount):
    pairs = []
    for z in range(4):
        for y in range(4):
            for c in range(2):
                for x in range(4):
                    to = {"z": z, "y": y, "x": x}
                    axis = ("xyz", "zxy")[c][phase]
                    to[axis] = (to[axis] + amount) % 4
                    pairs.append((((z * 4 + y) * 2 + c) * 4 + x, ((to["z"] * 4 + to["y"]) * 2 + c) * 4 + to["x"]))
    return pairs


def exchange(parts, phase):
    return [parts[0]] + [lax.ppermute(parts[r], ALL, shift(phase, r)) for r in (1, 3, 2)]


def join_kernel(*refs):
    for n in range(4):
        refs[-1][n] = refs[n][...]


def join(parts, after):
    whole = pl.BlockSpec(memory_space=pltpu.VMEM)
    return pl.pallas_call(
        join_kernel,
        in_specs=[whole] * 4 + [pl.BlockSpec(memory_space=pl.ANY)] * len(after),
        out_specs=whole,
        out_shape=jax.ShapeDtypeStruct((4,) + parts[0].shape, BF),
        compiler_params=pltpu.CompilerParams(vmem_limit_bytes=16 * MIB),
    )(*parts, *after)


def pick_kernel(me, w_ref, got_ref, out_ref):
    mine = w_ref[:, pl.ds(pl.multiple_of(me[2] * HALF, HALF), HEAD_DIM)]
    for core in range(2):

        @pl.when(me[2] == core)
        def _():
            out_ref[core * 64 : core * 64 + 64, :] = mine
            out_ref[64 - core * 64 : 128 - core * 64, :] = got_ref[...]


def pick(me, weights, got):
    whole = pl.BlockSpec(memory_space=pltpu.VMEM)
    return pl.pallas_call(
        pick_kernel,
        in_specs=[pl.BlockSpec(memory_space=pltpu.SMEM), whole, whole],
        out_specs=whole,
        out_shape=jax.ShapeDtypeStruct((128, HEAD_DIM), BF),
        compiler_params=pltpu.CompilerParams(vmem_limit_bytes=16 * MIB),
    )(me, weights, got)


def ring(value, phase, amount):
    return lax.ppermute(value, ALL, shift(phase, -amount))


def fold_kernel(a_ref, b_ref, got_a, got_b, after, out_a, out_b):
    for ref, got, out in ((a_ref, got_a, out_a), (b_ref, got_b, out_b)):
        out[...] = (ref[...].astype(jnp.float32) + got[...].astype(jnp.float32)).astype(BF)


def fold(ahead, behind, got_a, got_b, after):
    def block(start):
        return pl.BlockSpec((1, 4, 128, HEAD_DIM), lambda i: (i + start, 0, 0, 0))

    whole = jax.ShapeDtypeStruct(ahead.shape, BF)
    return pl.pallas_call(
        fold_kernel,
        grid=(2,),
        in_specs=[block(0), block(2), block(0), block(0), pl.BlockSpec(memory_space=pl.ANY)],
        out_specs=[block(0), block(2)],
        out_shape=[whole, whole],
        input_output_aliases={0: 0, 1: 1},
        compiler_params=pltpu.CompilerParams(vmem_limit_bytes=16 * MIB),
    )(ahead, behind, got_a, got_b, after)


def scatter_ring(own, ahead, behind, far_a, far_b, after):
    got_a = lax.ppermute(far_a, ALL, shift(0, 1))
    got_b = lax.ppermute(far_b, ALL, shift(0, -1))
    ahead, behind = fold(ahead, behind, got_a, got_b, after)
    return [own, lax.ppermute(ahead, ALL, shift(0, 1)), lax.ppermute(behind, ALL, shift(0, -1))]


def body(enc_hidden, kv_weights, queries, cotangent, enc_lengths, dec_lengths, dec_partner):
    z, y, c, x = (lax.axis_index(a) for a in ALL)
    me = jnp.stack([z, y, c, x]).astype(jnp.int32)
    cols = [kv_weights[:, n * HEAD_DIM : (n + 1) * HEAD_DIM] for n in range(4)]
    later = lax.all_gather(jnp.concatenate([cols[1], cols[3]], axis=1), ALL, axis=0).reshape(32, 4, 64, HALF)

    got = swap(jnp.where(c == 0, cols[2], cols[0]))
    own = pick(me, kv_weights, got)
    first = [own] + [ring(own, 2, n) for n in (1, 2, 3)]
    meta, info, leave_a, leave_b = depart(me, enc_lengths, dec_lengths, dec_partner, queries, cotangent)
    sent_a = lax.ppermute(leave_a, DP, SEND_A)
    sent_b = lax.ppermute(leave_b, DP, SEND_B)
    given = hand(me, queries, cotangent, [leave_a])
    part = join(first, [given])
    second = [part] + [ring(part, 1, n) for n in (1, 2, 3)]
    part = join(second, [])
    tokens, tokens_t = turn(enc_hidden, swap(enc_hidden), [part, sent_a])
    ahead, behind = ring(part, 0, 1), ring(part, 0, -1)
    weights = [[part, ahead, behind, ring(behind[:2], 0, -1), ring(ahead[2:], 0, 1)], [later]]

    shared = (meta, me, tokens, tokens_t)
    inputs = (queries, cotangent, swap(given), sent_a, sent_b)
    home = [back(SEND_A), back(SEND_B)]

    *results, d0, d1, d3, d2 = run_main(0, *shared, weights[0], *inputs)
    returned = [lax.ppermute(part, DP, pairs) for part, pairs in zip(results[2:], home)]
    parts = exchange([d0, d1, d2, d3], 0)
    *results, d0, d1, d3, far_a, far_b = run_main(1, *shared, weights[1], *inputs, before=results[:2])
    mine, other = results[:2]
    late = [lax.ppermute(part, DP, pairs) for part, pairs in zip(results[2:], home)]

    first = add_parts(parts, [mine, *returned])
    parts = scatter_ring(d0, d1, d3, far_a, far_b, first[0])
    first = exchange(first, 1)
    second = exchange(add_parts(parts, late), 1)
    context, grad_queries = finish(info, [mine, swap(other), *returned, *late])
    kept, given = add_last(me, exchange(add_both(first, second), 2), [context])
    got = swap(given)
    grad = jnp.concatenate([jnp.where(c == 0, kept, got), jnp.where(c == 0, got, kept)], axis=1)
    return context, grad_queries, grad


def solution(mesh):
    fine = Mesh(mesh.devices.reshape(4, 4, 2, 4), ALL)
    rows = P(ALL, None)
    cut = P(DP, "x")
    return jax.shard_map(
        body,
        mesh=fine,
        in_specs=(rows, cut, rows, rows, P(), P(), P()),
        out_specs=(rows, rows, cut),
        check_vma=False,
    )
```

```python
import functools

import jax
import jax.numpy as jnp
from jax import lax
from jax.experimental import pallas as pl
from jax.experimental.pallas import tpu as pltpu
from jax.sharding import Mesh, PartitionSpec as P

HEAD_DIM = 256
SEGS = 4
TOK = 512
PAIR = 2 * TOK
WIN = 176
POOL = PAIR + 2 * WIN
D = 2048
HALF = 512
GROUP = 4
DP = ("z", "y", "c")
ALL = ("z", "y", "c", "x")
MIB = 1024 * 1024
BF = jnp.bfloat16


def align(start, limit):
    return jnp.minimum((start // 16) * 16, limit - WIN)


def mm(a, b, dims):
    return lax.dot_general(a, b, (dims, ((), ())), preferred_element_type=jnp.float32)


def attend(meta, k_s, v_s, q_s, ct_s, ctx_s, gq_s, gk_s, gv_s):
    scale = HEAD_DIM ** -0.5
    col = lax.broadcasted_iota(jnp.int32, (WIN, WIN), 1)
    row = lax.broadcasted_iota(jnp.int32, (WIN, WIN), 0)
    row_wide = lax.broadcasted_iota(jnp.int32, (WIN, HEAD_DIM), 0)
    for first in range(0, 2 * SEGS, GROUP):
        spots, loaded, scores = [], [], []
        for e in range(first, first + GROUP):
            es, el, ds, dl = meta[e, 0], meta[e, 1], meta[e, 2], meta[e, 3]
            ew = pl.multiple_of(align(es, PAIR), 16)
            dw = pl.multiple_of(align(ds, POOL), 16)
            spots.append((pl.ds(ew, WIN), pl.ds(dw, WIN), es - ew, el, ds - dw, dl))
        for ewin, dwin, *_ in spots:
            k, v, q, ct = k_s[ewin, :], v_s[ewin, :], q_s[dwin, :], ct_s[dwin, :]
            loaded.append((k, v, q, ct))
            scores.append((mm(q, k, ((1,), (1,))), mm(ct, v, ((1,), (1,)))))
        weights = []
        for (_, _, elo, el, dlo, dl), (s, gw) in zip(spots, scores):
            k_live = (col >= elo) & (col < elo + el)
            q_live = (row[:, :1] >= dlo) & (row[:, :1] < dlo + dl)
            s = jnp.where(k_live, s * scale, -jnp.inf)
            p = jnp.exp(s - jnp.max(s, axis=1, keepdims=True))
            share = jnp.where(q_live, 1.0 / jnp.sum(p, axis=1, keepdims=True), 0.0)
            w = p * share
            delta = jnp.sum(w * gw, axis=1, keepdims=True)
            weights.append((w.astype(BF), (w * (gw - delta) * scale).astype(BF)))
        results = []
        for (k, v, q, ct), (w_low, gs) in zip(loaded, weights):
            results.append((
                mm(w_low, v, ((1,), (0,))).astype(BF),
                mm(gs, k, ((1,), (0,))).astype(BF),
                mm(gs, q, ((0,), (0,))).astype(BF),
                mm(w_low, ct, ((0,), (0,))).astype(BF),
            ))
        for (ewin, dwin, elo, el, dlo, dl), (ctx, gq, gk, gv) in zip(spots, results):
            d_in = (row_wide >= dlo) & (row_wide < dlo + dl)
            e_in = (row_wide >= elo) & (row_wide < elo + el)
            ctx_s[dwin, :] = jnp.where(d_in, ctx, ctx_s[dwin, :])
            gq_s[dwin, :] = jnp.where(d_in, gq, gq_s[dwin, :])
            gk_s[ewin, :] = jnp.where(e_in, gk, gk_s[ewin, :])
            gv_s[ewin, :] = jnp.where(e_in, gv, gv_s[ewin, :])


def places(me):
    z, y, c, x = me[0], me[1], me[2], me[3]

    def block(ra, rb, rc):
        first = c == 0
        bx = (x + jnp.where(first, ra, rb)) & 3
        by = (y + jnp.where(first, rb, rc)) & 3
        bz = (z + jnp.where(first, rc, ra)) & 3
        return bx, bz * 4 + by

    return block


def main_kernel(weights, extra, meta, me, x_ref, xt_ref, *refs):
    qm, qo, qa, qb, cm, co, ca, cb = refs[weights : weights + 8]
    om, oo, oa, ob, d0, d1, d3, *d2 = refs[weights + 8 + extra : -10]
    k_s, v_s, gk_s, gv_s, q_s, ct_s, ctx_s, gq_s, dw_s, w_s = refs[-10:]
    step = pl.program_id(0)
    block = places(me)

    if weights == 2:
        wk, wv = (ref[...].reshape(D, HEAD_DIM) for ref in refs[:2])
    else:
        w0, w1, w3, *w2 = refs[:weights]

        @pl.when(step == 0)
        def _():
            def take(rc, carry):
                for rb in range(4):
                    far = w2[rb // 2][rb % 2, rc]
                    for ra, value in enumerate((w0[rb, rc], w1[rb, rc], far, w3[rb, rc])):
                        bx, bzy = block(ra, rb, rc)
                        w_s[bx, pl.ds(pl.multiple_of(bzy * 128, 128), 128), :] = value
                return carry

            lax.fori_loop(0, 4, take, 0)

        wk, wv = w_s[step], w_s[2 + step]
    x = x_ref[...]
    k_s[...] = jnp.dot(x, wk, preferred_element_type=jnp.float32).astype(BF)
    v_s[...] = jnp.dot(x, wv, preferred_element_type=jnp.float32).astype(BF)
    for pool, parts in ((q_s, (qm, qo, qa, qb)), (ct_s, (cm, co, ca, cb))):
        pool[0:TOK, :] = parts[0][...]
        pool[TOK:PAIR, :] = parts[1][...]
        pool[PAIR : PAIR + WIN, :] = parts[2][...]
        pool[PAIR + WIN :, :] = parts[3][...]
    attend(meta, k_s, v_s, q_s, ct_s, ctx_s, gq_s, gk_s, gv_s)
    for kind, pool in enumerate((ctx_s, gq_s)):
        om[kind] = pool[0:TOK, :]
        oo[kind] = pool[TOK:PAIR, :]
        oa[kind] = pool[PAIR : PAIR + WIN, :]
        ob[kind] = pool[PAIR + WIN :, :]
    xt = xt_ref[...]
    dw_s[step] = jnp.dot(xt, gk_s[...], preferred_element_type=jnp.float32).astype(BF)
    dw_s[2 + step] = jnp.dot(xt, gv_s[...], preferred_element_type=jnp.float32).astype(BF)

    @pl.when(step == 1)
    def _():
        def put(rc, carry):
            for rb in range(4):
                for ra, out in ((0, d0), (1, d1), (3, d3), (2, d2[rb * len(d2) // 4])):
                    bx, bzy = block(ra, rb, rc)
                    at = rb % (4 // len(d2)) if ra == 2 else rb
                    out[at, rc] = dw_s[bx, pl.ds(pl.multiple_of(bzy * 128, 128), 128), :]
            return carry

        lax.fori_loop(0, 4, put, 0)


def run_main(chunk, meta, me, x, xt, weights, q, ct, given, sent_a, sent_b, before=()):
    def fixed(*shape):
        return pl.BlockSpec(shape, lambda i, m, e: (0,) * len(shape), pipeline_mode=pl.Buffered(1))

    def wide():
        return pl.BlockSpec((TOK, HEAD_DIM), lambda i, m, e: (0, i * 4 + e[2] * 2 + chunk))

    def narrow(rows, kind):
        return pl.BlockSpec((rows, HEAD_DIM), lambda i, m, e: (0, kind * 4 + i * 2 + chunk))

    def gathered(kind):
        return pl.BlockSpec((32, 1, 64, HEAD_DIM), lambda i, m, e: (0, kind * 2 + i, 0, e[2]))

    def handed(kind):
        return pl.BlockSpec((TOK, HEAD_DIM), lambda i, m, e: (0, i * 8 + kind * 2 + chunk))

    def out(rows):
        return pl.BlockSpec((2, rows, HEAD_DIM), lambda i, m, e: (0, 0, i * 2 + chunk))

    def out_far():
        return pl.BlockSpec((2, WIN, HEAD_DIM), lambda i, m, e: (0, 0, i))

    def part(shape):
        return pl.BlockSpec(shape, lambda i, m, e: (0, 0, 0, 0))

    parts = [(4, 4, 128, HEAD_DIM)] * 4 if chunk == 0 else [(4, 4, 128, HEAD_DIM)] * 3 + [(2, 4, 128, HEAD_DIM)] * 2
    anywhere = pl.BlockSpec(memory_space=pl.ANY)
    if len(weights) == 1:
        weights = [*weights, *weights]
        weight_specs = [gathered(0), gathered(1)]
    else:
        weight_specs = [fixed(*w.shape) for w in weights]
    pair = pltpu.VMEM((PAIR, HEAD_DIM), BF)
    pool = pltpu.VMEM((POOL, HEAD_DIM), BF)
    return pl.pallas_call(
        functools.partial(main_kernel, len(weights), len(before)),
        grid_spec=pltpu.PrefetchScalarGridSpec(
            num_scalar_prefetch=2,
            grid=(2,),
            in_specs=[fixed(PAIR, D), fixed(D, PAIR), *weight_specs,
                      wide(), handed(0), narrow(WIN, 0), narrow(WIN, 0),
                      wide(), handed(1), narrow(WIN, 1), narrow(WIN, 1)]
            + [anywhere] * len(before),
            out_specs=[out(TOK), out(TOK), out_far(), out_far(), *[part(shape) for shape in parts]],
            scratch_shapes=[pair, pair, pair, pair, pool, pool, pool, pool,
                            pltpu.VMEM((4, D, HEAD_DIM), BF), pltpu.VMEM((4, D, HEAD_DIM), BF)],
        ),
        out_shape=[jax.ShapeDtypeStruct((2, TOK, 2 * HALF), BF)] * 2
        + [jax.ShapeDtypeStruct((2, WIN, HALF), BF)] * 2
        + [jax.ShapeDtypeStruct(shape, BF) for shape in parts],
        input_output_aliases={12 + len(weights) + n: n for n in range(len(before))},
        compiler_params=pltpu.CompilerParams(vmem_limit_bytes=44 * MIB),
        cost_estimate=pl.CostEstimate(flops=12_000_000_000, bytes_accessed=24_000_000, transcendentals=500_000),
    )(meta, me, x, xt, *weights, q, given, sent_a, sent_b, ct, given, sent_a, sent_b, *before)


def add(refs):
    return sum(ref[...].astype(jnp.float32) for ref in refs)


def add_kernel(count, *refs):
    total = add(refs[:count]).astype(BF)
    for n, out in enumerate(refs[-4:]):
        out[...] = total[n]


def add_parts(parts, after):
    return pl.pallas_call(
        functools.partial(add_kernel, len(parts)),
        grid=(4,),
        in_specs=[pl.BlockSpec((4, 1, 128, HEAD_DIM), lambda i: (0, i, 0, 0))] * len(parts)
        + [pl.BlockSpec(memory_space=pl.ANY)] * len(after),
        out_specs=[pl.BlockSpec((1, 128, HEAD_DIM), lambda i: (i, 0, 0))] * 4,
        out_shape=[jax.ShapeDtypeStruct((4, 128, HEAD_DIM), BF)] * 4,
        compiler_params=pltpu.CompilerParams(vmem_limit_bytes=16 * MIB),
    )(*parts, *after)


def add_both_kernel(*refs):
    for chunk in range(2):
        total = add(refs[chunk * 4 : chunk * 4 + 4]).astype(BF)
        for n, out in enumerate(refs[8:]):
            out[:, chunk * HEAD_DIM : (chunk + 1) * HEAD_DIM] = total[n]


def add_both(first, second):
    whole = pl.BlockSpec(memory_space=pltpu.VMEM)
    return pl.pallas_call(
        add_both_kernel,
        in_specs=[whole] * 8,
        out_specs=[whole] * 4,
        out_shape=[jax.ShapeDtypeStruct((128, HALF), BF)] * 4,
        compiler_params=pltpu.CompilerParams(vmem_limit_bytes=16 * MIB),
    )(*first, *second)


def add_last_kernel(me, *refs):
    kept, given = refs[-2:]
    for row, out in ((me[2], kept), (1 - me[2], given)):
        rows = pl.ds(pl.multiple_of(row * 64, 64), 64)
        out[...] = sum(ref[rows, :].astype(jnp.float32) for ref in refs[:4])


def add_last(me, parts, after):
    whole = pl.BlockSpec(memory_space=pltpu.VMEM)
    return pl.pallas_call(
        add_last_kernel,
        in_specs=[pl.BlockSpec(memory_space=pltpu.SMEM)] + [whole] * 4
        + [pl.BlockSpec(memory_space=pl.ANY)] * len(after),
        out_specs=[whole] * 2,
        out_shape=[jax.ShapeDtypeStruct((64, HALF), jnp.float32)] * 2,
        compiler_params=pltpu.CompilerParams(vmem_limit_bytes=16 * MIB),
    )(me, *parts, *after)


def depart_kernel(me, enc_len, dec_len, partner, q_ref, ct_ref, meta, info, a_ref, b_ref, sems):
    core, x = me[2], me[3]
    t = me[0] * 4 + me[1]

    info[0], info[1], info[2], info[3] = jnp.int32(0), core, jnp.int32(0), jnp.int32(0)
    device = (t * 2 + core) * 4 + x
    start = jnp.int32(0)
    for slot in range(SEGS):
        begin, length = start, dec_len[slot, device]

        @pl.when((partner[slot, device] >> 5) != t)
        def _():
            info[0] = align(begin, TOK)
            info[2] = begin
            info[3] = length

        start = start + length

    rows = pl.ds(pl.multiple_of(info[0], 16), WIN)
    copies = []
    for n in range(4):
        source = (q_ref, ct_ref)[n // 2]
        for side, out in ((core, a_ref), (1 - core, b_ref)):
            begin = pl.ds(pl.multiple_of((n % 2) * 1024 + side * HALF, HALF), HALF)
            copies.append((source.at[rows, begin], out.at[:, pl.ds(n * HALF, HALF)]))
    copies = [pltpu.make_async_copy(a, b, sems.at[n]) for n, (a, b) in enumerate(copies)]
    for copy in copies:
        copy.start()

    for side in range(2):
        device = (t * 2 + (core if side == 0 else 1 - core)) * 4 + x
        start = jnp.int32(side * TOK)
        for slot in range(SEGS):
            meta[side * SEGS + slot, 0] = start
            meta[side * SEGS + slot, 1] = enc_len[slot, device]
            start = start + enc_len[slot, device]
    for near in range(4):
        dp = t * 2 - 1 + near
        device = jnp.clip(dp, 0, 31) * 4 + x
        real = (dp >= 0) & (dp < 32)
        same = (dp & 1) == core
        start = jnp.int32(0)
        for slot in range(SEGS):
            begin, length = start, dec_len[slot, device]
            owner = partner[slot, device] >> 4
            if near in (1, 2):
                at = begin + jnp.where(same, 0, TOK)
            else:
                at = begin - align(begin, TOK) + PAIR + jnp.where(same, 0, WIN)

            @pl.when(real & ((owner >> 1) == t))
            def _():
                entry = jnp.where((owner & 1) == core, 0, SEGS) + (partner[slot, device] & 3)
                meta[entry, 2] = at
                meta[entry, 3] = length

            start = start + length
    for copy in copies:
        copy.wait()


def depart(me, enc_lengths, dec_lengths, dec_partner, q, ct):
    whole = pl.BlockSpec(memory_space=pl.ANY)
    scalar = pl.BlockSpec(memory_space=pltpu.SMEM)
    return pl.pallas_call(
        depart_kernel,
        in_specs=[scalar, scalar, scalar, scalar, whole, whole],
        out_specs=[scalar, scalar, pl.BlockSpec(memory_space=pltpu.VMEM), pl.BlockSpec(memory_space=pltpu.VMEM)],
        scratch_shapes=[pltpu.SemaphoreType.DMA((8,))],
        out_shape=[jax.ShapeDtypeStruct((2 * SEGS, 4), jnp.int32), jax.ShapeDtypeStruct((4,), jnp.int32)]
        + [jax.ShapeDtypeStruct((WIN, 2048), BF)] * 2,
        compiler_params=pltpu.CompilerParams(vmem_limit_bytes=59 * MIB),
    )(me, enc_lengths.T, dec_lengths.T, dec_partner.T, q, ct)


def hand_kernel(me, q_ref, ct_ref, x_ref, *refs):
    refs[-1][:, :HALF] = q_ref[...]
    refs[-1][:, HALF : 2 * HALF] = ct_ref[...]
    refs[-1][:, 2 * HALF :] = x_ref[...]


def hand(me, q, ct, x, after):
    def half(i, me):
        return (0, i * 2 + 1 - me[2])

    part = pl.BlockSpec((TOK, HALF), half)
    return pl.pallas_call(
        hand_kernel,
        grid_spec=pltpu.PrefetchScalarGridSpec(
            num_scalar_prefetch=1,
            grid=(2,),
            in_specs=[part, part, pl.BlockSpec((TOK, 2 * HALF), lambda i, me: (0, i))]
            + [pl.BlockSpec(memory_space=pl.ANY)] * len(after),
            out_specs=pl.BlockSpec((TOK, 4 * HALF), lambda i, me: (0, i)),
        ),
        out_shape=jax.ShapeDtypeStruct((TOK, 4096), BF),
        compiler_params=pltpu.CompilerParams(vmem_limit_bytes=24 * MIB),
    )(me, q, ct, x, *after)


def turn_kernel(a_ref, b_ref, *refs):
    x_ref, xt_ref = refs[-2:]
    for n, ref in enumerate((a_ref, b_ref)):
        value = ref[...]
        x_ref[n * TOK : (n + 1) * TOK, :] = value
        xt_ref[:, n * TOK : (n + 1) * TOK] = value.T


def turn(a, b, after):
    part = pl.BlockSpec((TOK, 512), lambda i: (0, i))
    return pl.pallas_call(
        turn_kernel,
        grid=(D // 512,),
        in_specs=[part, pl.BlockSpec((TOK, 512), lambda i: (0, i + 2 + 2 * (i // 2)))]
        + [pl.BlockSpec(memory_space=pl.ANY)] * len(after),
        out_specs=[pl.BlockSpec((PAIR, 512), lambda i: (0, i)), pl.BlockSpec((512, PAIR), lambda i: (i, 0))],
        out_shape=[jax.ShapeDtypeStruct((PAIR, D), BF), jax.ShapeDtypeStruct((D, PAIR), BF)],
        compiler_params=pltpu.CompilerParams(vmem_limit_bytes=16 * MIB),
    )(a, b, *after)


def finish_kernel(info, *refs):
    ins, outs = refs[:6], refs[6:]
    win = pl.multiple_of(info[0], 16)
    core, start, length = info[1], info[2] - info[0], info[3]
    rows = pl.ds(win, WIN)
    place = lax.broadcasted_iota(jnp.int32, (WIN, HEAD_DIM), 0)
    inside = (place >= start) & (place < start + length)
    mine, theirs, *returned = ins
    for side, base, first in ((core, mine, 0), (1 - core, theirs, 1)):
        for chunk in range(2):
            cols = pl.ds(pl.multiple_of(side * HALF + chunk * HEAD_DIM, HEAD_DIM), HEAD_DIM)
            for kind, out in enumerate(outs):
                out[:, cols] = base[kind, :, chunk * HEAD_DIM : (chunk + 1) * HEAD_DIM]
                out[rows, cols] = jnp.where(inside, returned[chunk * 2 + first][kind], out[rows, cols])


def finish(info, pieces):
    def source(rows, cols):
        return pl.BlockSpec((2, rows, cols), lambda i, e: (0, 0, i))

    out = pl.BlockSpec((TOK, 1024), lambda i, e: (0, i))
    return pl.pallas_call(
        finish_kernel,
        grid_spec=pltpu.PrefetchScalarGridSpec(
            num_scalar_prefetch=1,
            grid=(2,),
            in_specs=[source(TOK, HALF)] * 2 + [source(WIN, HEAD_DIM)] * 4,
            out_specs=[out, out],
        ),
        out_shape=[jax.ShapeDtypeStruct((TOK, 2048), BF)] * 2,
        compiler_params=pltpu.CompilerParams(vmem_limit_bytes=32 * MIB),
    )(info, *pieces)


def swap(value):
    return lax.ppermute(value, "c", [(0, 1), (1, 0)])


SEND_A = [(2 * t, 2 * t - 2) for t in range(1, 16)] + [(2 * t + 1, 2 * t + 3) for t in range(15)]
SEND_B = [(2 * t, 2 * t - 1) for t in range(1, 16)] + [(2 * t + 1, 2 * t + 2) for t in range(15)]


def back(pairs):
    return [(b, a) for a, b in pairs]


def shift(phase, amount):
    pairs = []
    for z in range(4):
        for y in range(4):
            for c in range(2):
                for x in range(4):
                    to = {"z": z, "y": y, "x": x}
                    axis = ("xyz", "zxy")[c][phase]
                    to[axis] = (to[axis] + amount) % 4
                    pairs.append((((z * 4 + y) * 2 + c) * 4 + x, ((to["z"] * 4 + to["y"]) * 2 + c) * 4 + to["x"]))
    return pairs


def exchange(parts, phase):
    return [parts[0]] + [lax.ppermute(parts[r], ALL, shift(phase, r)) for r in (1, 3, 2)]


def join_kernel(*refs):
    for n in range(4):
        refs[-1][n] = refs[n][...]


def join(parts, after):
    whole = pl.BlockSpec(memory_space=pltpu.VMEM)
    return pl.pallas_call(
        join_kernel,
        in_specs=[whole] * 4 + [pl.BlockSpec(memory_space=pl.ANY)] * len(after),
        out_specs=whole,
        out_shape=jax.ShapeDtypeStruct((4,) + parts[0].shape, BF),
        compiler_params=pltpu.CompilerParams(vmem_limit_bytes=16 * MIB),
    )(*parts, *after)


def pick_kernel(me, w_ref, got_ref, after, out_ref):
    mine = w_ref[:, pl.ds(pl.multiple_of(me[2] * HALF, HALF), HEAD_DIM)]
    for core in range(2):

        @pl.when(me[2] == core)
        def _():
            out_ref[core * 64 : core * 64 + 64, :] = mine
            out_ref[64 - core * 64 : 128 - core * 64, :] = got_ref[...]


def pick(me, weights, got, after):
    whole = pl.BlockSpec(memory_space=pltpu.VMEM)
    return pl.pallas_call(
        pick_kernel,
        in_specs=[pl.BlockSpec(memory_space=pltpu.SMEM), whole, whole, pl.BlockSpec(memory_space=pl.ANY)],
        out_specs=whole,
        out_shape=jax.ShapeDtypeStruct((128, HEAD_DIM), BF),
        compiler_params=pltpu.CompilerParams(vmem_limit_bytes=16 * MIB),
    )(me, weights, got, after)


def ring(value, phase, amount):
    return lax.ppermute(value, ALL, shift(phase, -amount))


def fold_kernel(a_ref, b_ref, got_a, got_b, after, out_a, out_b):
    for ref, got, out in ((a_ref, got_a, out_a), (b_ref, got_b, out_b)):
        out[...] = (ref[...].astype(jnp.float32) + got[...].astype(jnp.float32)).astype(BF)


def fold(ahead, behind, got_a, got_b, after):
    def block(start):
        return pl.BlockSpec((1, 4, 128, HEAD_DIM), lambda i: (i + start, 0, 0, 0))

    whole = jax.ShapeDtypeStruct(ahead.shape, BF)
    return pl.pallas_call(
        fold_kernel,
        grid=(2,),
        in_specs=[block(0), block(2), block(0), block(0), pl.BlockSpec(memory_space=pl.ANY)],
        out_specs=[block(0), block(2)],
        out_shape=[whole, whole],
        input_output_aliases={0: 0, 1: 1},
        compiler_params=pltpu.CompilerParams(vmem_limit_bytes=16 * MIB),
    )(ahead, behind, got_a, got_b, after)


def scatter_ring(own, ahead, behind, far_a, far_b, after):
    got_a = lax.ppermute(far_a, ALL, shift(0, 1))
    got_b = lax.ppermute(far_b, ALL, shift(0, -1))
    ahead, behind = fold(ahead, behind, got_a, got_b, after)
    return [own, lax.ppermute(ahead, ALL, shift(0, 1)), lax.ppermute(behind, ALL, shift(0, -1))]


def body(enc_hidden, kv_weights, queries, cotangent, enc_lengths, dec_lengths, dec_partner):
    z, y, c, x = (lax.axis_index(a) for a in ALL)
    me = jnp.stack([z, y, c, x]).astype(jnp.int32)
    cols = [kv_weights[:, n * HEAD_DIM : (n + 1) * HEAD_DIM] for n in range(4)]
    later = lax.all_gather(jnp.concatenate([cols[1], cols[3]], axis=1), ALL, axis=0).reshape(32, 4, 64, HALF)

    meta, info, leave_a, leave_b = depart(me, enc_lengths, dec_lengths, dec_partner, queries, cotangent)
    sent_a = lax.ppermute(leave_a, DP, SEND_A)
    sent_b = lax.ppermute(leave_b, DP, SEND_B)

    got = swap(jnp.where(c == 0, cols[2], cols[0]))
    own = pick(me, kv_weights, got, leave_a)
    first = [own] + [ring(own, 2, n) for n in (1, 2, 3)]
    handed = hand(me, queries, cotangent, enc_hidden, first[1:])
    given = swap(handed)
    part = join(first, [handed, sent_a, sent_b])
    part = join([part] + [ring(part, 1, n) for n in (1, 2, 3)], [])
    tokens, tokens_t = turn(enc_hidden, given, [part])
    ahead, behind = ring(part, 0, 1), ring(part, 0, -1)
    weights = [[part, ahead, behind, ring(behind[:2], 0, -1), ring(ahead[2:], 0, 1)], [later]]

    shared = (meta, me, tokens, tokens_t)
    inputs = (queries, cotangent, given, sent_a, sent_b)
    home = [back(SEND_A), back(SEND_B)]

    *results, d0, d1, d3, d2 = run_main(0, *shared, weights[0], *inputs)
    returned = [lax.ppermute(part, DP, pairs) for part, pairs in zip(results[2:], home)]
    parts = exchange([d0, d1, d2, d3], 0)
    *results, d0, d1, d3, far_a, far_b = run_main(1, *shared, weights[1], *inputs, before=results[:2])
    mine, other = results[:2]
    late = [lax.ppermute(part, DP, pairs) for part, pairs in zip(results[2:], home)]

    first = add_parts(parts, [mine, *returned])
    parts = scatter_ring(d0, d1, d3, far_a, far_b, first[0])
    first = exchange(first, 1)
    second = exchange(add_parts(parts, late), 1)
    context, grad_queries = finish(info, [mine, swap(other), *returned, *late])
    kept, given = add_last(me, exchange(add_both(first, second), 2), [context])
    got = swap(given)
    grad = jnp.concatenate([jnp.where(c == 0, kept, got), jnp.where(c == 0, got, kept)], axis=1)
    return context, grad_queries, grad


def solution(mesh):
    fine = Mesh(mesh.devices.reshape(4, 4, 2, 4), ALL)
    rows = P(ALL, None)
    cut = P(DP, "x")
    return jax.shard_map(
        body,
        mesh=fine,
        in_specs=(rows, cut, rows, rows, P(), P(), P()),
        out_specs=(rows, rows, cut),
        check_vma=False,
    )
```

```python
import functools

import jax
import jax.numpy as jnp
from jax import lax
from jax.experimental import pallas as pl
from jax.experimental.pallas import tpu as pltpu
from jax.sharding import Mesh, PartitionSpec as P

HEAD_DIM = 256
SEGS = 4
TOK = 512
PAIR = 2 * TOK
WIN = 176
POOL = PAIR + 2 * WIN
D = 2048
HALF = 512
GROUP = 4
DP = ("z", "y", "c")
ALL = ("z", "y", "c", "x")
MIB = 1024 * 1024
BF = jnp.bfloat16


def align(start, limit):
    return jnp.minimum((start // 16) * 16, limit - WIN)


def mm(a, b, dims):
    return lax.dot_general(a, b, (dims, ((), ())), preferred_element_type=jnp.float32)


def attend(meta, k_s, v_s, q_s, ct_s, ctx_s, gq_s, gk_s, gv_s):
    scale = HEAD_DIM ** -0.5
    col = lax.broadcasted_iota(jnp.int32, (WIN, WIN), 1)
    row = lax.broadcasted_iota(jnp.int32, (WIN, WIN), 0)
    row_wide = lax.broadcasted_iota(jnp.int32, (WIN, HEAD_DIM), 0)
    for first in range(0, 2 * SEGS, GROUP):
        spots, loaded, scores = [], [], []
        for e in range(first, first + GROUP):
            es, el, ds, dl = meta[e, 0], meta[e, 1], meta[e, 2], meta[e, 3]
            ew = pl.multiple_of(align(es, PAIR), 16)
            dw = pl.multiple_of(align(ds, POOL), 16)
            spots.append((pl.ds(ew, WIN), pl.ds(dw, WIN), es - ew, el, ds - dw, dl))
        for ewin, dwin, *_ in spots:
            k, v, q, ct = k_s[ewin, :], v_s[ewin, :], q_s[dwin, :], ct_s[dwin, :]
            loaded.append((k, v, q, ct))
            scores.append((mm(q, k, ((1,), (1,))), mm(ct, v, ((1,), (1,)))))
        weights = []
        for (_, _, elo, el, dlo, dl), (s, gw) in zip(spots, scores):
            k_live = (col >= elo) & (col < elo + el)
            q_live = (row[:, :1] >= dlo) & (row[:, :1] < dlo + dl)
            s = jnp.where(k_live, s * scale, -jnp.inf)
            p = jnp.exp(s - jnp.max(s, axis=1, keepdims=True))
            share = jnp.where(q_live, 1.0 / jnp.sum(p, axis=1, keepdims=True), 0.0)
            w = p * share
            delta = jnp.sum(w * gw, axis=1, keepdims=True)
            weights.append((w.astype(BF), (w * (gw - delta) * scale).astype(BF)))
        results = []
        for (k, v, q, ct), (w_low, gs) in zip(loaded, weights):
            results.append((
                mm(w_low, v, ((1,), (0,))).astype(BF),
                mm(gs, k, ((1,), (0,))).astype(BF),
                mm(gs, q, ((0,), (0,))).astype(BF),
                mm(w_low, ct, ((0,), (0,))).astype(BF),
            ))
        for (ewin, dwin, elo, el, dlo, dl), (ctx, gq, gk, gv) in zip(spots, results):
            d_in = (row_wide >= dlo) & (row_wide < dlo + dl)
            e_in = (row_wide >= elo) & (row_wide < elo + el)
            ctx_s[dwin, :] = jnp.where(d_in, ctx, ctx_s[dwin, :])
            gq_s[dwin, :] = jnp.where(d_in, gq, gq_s[dwin, :])
            gk_s[ewin, :] = jnp.where(e_in, gk, gk_s[ewin, :])
            gv_s[ewin, :] = jnp.where(e_in, gv, gv_s[ewin, :])


def places(me):
    z, y, c, x = me[0], me[1], me[2], me[3]

    def block(ra, rb, rc):
        first = c == 0
        bx = (x + jnp.where(first, ra, rb)) & 3
        by = (y + jnp.where(first, rb, rc)) & 3
        bz = (z + jnp.where(first, rc, ra)) & 3
        return bx, bz * 4 + by

    return block


def main_kernel(weights, extra, meta, me, x_ref, xt_ref, *refs):
    qm, qo, qa, qb, cm, co, ca, cb = refs[weights : weights + 8]
    om, oo, oa, ob, d0, d1, d3, *d2 = refs[weights + 8 + extra : -10]
    k_s, v_s, gk_s, gv_s, q_s, ct_s, ctx_s, gq_s, dw_s, w_s = refs[-10:]
    step = pl.program_id(0)
    block = places(me)

    w0, w1, w3, *w2 = refs[:weights]

    @pl.when(step == 0)
    def _():
        def take(rc, carry):
            for rb in range(4):
                far = w2[rb * len(w2) // 4][rb % (4 // len(w2)), rc]
                for ra, value in enumerate((w0[rb, rc], w1[rb, rc], far, w3[rb, rc])):
                    bx, bzy = block(ra, rb, rc)
                    w_s[bx, pl.ds(pl.multiple_of(bzy * 128, 128), 128), :] = value
            return carry

        lax.fori_loop(0, 4, take, 0)

    x = x_ref[...]
    k_s[...] = jnp.dot(x, w_s[step], preferred_element_type=jnp.float32).astype(BF)
    v_s[...] = jnp.dot(x, w_s[2 + step], preferred_element_type=jnp.float32).astype(BF)
    for pool, parts in ((q_s, (qm, qo, qa, qb)), (ct_s, (cm, co, ca, cb))):
        pool[0:TOK, :] = parts[0][...]
        pool[TOK:PAIR, :] = parts[1][...]
        pool[PAIR : PAIR + WIN, :] = parts[2][...]
        pool[PAIR + WIN :, :] = parts[3][...]
    attend(meta, k_s, v_s, q_s, ct_s, ctx_s, gq_s, gk_s, gv_s)
    for kind, pool in enumerate((ctx_s, gq_s)):
        om[kind] = pool[0:TOK, :]
        oo[kind] = pool[TOK:PAIR, :]
        oa[kind] = pool[PAIR : PAIR + WIN, :]
        ob[kind] = pool[PAIR + WIN :, :]
    xt = xt_ref[...]
    dw_s[step] = jnp.dot(xt, gk_s[...], preferred_element_type=jnp.float32).astype(BF)
    dw_s[2 + step] = jnp.dot(xt, gv_s[...], preferred_element_type=jnp.float32).astype(BF)

    @pl.when(step == 1)
    def _():
        def put(rc, carry):
            for rb in range(4):
                for ra, out in ((0, d0), (1, d1), (3, d3), (2, d2[rb * len(d2) // 4])):
                    bx, bzy = block(ra, rb, rc)
                    at = rb % (4 // len(d2)) if ra == 2 else rb
                    out[at, rc] = dw_s[bx, pl.ds(pl.multiple_of(bzy * 128, 128), 128), :]
            return carry

        lax.fori_loop(0, 4, put, 0)


def run_main(chunk, meta, me, x, xt, weights, q, ct, given, sent_a, sent_b, before=()):
    def fixed(*shape):
        return pl.BlockSpec(shape, lambda i, m, e: (0,) * len(shape), pipeline_mode=pl.Buffered(1))

    def wide():
        return pl.BlockSpec((TOK, HEAD_DIM), lambda i, m, e: (0, i * 4 + e[2] * 2 + chunk))

    def narrow(rows, kind):
        return pl.BlockSpec((rows, HEAD_DIM), lambda i, m, e: (0, kind * 4 + i * 2 + chunk))

    def handed(kind):
        return pl.BlockSpec((TOK, HEAD_DIM), lambda i, m, e: (0, i * 8 + kind * 2 + chunk))

    def out(rows):
        return pl.BlockSpec((2, rows, HEAD_DIM), lambda i, m, e: (0, 0, i * 2 + chunk))

    def out_far():
        return pl.BlockSpec((2, WIN, HEAD_DIM), lambda i, m, e: (0, 0, i))

    def part(shape):
        return pl.BlockSpec(shape, lambda i, m, e: (0, 0, 0, 0))

    parts = [(4, 4, 128, HEAD_DIM)] * 4 if chunk == 0 else [(4, 4, 128, HEAD_DIM)] * 3 + [(2, 4, 128, HEAD_DIM)] * 2
    anywhere = pl.BlockSpec(memory_space=pl.ANY)
    pair = pltpu.VMEM((PAIR, HEAD_DIM), BF)
    pool = pltpu.VMEM((POOL, HEAD_DIM), BF)
    return pl.pallas_call(
        functools.partial(main_kernel, len(weights), len(before)),
        grid_spec=pltpu.PrefetchScalarGridSpec(
            num_scalar_prefetch=2,
            grid=(2,),
            in_specs=[fixed(PAIR, D), fixed(D, PAIR), *[fixed(*w.shape) for w in weights],
                      wide(), handed(0), narrow(WIN, 0), narrow(WIN, 0),
                      wide(), handed(1), narrow(WIN, 1), narrow(WIN, 1)]
            + [anywhere] * len(before),
            out_specs=[out(TOK), out(TOK), out_far(), out_far(), *[part(shape) for shape in parts]],
            scratch_shapes=[pair, pair, pair, pair, pool, pool, pool, pool,
                            pltpu.VMEM((4, D, HEAD_DIM), BF), pltpu.VMEM((4, D, HEAD_DIM), BF)],
        ),
        out_shape=[jax.ShapeDtypeStruct((2, TOK, 2 * HALF), BF)] * 2
        + [jax.ShapeDtypeStruct((2, WIN, HALF), BF)] * 2
        + [jax.ShapeDtypeStruct(shape, BF) for shape in parts],
        input_output_aliases={12 + len(weights) + n: n for n in range(len(before))},
        compiler_params=pltpu.CompilerParams(vmem_limit_bytes=44 * MIB),
        cost_estimate=pl.CostEstimate(flops=12_000_000_000, bytes_accessed=24_000_000, transcendentals=500_000),
    )(meta, me, x, xt, *weights, q, given, sent_a, sent_b, ct, given, sent_a, sent_b, *before)


def add(refs):
    return sum(ref[...].astype(jnp.float32) for ref in refs)


def add_kernel(count, *refs):
    total = add(refs[:count]).astype(BF)
    for n, out in enumerate(refs[-4:]):
        out[...] = total[n]


def add_parts(parts, after):
    return pl.pallas_call(
        functools.partial(add_kernel, len(parts)),
        grid=(4,),
        in_specs=[pl.BlockSpec((4, 1, 128, HEAD_DIM), lambda i: (0, i, 0, 0))] * len(parts)
        + [pl.BlockSpec(memory_space=pl.ANY)] * len(after),
        out_specs=[pl.BlockSpec((1, 128, HEAD_DIM), lambda i: (i, 0, 0))] * 4,
        out_shape=[jax.ShapeDtypeStruct((4, 128, HEAD_DIM), BF)] * 4,
        compiler_params=pltpu.CompilerParams(vmem_limit_bytes=16 * MIB),
    )(*parts, *after)


def add_both_kernel(*refs):
    for chunk in range(2):
        total = add(refs[chunk * 4 : chunk * 4 + 4]).astype(BF)
        for n, out in enumerate(refs[8:]):
            out[:, chunk * HEAD_DIM : (chunk + 1) * HEAD_DIM] = total[n]


def add_both(first, second):
    whole = pl.BlockSpec(memory_space=pltpu.VMEM)
    return pl.pallas_call(
        add_both_kernel,
        in_specs=[whole] * 8,
        out_specs=[whole] * 4,
        out_shape=[jax.ShapeDtypeStruct((128, HALF), BF)] * 4,
        compiler_params=pltpu.CompilerParams(vmem_limit_bytes=16 * MIB),
    )(*first, *second)


def add_last_kernel(me, *refs):
    kept, given = refs[-2:]
    for row, out in ((me[2], kept), (1 - me[2], given)):
        rows = pl.ds(pl.multiple_of(row * 64, 64), 64)
        out[...] = sum(ref[rows, :].astype(jnp.float32) for ref in refs[:4])


def add_last(me, parts, after):
    whole = pl.BlockSpec(memory_space=pltpu.VMEM)
    return pl.pallas_call(
        add_last_kernel,
        in_specs=[pl.BlockSpec(memory_space=pltpu.SMEM)] + [whole] * 4
        + [pl.BlockSpec(memory_space=pl.ANY)] * len(after),
        out_specs=[whole] * 2,
        out_shape=[jax.ShapeDtypeStruct((64, HALF), jnp.float32)] * 2,
        compiler_params=pltpu.CompilerParams(vmem_limit_bytes=16 * MIB),
    )(me, *parts, *after)


def depart_kernel(me, enc_len, dec_len, partner, q_ref, ct_ref, meta, info, a_ref, b_ref, sems):
    core, x = me[2], me[3]
    t = me[0] * 4 + me[1]

    info[0], info[1], info[2], info[3] = jnp.int32(0), core, jnp.int32(0), jnp.int32(0)
    device = (t * 2 + core) * 4 + x
    start = jnp.int32(0)
    for slot in range(SEGS):
        begin, length = start, dec_len[slot, device]

        @pl.when((partner[slot, device] >> 5) != t)
        def _():
            info[0] = align(begin, TOK)
            info[2] = begin
            info[3] = length

        start = start + length

    rows = pl.ds(pl.multiple_of(info[0], 16), WIN)
    copies = []
    for n in range(4):
        source = (q_ref, ct_ref)[n // 2]
        for side, out in ((core, a_ref), (1 - core, b_ref)):
            begin = pl.ds(pl.multiple_of((n % 2) * 1024 + side * HALF, HALF), HALF)
            copies.append((source.at[rows, begin], out.at[:, pl.ds(n * HALF, HALF)]))
    copies = [pltpu.make_async_copy(a, b, sems.at[n]) for n, (a, b) in enumerate(copies)]
    for copy in copies:
        copy.start()

    for side in range(2):
        device = (t * 2 + (core if side == 0 else 1 - core)) * 4 + x
        start = jnp.int32(side * TOK)
        for slot in range(SEGS):
            meta[side * SEGS + slot, 0] = start
            meta[side * SEGS + slot, 1] = enc_len[slot, device]
            start = start + enc_len[slot, device]
    for near in range(4):
        dp = t * 2 - 1 + near
        device = jnp.clip(dp, 0, 31) * 4 + x
        real = (dp >= 0) & (dp < 32)
        same = (dp & 1) == core
        start = jnp.int32(0)
        for slot in range(SEGS):
            begin, length = start, dec_len[slot, device]
            owner = partner[slot, device] >> 4
            if near in (1, 2):
                at = begin + jnp.where(same, 0, TOK)
            else:
                at = begin - align(begin, TOK) + PAIR + jnp.where(same, 0, WIN)

            @pl.when(real & ((owner >> 1) == t))
            def _():
                entry = jnp.where((owner & 1) == core, 0, SEGS) + (partner[slot, device] & 3)
                meta[entry, 2] = at
                meta[entry, 3] = length

            start = start + length
    for copy in copies:
        copy.wait()


def depart(me, enc_lengths, dec_lengths, dec_partner, q, ct):
    whole = pl.BlockSpec(memory_space=pl.ANY)
    scalar = pl.BlockSpec(memory_space=pltpu.SMEM)
    return pl.pallas_call(
        depart_kernel,
        in_specs=[scalar, scalar, scalar, scalar, whole, whole],
        out_specs=[scalar, scalar, pl.BlockSpec(memory_space=pltpu.VMEM), pl.BlockSpec(memory_space=pltpu.VMEM)],
        scratch_shapes=[pltpu.SemaphoreType.DMA((8,))],
        out_shape=[jax.ShapeDtypeStruct((2 * SEGS, 4), jnp.int32), jax.ShapeDtypeStruct((4,), jnp.int32)]
        + [jax.ShapeDtypeStruct((WIN, 2048), BF)] * 2,
        compiler_params=pltpu.CompilerParams(vmem_limit_bytes=59 * MIB),
    )(me, enc_lengths.T, dec_lengths.T, dec_partner.T, q, ct)


def hand_kernel(me, q_ref, ct_ref, x_ref, *refs):
    refs[-1][:, :HALF] = q_ref[...]
    refs[-1][:, HALF : 2 * HALF] = ct_ref[...]
    refs[-1][:, 2 * HALF :] = x_ref[...]


def hand(me, q, ct, x, after):
    def half(i, me):
        return (0, i * 2 + 1 - me[2])

    part = pl.BlockSpec((TOK, HALF), half)
    return pl.pallas_call(
        hand_kernel,
        grid_spec=pltpu.PrefetchScalarGridSpec(
            num_scalar_prefetch=1,
            grid=(2,),
            in_specs=[part, part, pl.BlockSpec((TOK, 2 * HALF), lambda i, me: (0, i))]
            + [pl.BlockSpec(memory_space=pl.ANY)] * len(after),
            out_specs=pl.BlockSpec((TOK, 4 * HALF), lambda i, me: (0, i)),
        ),
        out_shape=jax.ShapeDtypeStruct((TOK, 4096), BF),
        compiler_params=pltpu.CompilerParams(vmem_limit_bytes=24 * MIB),
    )(me, q, ct, x, *after)


def turn_kernel(a_ref, b_ref, *refs):
    x_ref, xt_ref = refs[-2:]
    for n, ref in enumerate((a_ref, b_ref)):
        value = ref[...]
        x_ref[n * TOK : (n + 1) * TOK, :] = value
        xt_ref[:, n * TOK : (n + 1) * TOK] = value.T


def turn(a, b, after):
    part = pl.BlockSpec((TOK, 512), lambda i: (0, i))
    return pl.pallas_call(
        turn_kernel,
        grid=(D // 512,),
        in_specs=[part, pl.BlockSpec((TOK, 512), lambda i: (0, i + 2 + 2 * (i // 2)))]
        + [pl.BlockSpec(memory_space=pl.ANY)] * len(after),
        out_specs=[pl.BlockSpec((PAIR, 512), lambda i: (0, i)), pl.BlockSpec((512, PAIR), lambda i: (i, 0))],
        out_shape=[jax.ShapeDtypeStruct((PAIR, D), BF), jax.ShapeDtypeStruct((D, PAIR), BF)],
        compiler_params=pltpu.CompilerParams(vmem_limit_bytes=16 * MIB),
    )(a, b, *after)


def finish_kernel(info, *refs):
    ins, outs = refs[:6], refs[6:]
    win = pl.multiple_of(info[0], 16)
    core, start, length = info[1], info[2] - info[0], info[3]
    rows = pl.ds(win, WIN)
    place = lax.broadcasted_iota(jnp.int32, (WIN, HEAD_DIM), 0)
    inside = (place >= start) & (place < start + length)
    mine, theirs, *returned = ins
    for side, base, first in ((core, mine, 0), (1 - core, theirs, 1)):
        for chunk in range(2):
            cols = pl.ds(pl.multiple_of(side * HALF + chunk * HEAD_DIM, HEAD_DIM), HEAD_DIM)
            for kind, out in enumerate(outs):
                out[:, cols] = base[kind, :, chunk * HEAD_DIM : (chunk + 1) * HEAD_DIM]
                out[rows, cols] = jnp.where(inside, returned[chunk * 2 + first][kind], out[rows, cols])


def finish(info, pieces):
    def source(rows, cols):
        return pl.BlockSpec((2, rows, cols), lambda i, e: (0, 0, i))

    out = pl.BlockSpec((TOK, 1024), lambda i, e: (0, i))
    return pl.pallas_call(
        finish_kernel,
        grid_spec=pltpu.PrefetchScalarGridSpec(
            num_scalar_prefetch=1,
            grid=(2,),
            in_specs=[source(TOK, HALF)] * 2 + [source(WIN, HEAD_DIM)] * 4,
            out_specs=[out, out],
        ),
        out_shape=[jax.ShapeDtypeStruct((TOK, 2048), BF)] * 2,
        compiler_params=pltpu.CompilerParams(vmem_limit_bytes=32 * MIB),
    )(info, *pieces)


def swap(value):
    return lax.ppermute(value, "c", [(0, 1), (1, 0)])


SEND_A = [(2 * t, 2 * t - 2) for t in range(1, 16)] + [(2 * t + 1, 2 * t + 3) for t in range(15)]
SEND_B = [(2 * t, 2 * t - 1) for t in range(1, 16)] + [(2 * t + 1, 2 * t + 2) for t in range(15)]


def back(pairs):
    return [(b, a) for a, b in pairs]


def shift(phase, amount):
    pairs = []
    for z in range(4):
        for y in range(4):
            for c in range(2):
                for x in range(4):
                    to = {"z": z, "y": y, "x": x}
                    axis = ("xyz", "zxy")[c][phase]
                    to[axis] = (to[axis] + amount) % 4
                    pairs.append((((z * 4 + y) * 2 + c) * 4 + x, ((to["z"] * 4 + to["y"]) * 2 + c) * 4 + to["x"]))
    return pairs


def exchange(parts, phase):
    return [parts[0]] + [lax.ppermute(parts[r], ALL, shift(phase, r)) for r in (1, 3, 2)]


def join_kernel(cols, *refs):
    for n in range(4):
        refs[-1][n] = refs[n][..., cols]


def join(parts, after, cols=slice(0, HEAD_DIM)):
    whole = pl.BlockSpec(memory_space=pltpu.VMEM)
    return pl.pallas_call(
        functools.partial(join_kernel, cols),
        in_specs=[whole] * 4 + [pl.BlockSpec(memory_space=pl.ANY)] * len(after),
        out_specs=whole,
        out_shape=jax.ShapeDtypeStruct((4,) + parts[0].shape[:-1] + (HEAD_DIM,), BF),
        compiler_params=pltpu.CompilerParams(vmem_limit_bytes=16 * MIB),
    )(*parts, *after)


def pick_kernel(me, w_ref, got_ref, after, out_ref):
    mine = w_ref[:, pl.ds(pl.multiple_of(me[2] * HALF, HALF), HALF)]
    for core in range(2):

        @pl.when(me[2] == core)
        def _():
            out_ref[core * 64 : core * 64 + 64, :] = mine
            out_ref[64 - core * 64 : 128 - core * 64, :] = got_ref[...]


def pick(me, weights, got, after):
    whole = pl.BlockSpec(memory_space=pltpu.VMEM)
    return pl.pallas_call(
        pick_kernel,
        in_specs=[pl.BlockSpec(memory_space=pltpu.SMEM), whole, whole, pl.BlockSpec(memory_space=pl.ANY)],
        out_specs=whole,
        out_shape=jax.ShapeDtypeStruct((128, HALF), BF),
        compiler_params=pltpu.CompilerParams(vmem_limit_bytes=16 * MIB),
    )(me, weights, got, after)


def ring(value, phase, amount):
    return lax.ppermute(value, ALL, shift(phase, -amount))


def fold_kernel(a_ref, b_ref, got_a, got_b, after, out_a, out_b):
    for ref, got, out in ((a_ref, got_a, out_a), (b_ref, got_b, out_b)):
        out[...] = (ref[...].astype(jnp.float32) + got[...].astype(jnp.float32)).astype(BF)


def fold(ahead, behind, got_a, got_b, after):
    def block(start):
        return pl.BlockSpec((1, 4, 128, HEAD_DIM), lambda i: (i + start, 0, 0, 0))

    whole = jax.ShapeDtypeStruct(ahead.shape, BF)
    return pl.pallas_call(
        fold_kernel,
        grid=(2,),
        in_specs=[block(0), block(2), block(0), block(0), pl.BlockSpec(memory_space=pl.ANY)],
        out_specs=[block(0), block(2)],
        out_shape=[whole, whole],
        input_output_aliases={0: 0, 1: 1},
        compiler_params=pltpu.CompilerParams(vmem_limit_bytes=16 * MIB),
    )(ahead, behind, got_a, got_b, after)


def scatter_ring(own, ahead, behind, far_a, far_b, after):
    got_a = lax.ppermute(far_a, ALL, shift(0, 1))
    got_b = lax.ppermute(far_b, ALL, shift(0, -1))
    ahead, behind = fold(ahead, behind, got_a, got_b, after)
    return [own, lax.ppermute(ahead, ALL, shift(0, 1)), lax.ppermute(behind, ALL, shift(0, -1))]


def body(enc_hidden, kv_weights, queries, cotangent, enc_lengths, dec_lengths, dec_partner):
    z, y, c, x = (lax.axis_index(a) for a in ALL)
    me = jnp.stack([z, y, c, x]).astype(jnp.int32)
    meta, info, leave_a, leave_b = depart(me, enc_lengths, dec_lengths, dec_partner, queries, cotangent)
    sent_a = lax.ppermute(leave_a, DP, SEND_A)
    sent_b = lax.ppermute(leave_b, DP, SEND_B)

    got = swap(jnp.where(c == 0, kv_weights[:, HALF:], kv_weights[:, :HALF]))
    own = pick(me, kv_weights, got, leave_a)
    first = [own] + [ring(own, 2, n) for n in (1, 2, 3)]
    part = join(first, [sent_a, sent_b])
    given = swap(hand(me, queries, cotangent, enc_hidden, [part]))
    part = join([part] + [ring(part, 1, n) for n in (1, 2, 3)], [])
    tokens, tokens_t = turn(enc_hidden, given, [part])
    ahead, behind = ring(part, 0, 1), ring(part, 0, -1)
    weights = [[part, ahead, behind, ring(behind[:2], 0, -1), ring(ahead[2:], 0, 1)]]
    part = join(first, [tokens_t], slice(HEAD_DIM, HALF))
    part = join([part] + [ring(part, 1, n) for n in (1, 2, 3)], weights[0][3:])
    weights.append([part, ring(part, 0, 1), ring(part, 0, -1), ring(part, 0, 2)])

    shared = (meta, me, tokens, tokens_t)
    inputs = (queries, cotangent, given, sent_a, sent_b)
    home = [back(SEND_A), back(SEND_B)]

    *results, d0, d1, d3, d2 = run_main(0, *shared, weights[0], *inputs)
    returned = [lax.ppermute(part, DP, pairs) for part, pairs in zip(results[2:], home)]
    parts = exchange([d0, d1, d2, d3], 0)
    *results, d0, d1, d3, far_a, far_b = run_main(1, *shared, weights[1], *inputs, before=results[:2])
    mine, other = results[:2]
    late = [lax.ppermute(part, DP, pairs) for part, pairs in zip(results[2:], home)]

    first = add_parts(parts, [mine, *returned])
    parts = scatter_ring(d0, d1, d3, far_a, far_b, first[0])
    first = exchange(first, 1)
    second = exchange(add_parts(parts, late), 1)
    context, grad_queries = finish(info, [mine, swap(other), *returned, *late])
    kept, given = add_last(me, exchange(add_both(first, second), 2), [context])
    got = swap(given)
    grad = jnp.concatenate([jnp.where(c == 0, kept, got), jnp.where(c == 0, got, kept)], axis=1)
    return context, grad_queries, grad


def solution(mesh):
    fine = Mesh(mesh.devices.reshape(4, 4, 2, 4), ALL)
    rows = P(ALL, None)
    cut = P(DP, "x")
    return jax.shard_map(
        body,
        mesh=fine,
        in_specs=(rows, cut, rows, rows, P(), P(), P()),
        out_specs=(rows, rows, cut),
        check_vma=False,
    )
```

```python
import functools

import jax
import jax.numpy as jnp
from jax import lax
from jax.experimental import pallas as pl
from jax.experimental.pallas import tpu as pltpu
from jax.sharding import Mesh, PartitionSpec as P

HEAD_DIM = 256
SEGS = 4
TOK = 512
PAIR = 2 * TOK
WIN = 176
POOL = PAIR + 2 * WIN
D = 2048
HALF = 512
GROUP = 4
DP = ("z", "y", "c")
ALL = ("z", "y", "c", "x")
MIB = 1024 * 1024
BF = jnp.bfloat16


def align(start, limit):
    return jnp.minimum((start // 16) * 16, limit - WIN)


def mm(a, b, dims):
    return lax.dot_general(a, b, (dims, ((), ())), preferred_element_type=jnp.float32)


def attend(meta, k_s, v_s, q_s, ct_s, ctx_s, gq_s, gk_s, gv_s):
    scale = HEAD_DIM ** -0.5
    col = lax.broadcasted_iota(jnp.int32, (WIN, WIN), 1)
    row = lax.broadcasted_iota(jnp.int32, (WIN, WIN), 0)
    row_wide = lax.broadcasted_iota(jnp.int32, (WIN, HEAD_DIM), 0)
    for first in range(0, 2 * SEGS, GROUP):
        spots, loaded, scores = [], [], []
        for e in range(first, first + GROUP):
            es, el, ds, dl = meta[e, 0], meta[e, 1], meta[e, 2], meta[e, 3]
            ew = pl.multiple_of(align(es, PAIR), 16)
            dw = pl.multiple_of(align(ds, POOL), 16)
            spots.append((pl.ds(ew, WIN), pl.ds(dw, WIN), es - ew, el, ds - dw, dl))
        for ewin, dwin, *_ in spots:
            k, v, q, ct = k_s[ewin, :], v_s[ewin, :], q_s[dwin, :], ct_s[dwin, :]
            loaded.append((k, v, q, ct))
            scores.append((mm(q, k, ((1,), (1,))), mm(ct, v, ((1,), (1,)))))
        weights = []
        for (_, _, elo, el, dlo, dl), (s, gw) in zip(spots, scores):
            k_live = (col >= elo) & (col < elo + el)
            q_live = (row[:, :1] >= dlo) & (row[:, :1] < dlo + dl)
            s = jnp.where(k_live, s * scale, -jnp.inf)
            p = jnp.exp(s - jnp.max(s, axis=1, keepdims=True))
            share = jnp.where(q_live, 1.0 / jnp.sum(p, axis=1, keepdims=True), 0.0)
            w = p * share
            delta = jnp.sum(w * gw, axis=1, keepdims=True)
            weights.append((w.astype(BF), (w * (gw - delta) * scale).astype(BF)))
        results = []
        for (k, v, q, ct), (w_low, gs) in zip(loaded, weights):
            results.append((
                mm(w_low, v, ((1,), (0,))).astype(BF),
                mm(gs, k, ((1,), (0,))).astype(BF),
                mm(gs, q, ((0,), (0,))).astype(BF),
                mm(w_low, ct, ((0,), (0,))).astype(BF),
            ))
        for (ewin, dwin, elo, el, dlo, dl), (ctx, gq, gk, gv) in zip(spots, results):
            d_in = (row_wide >= dlo) & (row_wide < dlo + dl)
            e_in = (row_wide >= elo) & (row_wide < elo + el)
            ctx_s[dwin, :] = jnp.where(d_in, ctx, ctx_s[dwin, :])
            gq_s[dwin, :] = jnp.where(d_in, gq, gq_s[dwin, :])
            gk_s[ewin, :] = jnp.where(e_in, gk, gk_s[ewin, :])
            gv_s[ewin, :] = jnp.where(e_in, gv, gv_s[ewin, :])


def places(me):
    z, y, c, x = me[0], me[1], me[2], me[3]

    def block(ra, rb, rc):
        first = c == 0
        bx = (x + jnp.where(first, ra, rb)) & 3
        by = (y + jnp.where(first, rb, rc)) & 3
        bz = (z + jnp.where(first, rc, ra)) & 3
        return bx, bz * 4 + by

    return block


def main_kernel(weights, extra, meta, me, x_ref, xt_ref, *refs):
    qm, qo, qa, qb, cm, co, ca, cb = refs[weights : weights + 8]
    om, oo, oa, ob, d0, d1, d3, *d2 = refs[weights + 8 + extra : -10]
    k_s, v_s, gk_s, gv_s, q_s, ct_s, ctx_s, gq_s, dw_s, w_s = refs[-10:]
    step = pl.program_id(0)
    block = places(me)

    w0, w1, w3, *w2 = refs[:weights]

    @pl.when(step == 0)
    def _():
        def take(rc, carry):
            for rb in range(4):
                far = w2[rb * len(w2) // 4][rb % (4 // len(w2)), rc]
                for ra, value in enumerate((w0[rb, rc], w1[rb, rc], far, w3[rb, rc])):
                    bx, bzy = block(ra, rb, rc)
                    w_s[bx, pl.ds(pl.multiple_of(bzy * 128, 128), 128), :] = value
            return carry

        lax.fori_loop(0, 4, take, 0)

    x = x_ref[...]
    k_s[...] = jnp.dot(x, w_s[step], preferred_element_type=jnp.float32).astype(BF)
    v_s[...] = jnp.dot(x, w_s[2 + step], preferred_element_type=jnp.float32).astype(BF)
    for pool, parts in ((q_s, (qm, qo, qa, qb)), (ct_s, (cm, co, ca, cb))):
        pool[0:TOK, :] = parts[0][...]
        pool[TOK:PAIR, :] = parts[1][...]
        pool[PAIR : PAIR + WIN, :] = parts[2][...]
        pool[PAIR + WIN :, :] = parts[3][...]
    attend(meta, k_s, v_s, q_s, ct_s, ctx_s, gq_s, gk_s, gv_s)
    for kind, pool in enumerate((ctx_s, gq_s)):
        om[kind] = pool[0:TOK, :]
        oo[kind] = pool[TOK:PAIR, :]
        oa[kind] = pool[PAIR : PAIR + WIN, :]
        ob[kind] = pool[PAIR + WIN :, :]
    xt = xt_ref[...]
    dw_s[step] = jnp.dot(xt, gk_s[...], preferred_element_type=jnp.float32).astype(BF)
    dw_s[2 + step] = jnp.dot(xt, gv_s[...], preferred_element_type=jnp.float32).astype(BF)

    @pl.when(step == 1)
    def _():
        def put(rc, carry):
            for rb in range(4):
                for ra, out in ((0, d0), (1, d1), (3, d3), (2, d2[rb * len(d2) // 4])):
                    bx, bzy = block(ra, rb, rc)
                    at = rb % (4 // len(d2)) if ra == 2 else rb
                    out[at, rc] = dw_s[bx, pl.ds(pl.multiple_of(bzy * 128, 128), 128), :]
            return carry

        lax.fori_loop(0, 4, put, 0)


def run_main(chunk, meta, me, x, xt, weights, q, ct, given, sent_a, sent_b, before=()):
    def fixed(*shape):
        return pl.BlockSpec(shape, lambda i, m, e: (0,) * len(shape), pipeline_mode=pl.Buffered(1))

    def wide():
        return pl.BlockSpec((TOK, HEAD_DIM), lambda i, m, e: (0, i * 4 + e[2] * 2 + chunk))

    def narrow(rows, kind):
        return pl.BlockSpec((rows, HEAD_DIM), lambda i, m, e: (0, kind * 4 + i * 2 + chunk))

    def handed(kind):
        return pl.BlockSpec((TOK, HEAD_DIM), lambda i, m, e: (0, i * 4 + kind * 2 + chunk))

    def out(rows):
        return pl.BlockSpec((2, rows, HEAD_DIM), lambda i, m, e: (0, 0, i * 2 + chunk))

    def out_far():
        return pl.BlockSpec((2, WIN, HEAD_DIM), lambda i, m, e: (0, 0, i))

    def part(shape):
        return pl.BlockSpec(shape, lambda i, m, e: (0, 0, 0, 0))

    parts = [(4, 4, 128, HEAD_DIM)] * 4 if chunk == 0 else [(4, 4, 128, HEAD_DIM)] * 3 + [(2, 4, 128, HEAD_DIM)] * 2
    anywhere = pl.BlockSpec(memory_space=pl.ANY)
    pair = pltpu.VMEM((PAIR, HEAD_DIM), BF)
    pool = pltpu.VMEM((POOL, HEAD_DIM), BF)
    return pl.pallas_call(
        functools.partial(main_kernel, len(weights), len(before)),
        grid_spec=pltpu.PrefetchScalarGridSpec(
            num_scalar_prefetch=2,
            grid=(2,),
            in_specs=[fixed(PAIR, D), fixed(D, PAIR), *[fixed(*w.shape) for w in weights],
                      wide(), handed(0), narrow(WIN, 0), narrow(WIN, 0),
                      wide(), handed(1), narrow(WIN, 1), narrow(WIN, 1)]
            + [anywhere] * len(before),
            out_specs=[out(TOK), out(TOK), out_far(), out_far(), *[part(shape) for shape in parts]],
            scratch_shapes=[pair, pair, pair, pair, pool, pool, pool, pool,
                            pltpu.VMEM((4, D, HEAD_DIM), BF), pltpu.VMEM((4, D, HEAD_DIM), BF)],
        ),
        out_shape=[jax.ShapeDtypeStruct((2, TOK, 2 * HALF), BF)] * 2
        + [jax.ShapeDtypeStruct((2, WIN, HALF), BF)] * 2
        + [jax.ShapeDtypeStruct(shape, BF) for shape in parts],
        input_output_aliases={12 + len(weights) + n: n for n in range(len(before))},
        compiler_params=pltpu.CompilerParams(vmem_limit_bytes=44 * MIB),
        cost_estimate=pl.CostEstimate(flops=12_000_000_000, bytes_accessed=24_000_000, transcendentals=500_000),
    )(meta, me, x, xt, *weights, q, given, sent_a, sent_b, ct, given, sent_a, sent_b, *before)


def add(refs):
    return sum(ref[...].astype(jnp.float32) for ref in refs)


def add_kernel(count, *refs):
    total = add(refs[:count]).astype(BF)
    for n, out in enumerate(refs[-4:]):
        out[...] = total[n]


def add_parts(parts, after):
    return pl.pallas_call(
        functools.partial(add_kernel, len(parts)),
        grid=(4,),
        in_specs=[pl.BlockSpec((4, 1, 128, HEAD_DIM), lambda i: (0, i, 0, 0))] * len(parts)
        + [pl.BlockSpec(memory_space=pl.ANY)] * len(after),
        out_specs=[pl.BlockSpec((1, 128, HEAD_DIM), lambda i: (i, 0, 0))] * 4,
        out_shape=[jax.ShapeDtypeStruct((4, 128, HEAD_DIM), BF)] * 4,
        compiler_params=pltpu.CompilerParams(vmem_limit_bytes=16 * MIB),
    )(*parts, *after)


def add_both_kernel(*refs):
    for chunk in range(2):
        total = add(refs[chunk * 4 : chunk * 4 + 4]).astype(BF)
        for n, out in enumerate(refs[-4:]):
            out[:, chunk * HEAD_DIM : (chunk + 1) * HEAD_DIM] = total[n]


def add_both(first, second, after):
    whole = pl.BlockSpec(memory_space=pltpu.VMEM)
    return pl.pallas_call(
        add_both_kernel,
        in_specs=[whole] * 8 + [pl.BlockSpec(memory_space=pl.ANY)] * len(after),
        out_specs=[whole] * 4,
        out_shape=[jax.ShapeDtypeStruct((128, HALF), BF)] * 4,
        compiler_params=pltpu.CompilerParams(vmem_limit_bytes=16 * MIB),
    )(*first, *second, *after)


def add_last_kernel(me, *refs):
    kept, given = refs[-2:]
    for row, out in ((me[2], kept), (1 - me[2], given)):
        rows = pl.ds(pl.multiple_of(row * 64, 64), 64)
        out[...] = sum(ref[rows, :].astype(jnp.float32) for ref in refs[:4])


def add_last(me, parts, after):
    whole = pl.BlockSpec(memory_space=pltpu.VMEM)
    return pl.pallas_call(
        add_last_kernel,
        in_specs=[pl.BlockSpec(memory_space=pltpu.SMEM)] + [whole] * 4
        + [pl.BlockSpec(memory_space=pl.ANY)] * len(after),
        out_specs=[whole] * 2,
        out_shape=[jax.ShapeDtypeStruct((64, HALF), jnp.float32)] * 2,
        compiler_params=pltpu.CompilerParams(vmem_limit_bytes=16 * MIB),
    )(me, *parts, *after)


def depart_kernel(me, enc_len, dec_len, partner, q_ref, ct_ref, meta, info, a_ref, b_ref, sems):
    core, x = me[2], me[3]
    t = me[0] * 4 + me[1]

    info[0], info[1], info[2], info[3] = jnp.int32(0), core, jnp.int32(0), jnp.int32(0)
    device = (t * 2 + core) * 4 + x
    start = jnp.int32(0)
    for slot in range(SEGS):
        begin, length = start, dec_len[slot, device]

        @pl.when((partner[slot, device] >> 5) != t)
        def _():
            info[0] = align(begin, TOK)
            info[2] = begin
            info[3] = length

        start = start + length

    rows = pl.ds(pl.multiple_of(info[0], 16), WIN)
    copies = []
    for n in range(4):
        source = (q_ref, ct_ref)[n // 2]
        for side, out in ((core, a_ref), (1 - core, b_ref)):
            begin = pl.ds(pl.multiple_of((n % 2) * 1024 + side * HALF, HALF), HALF)
            copies.append((source.at[rows, begin], out.at[:, pl.ds(n * HALF, HALF)]))
    copies = [pltpu.make_async_copy(a, b, sems.at[n]) for n, (a, b) in enumerate(copies)]
    for copy in copies:
        copy.start()

    for side in range(2):
        device = (t * 2 + (core if side == 0 else 1 - core)) * 4 + x
        start = jnp.int32(side * TOK)
        for slot in range(SEGS):
            meta[side * SEGS + slot, 0] = start
            meta[side * SEGS + slot, 1] = enc_len[slot, device]
            start = start + enc_len[slot, device]
    for near in range(4):
        dp = t * 2 - 1 + near
        device = jnp.clip(dp, 0, 31) * 4 + x
        real = (dp >= 0) & (dp < 32)
        same = (dp & 1) == core
        start = jnp.int32(0)
        for slot in range(SEGS):
            begin, length = start, dec_len[slot, device]
            owner = partner[slot, device] >> 4
            if near in (1, 2):
                at = begin + jnp.where(same, 0, TOK)
            else:
                at = begin - align(begin, TOK) + PAIR + jnp.where(same, 0, WIN)

            @pl.when(real & ((owner >> 1) == t))
            def _():
                entry = jnp.where((owner & 1) == core, 0, SEGS) + (partner[slot, device] & 3)
                meta[entry, 2] = at
                meta[entry, 3] = length

            start = start + length
    for copy in copies:
        copy.wait()


def depart(me, enc_lengths, dec_lengths, dec_partner, q, ct):
    whole = pl.BlockSpec(memory_space=pl.ANY)
    scalar = pl.BlockSpec(memory_space=pltpu.SMEM)
    return pl.pallas_call(
        depart_kernel,
        in_specs=[scalar, scalar, scalar, scalar, whole, whole],
        out_specs=[scalar, scalar, pl.BlockSpec(memory_space=pltpu.VMEM), pl.BlockSpec(memory_space=pltpu.VMEM)],
        scratch_shapes=[pltpu.SemaphoreType.DMA((8,))],
        out_shape=[jax.ShapeDtypeStruct((2 * SEGS, 4), jnp.int32), jax.ShapeDtypeStruct((4,), jnp.int32)]
        + [jax.ShapeDtypeStruct((WIN, 2048), BF)] * 2,
        compiler_params=pltpu.CompilerParams(vmem_limit_bytes=59 * MIB),
    )(me, enc_lengths.T, dec_lengths.T, dec_partner.T, q, ct)


def hand_kernel(me, q_ref, ct_ref, *refs):
    refs[-1][:, :HALF] = q_ref[...]
    refs[-1][:, HALF:] = ct_ref[...]


def hand(me, q, ct, after):
    def half(i, me):
        return (0, i * 2 + 1 - me[2])

    part = pl.BlockSpec((TOK, HALF), half)
    return pl.pallas_call(
        hand_kernel,
        grid_spec=pltpu.PrefetchScalarGridSpec(
            num_scalar_prefetch=1,
            grid=(2,),
            in_specs=[part, part] + [pl.BlockSpec(memory_space=pl.ANY)] * len(after),
            out_specs=pl.BlockSpec((TOK, 2 * HALF), lambda i, me: (0, i)),
        ),
        out_shape=jax.ShapeDtypeStruct((TOK, 2048), BF),
        compiler_params=pltpu.CompilerParams(vmem_limit_bytes=57 * MIB),
    )(me, q, ct, *after)


def turn_kernel(a_ref, b_ref, *refs):
    x_ref, xt_ref, mark = refs[-3:]
    mark[...] = jnp.zeros_like(mark)
    for n, ref in enumerate((a_ref, b_ref)):
        value = ref[...]
        x_ref[n * TOK : (n + 1) * TOK, :] = value
        xt_ref[:, n * TOK : (n + 1) * TOK] = value.T


def turn(a, b, after):
    part = pl.BlockSpec((TOK, 512), lambda i: (0, i))
    return pl.pallas_call(
        turn_kernel,
        grid=(D // 512,),
        in_specs=[part, part]
        + [pl.BlockSpec(memory_space=pl.ANY)] * len(after),
        out_specs=[pl.BlockSpec((PAIR, 512), lambda i: (0, i)), pl.BlockSpec((512, PAIR), lambda i: (i, 0)),
                   pl.BlockSpec((8, 128), lambda i: (0, 0))],
        out_shape=[jax.ShapeDtypeStruct((PAIR, D), BF), jax.ShapeDtypeStruct((D, PAIR), BF),
                   jax.ShapeDtypeStruct((8, 128), jnp.float32)],
        compiler_params=pltpu.CompilerParams(vmem_limit_bytes=57 * MIB),
    )(a, b, *after)


def finish_kernel(info, *refs):
    ins, outs, mark = refs[:6], refs[6:8], refs[8]
    mark[...] = jnp.zeros_like(mark)
    win = pl.multiple_of(info[0], 16)
    core, start, length = info[1], info[2] - info[0], info[3]
    rows = pl.ds(win, WIN)
    place = lax.broadcasted_iota(jnp.int32, (WIN, HEAD_DIM), 0)
    inside = (place >= start) & (place < start + length)
    mine, theirs, *returned = ins
    for side, base, first in ((core, mine, 0), (1 - core, theirs, 1)):
        for chunk in range(2):
            cols = pl.ds(pl.multiple_of(side * HALF + chunk * HEAD_DIM, HEAD_DIM), HEAD_DIM)
            for kind, out in enumerate(outs):
                out[:, cols] = base[kind, :, chunk * HEAD_DIM : (chunk + 1) * HEAD_DIM]
                out[rows, cols] = jnp.where(inside, returned[chunk * 2 + first][kind], out[rows, cols])


def finish(info, pieces):
    def source(rows, cols):
        return pl.BlockSpec((2, rows, cols), lambda i, e: (0, 0, i))

    out = pl.BlockSpec((TOK, 1024), lambda i, e: (0, i))
    return pl.pallas_call(
        finish_kernel,
        grid_spec=pltpu.PrefetchScalarGridSpec(
            num_scalar_prefetch=1,
            grid=(2,),
            in_specs=[source(TOK, HALF)] * 2 + [source(WIN, HEAD_DIM)] * 4,
            out_specs=[out, out, pl.BlockSpec((8, 128), lambda i, e: (0, 0))],
        ),
        out_shape=[jax.ShapeDtypeStruct((TOK, 2048), BF)] * 2 + [jax.ShapeDtypeStruct((8, 128), jnp.float32)],
        compiler_params=pltpu.CompilerParams(vmem_limit_bytes=59 * MIB),
    )(info, *pieces)


def swap(value):
    return lax.ppermute(value, "c", [(0, 1), (1, 0)])


SEND_A = [(2 * t, 2 * t - 2) for t in range(1, 16)] + [(2 * t + 1, 2 * t + 3) for t in range(15)]
SEND_B = [(2 * t, 2 * t - 1) for t in range(1, 16)] + [(2 * t + 1, 2 * t + 2) for t in range(15)]


def back(pairs):
    return [(b, a) for a, b in pairs]


def shift(phase, amount):
    pairs = []
    for z in range(4):
        for y in range(4):
            for c in range(2):
                for x in range(4):
                    to = {"z": z, "y": y, "x": x}
                    axis = ("xyz", "zxy")[c][phase]
                    to[axis] = (to[axis] + amount) % 4
                    pairs.append((((z * 4 + y) * 2 + c) * 4 + x, ((to["z"] * 4 + to["y"]) * 2 + c) * 4 + to["x"]))
    return pairs


def exchange(parts, phase):
    return [parts[0]] + [lax.ppermute(parts[r], ALL, shift(phase, r)) for r in (1, 3, 2)]


def join_kernel(cols, *refs):
    for n in range(4):
        refs[-1][n] = refs[n][..., cols]


def join(parts, after, cols=slice(0, HEAD_DIM)):
    whole = pl.BlockSpec(memory_space=pltpu.VMEM)
    return pl.pallas_call(
        functools.partial(join_kernel, cols),
        in_specs=[whole] * 4 + [pl.BlockSpec(memory_space=pl.ANY)] * len(after),
        out_specs=whole,
        out_shape=jax.ShapeDtypeStruct((4,) + parts[0].shape[:-1] + (HEAD_DIM,), BF),
        compiler_params=pltpu.CompilerParams(vmem_limit_bytes=16 * MIB),
    )(*parts, *after)


def pick_kernel(me, w_ref, got_ref, *refs):
    out_ref = refs[-1]
    mine = w_ref[:, pl.ds(pl.multiple_of(me[2] * HALF, HALF), HALF)]
    for core in range(2):

        @pl.when(me[2] == core)
        def _():
            out_ref[core * 64 : core * 64 + 64, :] = mine
            out_ref[64 - core * 64 : 128 - core * 64, :] = got_ref[...]


def pick(me, weights, got, after):
    whole = pl.BlockSpec(memory_space=pltpu.VMEM)
    return pl.pallas_call(
        pick_kernel,
        in_specs=[pl.BlockSpec(memory_space=pltpu.SMEM), whole, whole]
        + [pl.BlockSpec(memory_space=pl.ANY)] * len(after),
        out_specs=whole,
        out_shape=jax.ShapeDtypeStruct((128, HALF), BF),
        compiler_params=pltpu.CompilerParams(vmem_limit_bytes=16 * MIB),
    )(me, weights, got, *after)


def ring(value, phase, amount):
    return lax.ppermute(value, ALL, shift(phase, -amount))


def fold_kernel(a_ref, b_ref, got_a, got_b, after, out_a, out_b):
    for ref, got, out in ((a_ref, got_a, out_a), (b_ref, got_b, out_b)):
        out[...] = (ref[...].astype(jnp.float32) + got[...].astype(jnp.float32)).astype(BF)


def fold(ahead, behind, got_a, got_b, after):
    def block(start):
        return pl.BlockSpec((1, 4, 128, HEAD_DIM), lambda i: (i + start, 0, 0, 0))

    whole = jax.ShapeDtypeStruct(ahead.shape, BF)
    return pl.pallas_call(
        fold_kernel,
        grid=(2,),
        in_specs=[block(0), block(2), block(0), block(0), pl.BlockSpec(memory_space=pl.ANY)],
        out_specs=[block(0), block(2)],
        out_shape=[whole, whole],
        input_output_aliases={0: 0, 1: 1},
        compiler_params=pltpu.CompilerParams(vmem_limit_bytes=16 * MIB),
    )(ahead, behind, got_a, got_b, after)


def scatter_ring(own, ahead, behind, far_a, far_b, after):
    got_a = lax.ppermute(far_a, ALL, shift(0, 1))
    got_b = lax.ppermute(far_b, ALL, shift(0, -1))
    ahead, behind = fold(ahead, behind, got_a, got_b, after)
    return [own, lax.ppermute(ahead, ALL, shift(0, 1)), lax.ppermute(behind, ALL, shift(0, -1))]


def body(enc_hidden, kv_weights, queries, cotangent, enc_lengths, dec_lengths, dec_partner):
    z, y, c, x = (lax.axis_index(a) for a in ALL)
    me = jnp.stack([z, y, c, x]).astype(jnp.int32)
    swapped = swap(enc_hidden)
    meta, info, leave_a, leave_b = depart(me, enc_lengths, dec_lengths, dec_partner, queries, cotangent)
    sent_a = lax.ppermute(leave_a, DP, SEND_A)
    sent_b = lax.ppermute(leave_b, DP, SEND_B)

    got = swap(jnp.where(c == 0, kv_weights[:, HALF:], kv_weights[:, :HALF]))
    own = pick(me, kv_weights, got, [info, swapped])
    first = [own] + [ring(own, 2, n) for n in (1, 2, 3)]
    part = join(first, [sent_a, sent_b])
    given = swap(hand(me, queries, cotangent, [part]))
    part = join([part] + [ring(part, 1, n) for n in (1, 2, 3)], [])
    tokens, tokens_t, turned = turn(enc_hidden, swapped, [part])
    ahead, behind = ring(part, 0, 1), ring(part, 0, -1)
    weights = [[part, ahead, behind, ring(behind[:2], 0, -1), ring(ahead[2:], 0, 1)]]
    part = join(first, [turned], slice(HEAD_DIM, HALF))
    part = join([part] + [ring(part, 1, n) for n in (1, 2, 3)], [ahead, behind])
    weights.append([part, ring(part, 0, 1), ring(part, 0, -1), ring(part, 0, 2)])

    shared = (meta, me, tokens, tokens_t)
    inputs = (queries, cotangent, given, sent_a, sent_b)
    home = [back(SEND_A), back(SEND_B)]

    *results, d0, d1, d3, d2 = run_main(0, *shared, weights[0], *inputs)
    returned = [lax.ppermute(part, DP, pairs) for part, pairs in zip(results[2:], home)]
    parts = exchange([d0, d1, d2, d3], 0)
    *results, d0, d1, d3, far_a, far_b = run_main(1, *shared, weights[1], *inputs, before=results[:2])
    mine, other = results[:2]
    late = [lax.ppermute(part, DP, pairs) for part, pairs in zip(results[2:], home)]

    first = add_parts(parts, [far_a, *returned])
    parts = scatter_ring(d0, d1, d3, far_a, far_b, first[0])
    first = exchange(first, 1)
    second = exchange(add_parts(parts, first[1:]), 1)
    context, grad_queries, finished = finish(info, [mine, swap(other), *returned, *late])
    kept, given = add_last(me, exchange(add_both(first, second, late), 2), [finished])
    got = swap(given)
    grad = jnp.concatenate([jnp.where(c == 0, kept, got), jnp.where(c == 0, got, kept)], axis=1)
    return context, grad_queries, grad


def solution(mesh):
    fine = Mesh(mesh.devices.reshape(4, 4, 2, 4), ALL)
    rows = P(ALL, None)
    cut = P(DP, "x")
    return jax.shard_map(
        body,
        mesh=fine,
        in_specs=(rows, cut, rows, rows, P(), P(), P()),
        out_specs=(rows, rows, cut),
        check_vma=False,
    )
```

```python
import functools

import jax
import jax.numpy as jnp
from jax import lax
from jax.experimental import pallas as pl
from jax.experimental.pallas import tpu as pltpu
from jax.sharding import Mesh, PartitionSpec as P

HEAD_DIM = 256
SEGS = 4
TOK = 512
PAIR = 2 * TOK
WIN = 176
POOL = PAIR + 2 * WIN
D = 2048
HALF = 512
GROUP = 4
DP = ("z", "y", "c")
ALL = ("z", "y", "c", "x")
MIB = 1024 * 1024
BF = jnp.bfloat16


def align(start, limit):
    return jnp.minimum((start // 16) * 16, limit - WIN)


def mm(a, b, dims):
    return lax.dot_general(a, b, (dims, ((), ())), preferred_element_type=jnp.float32)


def attend(meta, k_s, v_s, q_s, ct_s, ctx_s, gq_s, gk_s, gv_s):
    scale = HEAD_DIM ** -0.5
    col = lax.broadcasted_iota(jnp.int32, (WIN, WIN), 1)
    row = lax.broadcasted_iota(jnp.int32, (WIN, WIN), 0)
    row_wide = lax.broadcasted_iota(jnp.int32, (WIN, HEAD_DIM), 0)
    for first in range(0, 2 * SEGS, GROUP):
        spots, loaded, scores = [], [], []
        for e in range(first, first + GROUP):
            es, el, ds, dl = meta[e, 0], meta[e, 1], meta[e, 2], meta[e, 3]
            ew = pl.multiple_of(align(es, PAIR), 16)
            dw = pl.multiple_of(align(ds, POOL), 16)
            spots.append((pl.ds(ew, WIN), pl.ds(dw, WIN), es - ew, el, ds - dw, dl))
        for ewin, dwin, *_ in spots:
            k, v, q, ct = k_s[ewin, :], v_s[ewin, :], q_s[dwin, :], ct_s[dwin, :]
            loaded.append((k, v, q, ct))
            scores.append((mm(q, k, ((1,), (1,))), mm(ct, v, ((1,), (1,)))))
        weights = []
        for (_, _, elo, el, dlo, dl), (s, gw) in zip(spots, scores):
            k_live = (col >= elo) & (col < elo + el)
            q_live = (row[:, :1] >= dlo) & (row[:, :1] < dlo + dl)
            s = jnp.where(k_live, s * scale, -jnp.inf)
            p = jnp.exp(s - jnp.max(s, axis=1, keepdims=True))
            share = jnp.where(q_live, 1.0 / jnp.sum(p, axis=1, keepdims=True), 0.0)
            w = p * share
            delta = jnp.sum(w * gw, axis=1, keepdims=True)
            weights.append((w.astype(BF), (w * (gw - delta) * scale).astype(BF)))
        results = []
        for (k, v, q, ct), (w_low, gs) in zip(loaded, weights):
            results.append((
                mm(w_low, v, ((1,), (0,))).astype(BF),
                mm(gs, k, ((1,), (0,))).astype(BF),
                mm(gs, q, ((0,), (0,))).astype(BF),
                mm(w_low, ct, ((0,), (0,))).astype(BF),
            ))
        for (ewin, dwin, elo, el, dlo, dl), (ctx, gq, gk, gv) in zip(spots, results):
            d_in = (row_wide >= dlo) & (row_wide < dlo + dl)
            e_in = (row_wide >= elo) & (row_wide < elo + el)
            ctx_s[dwin, :] = jnp.where(d_in, ctx, ctx_s[dwin, :])
            gq_s[dwin, :] = jnp.where(d_in, gq, gq_s[dwin, :])
            gk_s[ewin, :] = jnp.where(e_in, gk, gk_s[ewin, :])
            gv_s[ewin, :] = jnp.where(e_in, gv, gv_s[ewin, :])


def places(me):
    z, y, c, x = me[0], me[1], me[2], me[3]

    def block(ra, rb, rc):
        first = c == 0
        bx = (x + jnp.where(first, ra, rb)) & 3
        by = (y + jnp.where(first, rb, rc)) & 3
        bz = (z + jnp.where(first, rc, ra)) & 3
        return bx, bz * 4 + by

    return block


def main_kernel(weights, extra, meta, me, x_ref, xt_ref, *refs):
    qm, qo, qa, qb, cm, co, ca, cb = refs[weights : weights + 8]
    om, oo, oa, ob, d0, d1, d3, *d2 = refs[weights + 8 + extra : -10]
    k_s, v_s, gk_s, gv_s, q_s, ct_s, ctx_s, gq_s, dw_s, w_s = refs[-10:]
    step = pl.program_id(0)
    block = places(me)

    w0, w1, w3, *w2 = refs[:weights]

    @pl.when(step == 0)
    def _():
        def take(rc, carry):
            for rb in range(4):
                far = w2[rb * len(w2) // 4][rb % (4 // len(w2)), rc]
                for ra, value in enumerate((w0[rb, rc], w1[rb, rc], far, w3[rb, rc])):
                    bx, bzy = block(ra, rb, rc)
                    w_s[bx, pl.ds(pl.multiple_of(bzy * 128, 128), 128), :] = value
            return carry

        lax.fori_loop(0, 4, take, 0)

    x = x_ref[...]
    k_s[...] = jnp.dot(x, w_s[step], preferred_element_type=jnp.float32).astype(BF)
    v_s[...] = jnp.dot(x, w_s[2 + step], preferred_element_type=jnp.float32).astype(BF)
    for pool, parts in ((q_s, (qm, qo, qa, qb)), (ct_s, (cm, co, ca, cb))):
        pool[0:TOK, :] = parts[0][...]
        pool[TOK:PAIR, :] = parts[1][...]
        pool[PAIR : PAIR + WIN, :] = parts[2][...]
        pool[PAIR + WIN :, :] = parts[3][...]
    attend(meta, k_s, v_s, q_s, ct_s, ctx_s, gq_s, gk_s, gv_s)
    for kind, pool in enumerate((ctx_s, gq_s)):
        om[kind] = pool[0:TOK, :]
        oo[kind] = pool[TOK:PAIR, :]
        oa[kind] = pool[PAIR : PAIR + WIN, :]
        ob[kind] = pool[PAIR + WIN :, :]
    xt = xt_ref[...]
    dw_s[step] = jnp.dot(xt, gk_s[...], preferred_element_type=jnp.float32).astype(BF)
    dw_s[2 + step] = jnp.dot(xt, gv_s[...], preferred_element_type=jnp.float32).astype(BF)

    @pl.when(step == 1)
    def _():
        def put(rc, carry):
            for rb in range(4):
                for ra, out in ((0, d0), (1, d1), (3, d3), (2, d2[rb * len(d2) // 4])):
                    bx, bzy = block(ra, rb, rc)
                    at = rb % (4 // len(d2)) if ra == 2 else rb
                    out[at, rc] = dw_s[bx, pl.ds(pl.multiple_of(bzy * 128, 128), 128), :]
            return carry

        lax.fori_loop(0, 4, put, 0)


def run_main(chunk, meta, me, x, xt, weights, q, ct, given, sent_a, sent_b, before=()):
    whole = pl.BlockSpec(memory_space=pltpu.VMEM)

    def wide():
        return pl.BlockSpec((TOK, HEAD_DIM), lambda i, m, e: (0, i * 4 + e[2] * 2 + chunk))

    def narrow(rows, kind):
        return pl.BlockSpec((rows, HEAD_DIM), lambda i, m, e: (0, kind * 4 + i * 2 + chunk))

    def handed(kind):
        return pl.BlockSpec((TOK, HEAD_DIM), lambda i, m, e: (0, i * 4 + kind * 2 + chunk))

    def out(rows):
        return pl.BlockSpec((2, rows, HEAD_DIM), lambda i, m, e: (0, 0, i * 2 + chunk))

    def out_far():
        return pl.BlockSpec((2, WIN, HEAD_DIM), lambda i, m, e: (0, 0, i))

    parts = [(4, 4, 128, HEAD_DIM)] * 4 if chunk == 0 else [(4, 4, 128, HEAD_DIM)] * 3 + [(2, 4, 128, HEAD_DIM)] * 2
    anywhere = pl.BlockSpec(memory_space=pl.ANY)
    pair = pltpu.VMEM((PAIR, HEAD_DIM), BF)
    pool = pltpu.VMEM((POOL, HEAD_DIM), BF)
    return pl.pallas_call(
        functools.partial(main_kernel, len(weights), len(before)),
        grid_spec=pltpu.PrefetchScalarGridSpec(
            num_scalar_prefetch=2,
            grid=(2,),
            in_specs=[whole, whole, *[whole for w in weights],
                      wide(), handed(0), narrow(WIN, 0), narrow(WIN, 0),
                      wide(), handed(1), narrow(WIN, 1), narrow(WIN, 1)]
            + [anywhere] * len(before),
            out_specs=[out(TOK), out(TOK), out_far(), out_far(), *[whole for shape in parts]],
            scratch_shapes=[pair, pair, pair, pair, pool, pool, pool, pool,
                            pltpu.VMEM((4, D, HEAD_DIM), BF), pltpu.VMEM((4, D, HEAD_DIM), BF)],
        ),
        out_shape=[jax.ShapeDtypeStruct((2, TOK, 2 * HALF), BF)] * 2
        + [jax.ShapeDtypeStruct((2, WIN, HALF), BF)] * 2
        + [jax.ShapeDtypeStruct(shape, BF) for shape in parts],
        input_output_aliases={12 + len(weights) + n: n for n in range(len(before))},
        compiler_params=pltpu.CompilerParams(vmem_limit_bytes=28 * MIB),
        cost_estimate=pl.CostEstimate(flops=12_000_000_000, bytes_accessed=24_000_000, transcendentals=500_000),
    )(meta, me, x, xt, *weights, q, given, sent_a, sent_b, ct, given, sent_a, sent_b, *before)


def add(refs):
    return sum(ref[...].astype(jnp.float32) for ref in refs)


def add_kernel(count, *refs):
    total = add(refs[:count]).astype(BF)
    for n, out in enumerate(refs[-4:]):
        out[...] = total[n]


def add_parts(parts, after):
    return pl.pallas_call(
        functools.partial(add_kernel, len(parts)),
        grid=(4,),
        in_specs=[pl.BlockSpec((4, 1, 128, HEAD_DIM), lambda i: (0, i, 0, 0))] * len(parts)
        + [pl.BlockSpec(memory_space=pl.ANY)] * len(after),
        out_specs=[pl.BlockSpec((1, 128, HEAD_DIM), lambda i: (i, 0, 0))] * 4,
        out_shape=[jax.ShapeDtypeStruct((4, 128, HEAD_DIM), BF)] * 4,
        compiler_params=pltpu.CompilerParams(vmem_limit_bytes=16 * MIB),
    )(*parts, *after)


def add_both_kernel(*refs):
    for chunk in range(2):
        total = add(refs[chunk * 4 : chunk * 4 + 4]).astype(BF)
        for n, out in enumerate(refs[-4:]):
            out[:, chunk * HEAD_DIM : (chunk + 1) * HEAD_DIM] = total[n]


def add_both(first, second, after):
    whole = pl.BlockSpec(memory_space=pltpu.VMEM)
    return pl.pallas_call(
        add_both_kernel,
        in_specs=[whole] * 8 + [pl.BlockSpec(memory_space=pl.ANY)] * len(after),
        out_specs=[whole] * 4,
        out_shape=[jax.ShapeDtypeStruct((128, HALF), BF)] * 4,
        compiler_params=pltpu.CompilerParams(vmem_limit_bytes=16 * MIB),
    )(*first, *second, *after)


def add_last_kernel(me, *refs):
    kept, given = refs[-2:]
    for row, out in ((me[2], kept), (1 - me[2], given)):
        rows = pl.ds(pl.multiple_of(row * 64, 64), 64)
        out[...] = sum(ref[rows, :].astype(jnp.float32) for ref in refs[:4])


def add_last(me, parts, after):
    whole = pl.BlockSpec(memory_space=pltpu.VMEM)
    return pl.pallas_call(
        add_last_kernel,
        in_specs=[pl.BlockSpec(memory_space=pltpu.SMEM)] + [whole] * 4
        + [pl.BlockSpec(memory_space=pl.ANY)] * len(after),
        out_specs=[whole] * 2,
        out_shape=[jax.ShapeDtypeStruct((64, HALF), jnp.float32)] * 2,
        compiler_params=pltpu.CompilerParams(vmem_limit_bytes=16 * MIB),
    )(me, *parts, *after)


def depart_kernel(me, enc_len, dec_len, partner, q_ref, ct_ref, meta, info, a_ref, b_ref, sems):
    core, x = me[2], me[3]
    t = me[0] * 4 + me[1]

    info[0], info[1], info[2], info[3] = jnp.int32(0), core, jnp.int32(0), jnp.int32(0)
    device = (t * 2 + core) * 4 + x
    start = jnp.int32(0)
    for slot in range(SEGS):
        begin, length = start, dec_len[slot, device]

        @pl.when((partner[slot, device] >> 5) != t)
        def _():
            info[0] = align(begin, TOK)
            info[2] = begin
            info[3] = length

        start = start + length

    rows = pl.ds(pl.multiple_of(info[0], 16), WIN)
    copies = []
    for n in range(4):
        source = (q_ref, ct_ref)[n // 2]
        for side, out in ((core, a_ref), (1 - core, b_ref)):
            begin = pl.ds(pl.multiple_of((n % 2) * 1024 + side * HALF, HALF), HALF)
            copies.append((source.at[rows, begin], out.at[:, pl.ds(n * HALF, HALF)]))
    copies = [pltpu.make_async_copy(a, b, sems.at[n]) for n, (a, b) in enumerate(copies)]
    for copy in copies:
        copy.start()

    for side in range(2):
        device = (t * 2 + (core if side == 0 else 1 - core)) * 4 + x
        start = jnp.int32(side * TOK)
        for slot in range(SEGS):
            meta[side * SEGS + slot, 0] = start
            meta[side * SEGS + slot, 1] = enc_len[slot, device]
            start = start + enc_len[slot, device]
    for near in range(4):
        dp = t * 2 - 1 + near
        device = jnp.clip(dp, 0, 31) * 4 + x
        real = (dp >= 0) & (dp < 32)
        same = (dp & 1) == core
        start = jnp.int32(0)
        for slot in range(SEGS):
            begin, length = start, dec_len[slot, device]
            owner = partner[slot, device] >> 4
            if near in (1, 2):
                at = begin + jnp.where(same, 0, TOK)
            else:
                at = begin - align(begin, TOK) + PAIR + jnp.where(same, 0, WIN)

            @pl.when(real & ((owner >> 1) == t))
            def _():
                entry = jnp.where((owner & 1) == core, 0, SEGS) + (partner[slot, device] & 3)
                meta[entry, 2] = at
                meta[entry, 3] = length

            start = start + length
    for copy in copies:
        copy.wait()


def depart(me, enc_lengths, dec_lengths, dec_partner, q, ct):
    whole = pl.BlockSpec(memory_space=pl.ANY)
    scalar = pl.BlockSpec(memory_space=pltpu.SMEM)
    return pl.pallas_call(
        depart_kernel,
        in_specs=[scalar, scalar, scalar, scalar, whole, whole],
        out_specs=[scalar, scalar, pl.BlockSpec(memory_space=pltpu.VMEM), pl.BlockSpec(memory_space=pltpu.VMEM)],
        scratch_shapes=[pltpu.SemaphoreType.DMA((8,))],
        out_shape=[jax.ShapeDtypeStruct((2 * SEGS, 4), jnp.int32), jax.ShapeDtypeStruct((4,), jnp.int32)]
        + [jax.ShapeDtypeStruct((WIN, 2048), BF)] * 2,
        compiler_params=pltpu.CompilerParams(vmem_limit_bytes=59 * MIB),
    )(me, enc_lengths.T, dec_lengths.T, dec_partner.T, q, ct)


def hand_kernel(me, q_ref, ct_ref, *refs):
    refs[-1][:, :HALF] = q_ref[...]
    refs[-1][:, HALF:] = ct_ref[...]


def hand(me, q, ct, after):
    def half(i, me):
        return (0, i * 2 + 1 - me[2])

    part = pl.BlockSpec((TOK, HALF), half)
    return pl.pallas_call(
        hand_kernel,
        grid_spec=pltpu.PrefetchScalarGridSpec(
            num_scalar_prefetch=1,
            grid=(2,),
            in_specs=[part, part] + [pl.BlockSpec(memory_space=pl.ANY)] * len(after),
            out_specs=pl.BlockSpec((TOK, 2 * HALF), lambda i, me: (0, i)),
        ),
        out_shape=jax.ShapeDtypeStruct((TOK, 2048), BF),
        compiler_params=pltpu.CompilerParams(vmem_limit_bytes=57 * MIB),
    )(me, q, ct, *after)


def turn_kernel(a_ref, b_ref, *refs):
    x_ref, xt_ref, mark = refs[-3:]
    mark[...] = jnp.zeros_like(mark)
    for n, ref in enumerate((a_ref, b_ref)):
        value = ref[...]
        x_ref[n * TOK : (n + 1) * TOK, :] = value
        xt_ref[:, n * TOK : (n + 1) * TOK] = value.T


def turn(a, b, after):
    part = pl.BlockSpec((TOK, 512), lambda i: (0, i))
    return pl.pallas_call(
        turn_kernel,
        grid=(D // 512,),
        in_specs=[part, part]
        + [pl.BlockSpec(memory_space=pl.ANY)] * len(after),
        out_specs=[pl.BlockSpec((PAIR, 512), lambda i: (0, i)), pl.BlockSpec((512, PAIR), lambda i: (i, 0)),
                   pl.BlockSpec((8, 128), lambda i: (0, 0))],
        out_shape=[jax.ShapeDtypeStruct((PAIR, D), BF), jax.ShapeDtypeStruct((D, PAIR), BF),
                   jax.ShapeDtypeStruct((8, 128), jnp.float32)],
        compiler_params=pltpu.CompilerParams(vmem_limit_bytes=57 * MIB),
    )(a, b, *after)


def finish_kernel(info, *refs):
    ins, outs, mark = refs[:6], refs[6:8], refs[8]
    mark[...] = jnp.zeros_like(mark)
    win = pl.multiple_of(info[0], 16)
    core, start, length = info[1], info[2] - info[0], info[3]
    rows = pl.ds(win, WIN)
    place = lax.broadcasted_iota(jnp.int32, (WIN, HEAD_DIM), 0)
    inside = (place >= start) & (place < start + length)
    mine, theirs, *returned = ins
    for side, base, first in ((core, mine, 0), (1 - core, theirs, 1)):
        for chunk in range(2):
            cols = pl.ds(pl.multiple_of(side * HALF + chunk * HEAD_DIM, HEAD_DIM), HEAD_DIM)
            for kind, out in enumerate(outs):
                out[:, cols] = base[kind, :, chunk * HEAD_DIM : (chunk + 1) * HEAD_DIM]
                out[rows, cols] = jnp.where(inside, returned[chunk * 2 + first][kind], out[rows, cols])


def finish(info, pieces):
    def source(rows, cols):
        return pl.BlockSpec((2, rows, cols), lambda i, e: (0, 0, i))

    out = pl.BlockSpec((TOK, 1024), lambda i, e: (0, i))
    return pl.pallas_call(
        finish_kernel,
        grid_spec=pltpu.PrefetchScalarGridSpec(
            num_scalar_prefetch=1,
            grid=(2,),
            in_specs=[source(TOK, HALF)] * 2 + [source(WIN, HEAD_DIM)] * 4,
            out_specs=[out, out, pl.BlockSpec((8, 128), lambda i, e: (0, 0))],
        ),
        out_shape=[jax.ShapeDtypeStruct((TOK, 2048), BF)] * 2 + [jax.ShapeDtypeStruct((8, 128), jnp.float32)],
        compiler_params=pltpu.CompilerParams(vmem_limit_bytes=59 * MIB),
    )(info, *pieces)


def swap(value):
    return lax.ppermute(value, "c", [(0, 1), (1, 0)])


SEND_A = [(2 * t, 2 * t - 2) for t in range(1, 16)] + [(2 * t + 1, 2 * t + 3) for t in range(15)]
SEND_B = [(2 * t, 2 * t - 1) for t in range(1, 16)] + [(2 * t + 1, 2 * t + 2) for t in range(15)]


def back(pairs):
    return [(b, a) for a, b in pairs]


def shift(phase, amount):
    pairs = []
    for z in range(4):
        for y in range(4):
            for c in range(2):
                for x in range(4):
                    to = {"z": z, "y": y, "x": x}
                    axis = ("xyz", "zxy")[c][phase]
                    to[axis] = (to[axis] + amount) % 4
                    pairs.append((((z * 4 + y) * 2 + c) * 4 + x, ((to["z"] * 4 + to["y"]) * 2 + c) * 4 + to["x"]))
    return pairs


def exchange(parts, phase):
    return [parts[0]] + [lax.ppermute(parts[r], ALL, shift(phase, r)) for r in (1, 3, 2)]


def join_kernel(cols, *refs):
    for n in range(4):
        refs[-1][n] = refs[n][..., cols]


def join(parts, after, cols=slice(0, HEAD_DIM)):
    whole = pl.BlockSpec(memory_space=pltpu.VMEM)
    return pl.pallas_call(
        functools.partial(join_kernel, cols),
        in_specs=[whole] * 4 + [pl.BlockSpec(memory_space=pl.ANY)] * len(after),
        out_specs=whole,
        out_shape=jax.ShapeDtypeStruct((4,) + parts[0].shape[:-1] + (HEAD_DIM,), BF),
        compiler_params=pltpu.CompilerParams(vmem_limit_bytes=16 * MIB),
    )(*parts, *after)


def pick_kernel(me, w_ref, got_ref, *refs):
    out_ref = refs[-1]
    mine = w_ref[:, pl.ds(pl.multiple_of(me[2] * HALF, HALF), HALF)]
    for core in range(2):

        @pl.when(me[2] == core)
        def _():
            out_ref[core * 64 : core * 64 + 64, :] = mine
            out_ref[64 - core * 64 : 128 - core * 64, :] = got_ref[...]


def pick(me, weights, got, after):
    whole = pl.BlockSpec(memory_space=pltpu.VMEM)
    return pl.pallas_call(
        pick_kernel,
        in_specs=[pl.BlockSpec(memory_space=pltpu.SMEM), whole, whole]
        + [pl.BlockSpec(memory_space=pl.ANY)] * len(after),
        out_specs=whole,
        out_shape=jax.ShapeDtypeStruct((128, HALF), BF),
        compiler_params=pltpu.CompilerParams(vmem_limit_bytes=16 * MIB),
    )(me, weights, got, *after)


def ring(value, phase, amount):
    return lax.ppermute(value, ALL, shift(phase, -amount))


def fold_kernel(a_ref, b_ref, got_a, got_b, after, out_a, out_b):
    for ref, got, out in ((a_ref, got_a, out_a), (b_ref, got_b, out_b)):
        out[...] = (ref[...].astype(jnp.float32) + got[...].astype(jnp.float32)).astype(BF)


def fold(ahead, behind, got_a, got_b, after):
    def block(start):
        return pl.BlockSpec((1, 4, 128, HEAD_DIM), lambda i: (i + start, 0, 0, 0))

    whole = jax.ShapeDtypeStruct(ahead.shape, BF)
    return pl.pallas_call(
        fold_kernel,
        grid=(2,),
        in_specs=[block(0), block(2), block(0), block(0), pl.BlockSpec(memory_space=pl.ANY)],
        out_specs=[block(0), block(2)],
        out_shape=[whole, whole],
        input_output_aliases={0: 0, 1: 1},
        compiler_params=pltpu.CompilerParams(vmem_limit_bytes=16 * MIB),
    )(ahead, behind, got_a, got_b, after)


def scatter_ring(own, ahead, behind, far_a, far_b, after):
    got_a = lax.ppermute(far_a, ALL, shift(0, 1))
    got_b = lax.ppermute(far_b, ALL, shift(0, -1))
    ahead, behind = fold(ahead, behind, got_a, got_b, after)
    return [own, lax.ppermute(ahead, ALL, shift(0, 1)), lax.ppermute(behind, ALL, shift(0, -1))]


def body(enc_hidden, kv_weights, queries, cotangent, enc_lengths, dec_lengths, dec_partner):
    z, y, c, x = (lax.axis_index(a) for a in ALL)
    me = jnp.stack([z, y, c, x]).astype(jnp.int32)
    swapped = swap(enc_hidden)
    meta, info, leave_a, leave_b = depart(me, enc_lengths, dec_lengths, dec_partner, queries, cotangent)
    sent_a = lax.ppermute(leave_a, DP, SEND_A)
    sent_b = lax.ppermute(leave_b, DP, SEND_B)

    got = swap(jnp.where(c == 0, kv_weights[:, HALF:], kv_weights[:, :HALF]))
    own = pick(me, kv_weights, got, [info, swapped])
    first = [own] + [ring(own, 2, n) for n in (1, 2, 3)]
    part = join(first, [sent_a, sent_b])
    given = swap(hand(me, queries, cotangent, [part]))
    part = join([part] + [ring(part, 1, n) for n in (1, 2, 3)], [])
    tokens, tokens_t, turned = turn(enc_hidden, swapped, [part])
    ahead, behind = ring(part, 0, 1), ring(part, 0, -1)
    weights = [[part, ahead, behind, ring(behind[:2], 0, -1), ring(ahead[2:], 0, 1)]]
    part = join(first, [turned], slice(HEAD_DIM, HALF))
    part = join([part] + [ring(part, 1, n) for n in (1, 2, 3)], [ahead, behind])
    weights.append([part, ring(part, 0, 1), ring(part, 0, -1), ring(part, 0, 2)])

    shared = (meta, me, tokens, tokens_t)
    inputs = (queries, cotangent, given, sent_a, sent_b)
    home = [back(SEND_A), back(SEND_B)]

    *results, d0, d1, d3, d2 = run_main(0, *shared, weights[0], *inputs)
    returned = [lax.ppermute(part, DP, pairs) for part, pairs in zip(results[2:], home)]
    parts = exchange([d0, d1, d2, d3], 0)
    *results, d0, d1, d3, far_a, far_b = run_main(1, *shared, weights[1], *inputs, before=results[:2])
    mine, other = results[:2]
    late = [lax.ppermute(part, DP, pairs) for part, pairs in zip(results[2:], home)]

    first = add_parts(parts, [far_a, *returned])
    parts = scatter_ring(d0, d1, d3, far_a, far_b, first[0])
    first = exchange(first, 1)
    second = exchange(add_parts(parts, first[1:]), 1)
    context, grad_queries, finished = finish(info, [mine, swap(other), *returned, *late])
    kept, given = add_last(me, exchange(add_both(first, second, [finished]), 2), [])
    got = swap(given)
    grad = jnp.concatenate([jnp.where(c == 0, kept, got), jnp.where(c == 0, got, kept)], axis=1)
    return context, grad_queries, grad


def solution(mesh):
    fine = Mesh(mesh.devices.reshape(4, 4, 2, 4), ALL)
    rows = P(ALL, None)
    cut = P(DP, "x")
    return jax.shard_map(
        body,
        mesh=fine,
        in_specs=(rows, cut, rows, rows, P(), P(), P()),
        out_specs=(rows, rows, cut),
        check_vma=False,
    )
```

```python
import functools

import jax
import jax.numpy as jnp
from jax import lax
from jax.experimental import pallas as pl
from jax.experimental.pallas import tpu as pltpu
from jax.sharding import Mesh, PartitionSpec as P

HEAD_DIM = 256
SEGS = 4
TOK = 512
PAIR = 2 * TOK
WIN = 176
POOL = PAIR + 2 * WIN
D = 2048
HALF = 512
GROUP = 4
DP = ("z", "y", "c")
ALL = ("z", "y", "c", "x")
MIB = 1024 * 1024
BF = jnp.bfloat16


def align(start, limit):
    return jnp.minimum((start // 16) * 16, limit - WIN)


def mm(a, b, dims):
    return lax.dot_general(a, b, (dims, ((), ())), preferred_element_type=jnp.float32)


def attend(meta, k_s, v_s, q_s, ct_s, ctx_s, gq_s, gk_s, gv_s):
    scale = HEAD_DIM ** -0.5
    col = lax.broadcasted_iota(jnp.int32, (WIN, WIN), 1)
    row = lax.broadcasted_iota(jnp.int32, (WIN, WIN), 0)
    row_wide = lax.broadcasted_iota(jnp.int32, (WIN, HEAD_DIM), 0)
    for first in range(0, 2 * SEGS, GROUP):
        spots, loaded, scores = [], [], []
        for e in range(first, first + GROUP):
            es, el, ds, dl = meta[e, 0], meta[e, 1], meta[e, 2], meta[e, 3]
            ew = pl.multiple_of(align(es, PAIR), 16)
            dw = pl.multiple_of(align(ds, POOL), 16)
            spots.append((pl.ds(ew, WIN), pl.ds(dw, WIN), es - ew, el, ds - dw, dl))
        for ewin, dwin, *_ in spots:
            k, v, q, ct = k_s[ewin, :], v_s[ewin, :], q_s[dwin, :], ct_s[dwin, :]
            loaded.append((k, v, q, ct))
            scores.append((mm(q, k, ((1,), (1,))), mm(ct, v, ((1,), (1,)))))
        weights = []
        for (_, _, elo, el, dlo, dl), (s, gw) in zip(spots, scores):
            k_live = (col >= elo) & (col < elo + el)
            q_live = (row[:, :1] >= dlo) & (row[:, :1] < dlo + dl)
            s = jnp.where(k_live, s * scale, -jnp.inf)
            p = jnp.exp(s - jnp.max(s, axis=1, keepdims=True))
            share = jnp.where(q_live, 1.0 / jnp.sum(p, axis=1, keepdims=True), 0.0)
            w = p * share
            delta = jnp.sum(w * gw, axis=1, keepdims=True)
            weights.append((w.astype(BF), (w * (gw - delta) * scale).astype(BF)))
        results = []
        for (k, v, q, ct), (w_low, gs) in zip(loaded, weights):
            results.append((
                mm(w_low, v, ((1,), (0,))).astype(BF),
                mm(gs, k, ((1,), (0,))).astype(BF),
                mm(gs, q, ((0,), (0,))).astype(BF),
                mm(w_low, ct, ((0,), (0,))).astype(BF),
            ))
        for (ewin, dwin, elo, el, dlo, dl), (ctx, gq, gk, gv) in zip(spots, results):
            d_in = (row_wide >= dlo) & (row_wide < dlo + dl)
            e_in = (row_wide >= elo) & (row_wide < elo + el)
            ctx_s[dwin, :] = jnp.where(d_in, ctx, ctx_s[dwin, :])
            gq_s[dwin, :] = jnp.where(d_in, gq, gq_s[dwin, :])
            gk_s[ewin, :] = jnp.where(e_in, gk, gk_s[ewin, :])
            gv_s[ewin, :] = jnp.where(e_in, gv, gv_s[ewin, :])


def places(me):
    z, y, c, x = me[0], me[1], me[2], me[3]

    def block(ra, rb, rc):
        first = c == 0
        bx = (x + jnp.where(first, ra, rb)) & 3
        by = (y + jnp.where(first, rb, rc)) & 3
        bz = (z + jnp.where(first, rc, ra)) & 3
        return bx, bz * 4 + by

    return block


def main_kernel(weights, extra, meta, me, x_ref, xt_ref, *refs):
    qm, qo, qa, qb, cm, co, ca, cb = refs[weights : weights + 8]
    om, oo, oa, ob, d0, d1, d3, *d2 = refs[weights + 8 + extra : -10]
    k_s, v_s, gk_s, gv_s, q_s, ct_s, ctx_s, gq_s, dw_s, w_s = refs[-10:]
    step = pl.program_id(0)
    block = places(me)

    w0, w1, w3, *w2 = refs[:weights]

    @pl.when(step == 0)
    def _():
        def take(rc, carry):
            for rb in range(4):
                far = w2[rb * len(w2) // 4][rb % (4 // len(w2)), rc]
                for ra, value in enumerate((w0[rb, rc], w1[rb, rc], far, w3[rb, rc])):
                    bx, bzy = block(ra, rb, rc)
                    w_s[bx, pl.ds(pl.multiple_of(bzy * 128, 128), 128), :] = value
            return carry

        lax.fori_loop(0, 4, take, 0)

    x = x_ref[...]
    k_s[...] = jnp.dot(x, w_s[step], preferred_element_type=jnp.float32).astype(BF)
    v_s[...] = jnp.dot(x, w_s[2 + step], preferred_element_type=jnp.float32).astype(BF)
    for pool, parts in ((q_s, (qm, qo, qa, qb)), (ct_s, (cm, co, ca, cb))):
        pool[0:TOK, :] = parts[0][...]
        pool[TOK:PAIR, :] = parts[1][...]
        pool[PAIR : PAIR + WIN, :] = parts[2][...]
        pool[PAIR + WIN :, :] = parts[3][...]
    attend(meta, k_s, v_s, q_s, ct_s, ctx_s, gq_s, gk_s, gv_s)
    for kind, pool in enumerate((ctx_s, gq_s)):
        om[kind] = pool[0:TOK, :]
        oo[kind] = pool[TOK:PAIR, :]
        oa[kind] = pool[PAIR : PAIR + WIN, :]
        ob[kind] = pool[PAIR + WIN :, :]
    xt = xt_ref[...]
    dw_s[step] = jnp.dot(xt, gk_s[...], preferred_element_type=jnp.float32).astype(BF)
    dw_s[2 + step] = jnp.dot(xt, gv_s[...], preferred_element_type=jnp.float32).astype(BF)

    @pl.when(step == 1)
    def _():
        def put(rc, carry):
            for rb in range(4):
                for ra, out in ((0, d0), (1, d1), (3, d3), (2, d2[rb * len(d2) // 4])):
                    bx, bzy = block(ra, rb, rc)
                    at = rb % (4 // len(d2)) if ra == 2 else rb
                    out[at, rc] = dw_s[bx, pl.ds(pl.multiple_of(bzy * 128, 128), 128), :]
            return carry

        lax.fori_loop(0, 4, put, 0)


def run_main(chunk, meta, me, x, xt, weights, q, ct, q_other, ct_other, sent_a, sent_b, before=()):
    whole = pl.BlockSpec(memory_space=pltpu.VMEM)

    def wide():
        return pl.BlockSpec((TOK, HEAD_DIM), lambda i, m, e: (0, i * 4 + e[2] * 2 + chunk))

    def narrow(rows, kind):
        return pl.BlockSpec((rows, HEAD_DIM), lambda i, m, e: (0, kind * 4 + i * 2 + chunk))

    def out(rows):
        return pl.BlockSpec((2, rows, HEAD_DIM), lambda i, m, e: (0, 0, i * 2 + chunk))

    def out_far():
        return pl.BlockSpec((2, WIN, HEAD_DIM), lambda i, m, e: (0, 0, i))

    parts = [(4, 4, 128, HEAD_DIM)] * 4 if chunk == 0 else [(4, 4, 128, HEAD_DIM)] * 3 + [(2, 4, 128, HEAD_DIM)] * 2
    anywhere = pl.BlockSpec(memory_space=pl.ANY)
    pair = pltpu.VMEM((PAIR, HEAD_DIM), BF)
    pool = pltpu.VMEM((POOL, HEAD_DIM), BF)
    return pl.pallas_call(
        functools.partial(main_kernel, len(weights), len(before)),
        grid_spec=pltpu.PrefetchScalarGridSpec(
            num_scalar_prefetch=2,
            grid=(2,),
            in_specs=[whole, whole, *[whole for w in weights],
                      wide(), wide(), narrow(WIN, 0), narrow(WIN, 0),
                      wide(), wide(), narrow(WIN, 1), narrow(WIN, 1)]
            + [anywhere] * len(before),
            out_specs=[out(TOK), out(TOK), out_far(), out_far(), *[whole for shape in parts]],
            scratch_shapes=[pair, pair, pair, pair, pool, pool, pool, pool,
                            pltpu.VMEM((4, D, HEAD_DIM), BF), pltpu.VMEM((4, D, HEAD_DIM), BF)],
        ),
        out_shape=[jax.ShapeDtypeStruct((2, TOK, 2 * HALF), BF)] * 2
        + [jax.ShapeDtypeStruct((2, WIN, HALF), BF)] * 2
        + [jax.ShapeDtypeStruct(shape, BF) for shape in parts],
        input_output_aliases={12 + len(weights) + n: n for n in range(len(before))},
        compiler_params=pltpu.CompilerParams(vmem_limit_bytes=34 * MIB),
        cost_estimate=pl.CostEstimate(flops=12_000_000_000, bytes_accessed=24_000_000, transcendentals=500_000),
    )(meta, me, x, xt, *weights, q, q_other, sent_a, sent_b, ct, ct_other, sent_a, sent_b, *before)


def add(refs):
    return sum(ref[...].astype(jnp.float32) for ref in refs)


def add_kernel(count, *refs):
    total = add(refs[:count]).astype(BF)
    for n, out in enumerate(refs[-4:]):
        out[...] = total[n]


def add_parts(parts, after):
    return pl.pallas_call(
        functools.partial(add_kernel, len(parts)),
        grid=(4,),
        in_specs=[pl.BlockSpec((4, 1, 128, HEAD_DIM), lambda i: (0, i, 0, 0))] * len(parts)
        + [pl.BlockSpec(memory_space=pl.ANY)] * len(after),
        out_specs=[pl.BlockSpec((1, 128, HEAD_DIM), lambda i: (i, 0, 0))] * 4,
        out_shape=[jax.ShapeDtypeStruct((4, 128, HEAD_DIM), BF)] * 4,
        compiler_params=pltpu.CompilerParams(vmem_limit_bytes=16 * MIB),
    )(*parts, *after)


def add_both_kernel(*refs):
    for chunk in range(2):
        total = add(refs[chunk * 4 : chunk * 4 + 4]).astype(BF)
        for n, out in enumerate(refs[-4:]):
            out[:, chunk * HEAD_DIM : (chunk + 1) * HEAD_DIM] = total[n]


def add_both(first, second, after):
    whole = pl.BlockSpec(memory_space=pltpu.VMEM)
    return pl.pallas_call(
        add_both_kernel,
        in_specs=[whole] * 8 + [pl.BlockSpec(memory_space=pl.ANY)] * len(after),
        out_specs=[whole] * 4,
        out_shape=[jax.ShapeDtypeStruct((128, HALF), BF)] * 4,
        compiler_params=pltpu.CompilerParams(vmem_limit_bytes=16 * MIB),
    )(*first, *second, *after)


def add_last_kernel(me, *refs):
    kept, given = refs[-2:]
    for row, out in ((me[2], kept), (1 - me[2], given)):
        rows = pl.ds(pl.multiple_of(row * 64, 64), 64)
        out[...] = sum(ref[rows, :].astype(jnp.float32) for ref in refs[:4])


def add_last(me, parts, after):
    whole = pl.BlockSpec(memory_space=pltpu.VMEM)
    return pl.pallas_call(
        add_last_kernel,
        in_specs=[pl.BlockSpec(memory_space=pltpu.SMEM)] + [whole] * 4
        + [pl.BlockSpec(memory_space=pl.ANY)] * len(after),
        out_specs=[whole] * 2,
        out_shape=[jax.ShapeDtypeStruct((64, HALF), jnp.float32)] * 2,
        compiler_params=pltpu.CompilerParams(vmem_limit_bytes=16 * MIB),
    )(me, *parts, *after)


def depart_kernel(me, enc_len, dec_len, partner, q_ref, ct_ref, meta, info, a_ref, b_ref, sems):
    core, x = me[2], me[3]
    t = me[0] * 4 + me[1]

    info[0], info[1], info[2], info[3] = jnp.int32(0), core, jnp.int32(0), jnp.int32(0)
    device = (t * 2 + core) * 4 + x
    start = jnp.int32(0)
    for slot in range(SEGS):
        begin, length = start, dec_len[slot, device]

        @pl.when((partner[slot, device] >> 5) != t)
        def _():
            info[0] = align(begin, TOK)
            info[2] = begin
            info[3] = length

        start = start + length

    rows = pl.ds(pl.multiple_of(info[0], 16), WIN)
    copies = []
    for n in range(4):
        source = (q_ref, ct_ref)[n // 2]
        for side, out in ((core, a_ref), (1 - core, b_ref)):
            begin = pl.ds(pl.multiple_of((n % 2) * 1024 + side * HALF, HALF), HALF)
            copies.append((source.at[rows, begin], out.at[:, pl.ds(n * HALF, HALF)]))
    copies = [pltpu.make_async_copy(a, b, sems.at[n]) for n, (a, b) in enumerate(copies)]
    for copy in copies:
        copy.start()

    for side in range(2):
        device = (t * 2 + (core if side == 0 else 1 - core)) * 4 + x
        start = jnp.int32(side * TOK)
        for slot in range(SEGS):
            meta[side * SEGS + slot, 0] = start
            meta[side * SEGS + slot, 1] = enc_len[slot, device]
            start = start + enc_len[slot, device]
    for near in range(4):
        dp = t * 2 - 1 + near
        device = jnp.clip(dp, 0, 31) * 4 + x
        real = (dp >= 0) & (dp < 32)
        same = (dp & 1) == core
        start = jnp.int32(0)
        for slot in range(SEGS):
            begin, length = start, dec_len[slot, device]
            owner = partner[slot, device] >> 4
            if near in (1, 2):
                at = begin + jnp.where(same, 0, TOK)
            else:
                at = begin - align(begin, TOK) + PAIR + jnp.where(same, 0, WIN)

            @pl.when(real & ((owner >> 1) == t))
            def _():
                entry = jnp.where((owner & 1) == core, 0, SEGS) + (partner[slot, device] & 3)
                meta[entry, 2] = at
                meta[entry, 3] = length

            start = start + length
    for copy in copies:
        copy.wait()


def depart(me, enc_lengths, dec_lengths, dec_partner, q, ct):
    whole = pl.BlockSpec(memory_space=pl.ANY)
    scalar = pl.BlockSpec(memory_space=pltpu.SMEM)
    return pl.pallas_call(
        depart_kernel,
        in_specs=[scalar, scalar, scalar, scalar, whole, whole],
        out_specs=[scalar, scalar, pl.BlockSpec(memory_space=pltpu.VMEM), pl.BlockSpec(memory_space=pltpu.VMEM)],
        scratch_shapes=[pltpu.SemaphoreType.DMA((8,))],
        out_shape=[jax.ShapeDtypeStruct((2 * SEGS, 4), jnp.int32), jax.ShapeDtypeStruct((4,), jnp.int32)]
        + [jax.ShapeDtypeStruct((WIN, 2048), BF)] * 2,
        compiler_params=pltpu.CompilerParams(vmem_limit_bytes=59 * MIB),
    )(me, enc_lengths.T, dec_lengths.T, dec_partner.T, q, ct)


def turn_kernel(a_ref, b_ref, *refs):
    x_ref, xt_ref, mark = refs[-3:]
    mark[...] = jnp.zeros_like(mark)
    for n, ref in enumerate((a_ref, b_ref)):
        value = ref[...]
        x_ref[n * TOK : (n + 1) * TOK, :] = value
        xt_ref[:, n * TOK : (n + 1) * TOK] = value.T


def turn(a, b, after):
    part = pl.BlockSpec((TOK, 512), lambda i: (0, i))
    return pl.pallas_call(
        turn_kernel,
        grid=(D // 512,),
        in_specs=[part, part]
        + [pl.BlockSpec(memory_space=pl.ANY)] * len(after),
        out_specs=[pl.BlockSpec((PAIR, 512), lambda i: (0, i)), pl.BlockSpec((512, PAIR), lambda i: (i, 0)),
                   pl.BlockSpec((8, 128), lambda i: (0, 0))],
        out_shape=[jax.ShapeDtypeStruct((PAIR, D), BF), jax.ShapeDtypeStruct((D, PAIR), BF),
                   jax.ShapeDtypeStruct((8, 128), jnp.float32)],
        compiler_params=pltpu.CompilerParams(vmem_limit_bytes=16 * MIB),
    )(a, b, *after)


def finish_kernel(info, *refs):
    ins, outs, mark = refs[:6], refs[6:8], refs[8]
    mark[...] = jnp.zeros_like(mark)
    win = pl.multiple_of(info[0], 16)
    core, start, length = info[1], info[2] - info[0], info[3]
    rows = pl.ds(win, WIN)
    place = lax.broadcasted_iota(jnp.int32, (WIN, HEAD_DIM), 0)
    inside = (place >= start) & (place < start + length)
    mine, theirs, *returned = ins
    for side, base, first in ((core, mine, 0), (1 - core, theirs, 1)):
        for chunk in range(2):
            cols = pl.ds(pl.multiple_of(side * HALF + chunk * HEAD_DIM, HEAD_DIM), HEAD_DIM)
            for kind, out in enumerate(outs):
                out[:, cols] = base[kind, :, chunk * HEAD_DIM : (chunk + 1) * HEAD_DIM]
                out[rows, cols] = jnp.where(inside, returned[chunk * 2 + first][kind], out[rows, cols])


def finish(info, pieces):
    def source(rows, cols):
        return pl.BlockSpec((2, rows, cols), lambda i, e: (0, 0, i))

    out = pl.BlockSpec((TOK, 1024), lambda i, e: (0, i))
    return pl.pallas_call(
        finish_kernel,
        grid_spec=pltpu.PrefetchScalarGridSpec(
            num_scalar_prefetch=1,
            grid=(2,),
            in_specs=[source(TOK, HALF)] * 2 + [source(WIN, HEAD_DIM)] * 4,
            out_specs=[out, out, pl.BlockSpec((8, 128), lambda i, e: (0, 0))],
        ),
        out_shape=[jax.ShapeDtypeStruct((TOK, 2048), BF)] * 2 + [jax.ShapeDtypeStruct((8, 128), jnp.float32)],
        compiler_params=pltpu.CompilerParams(vmem_limit_bytes=59 * MIB),
    )(info, *pieces)


def swap(value):
    return lax.ppermute(value, "c", [(0, 1), (1, 0)])


SEND_A = [(2 * t, 2 * t - 2) for t in range(1, 16)] + [(2 * t + 1, 2 * t + 3) for t in range(15)]
SEND_B = [(2 * t, 2 * t - 1) for t in range(1, 16)] + [(2 * t + 1, 2 * t + 2) for t in range(15)]


def back(pairs):
    return [(b, a) for a, b in pairs]


def shift(phase, amount):
    pairs = []
    for z in range(4):
        for y in range(4):
            for c in range(2):
                for x in range(4):
                    to = {"z": z, "y": y, "x": x}
                    axis = ("xyz", "zxy")[c][phase]
                    to[axis] = (to[axis] + amount) % 4
                    pairs.append((((z * 4 + y) * 2 + c) * 4 + x, ((to["z"] * 4 + to["y"]) * 2 + c) * 4 + to["x"]))
    return pairs


def exchange(parts, phase):
    return [parts[0]] + [lax.ppermute(parts[r], ALL, shift(phase, r)) for r in (1, 3, 2)]


def join_kernel(cols, *refs):
    for n in range(4):
        refs[-1][n] = refs[n][..., cols]


def join(parts, after, cols=slice(0, HEAD_DIM)):
    whole = pl.BlockSpec(memory_space=pltpu.VMEM)
    return pl.pallas_call(
        functools.partial(join_kernel, cols),
        in_specs=[whole] * 4 + [pl.BlockSpec(memory_space=pl.ANY)] * len(after),
        out_specs=whole,
        out_shape=jax.ShapeDtypeStruct((4,) + parts[0].shape[:-1] + (HEAD_DIM,), BF),
        compiler_params=pltpu.CompilerParams(vmem_limit_bytes=16 * MIB),
    )(*parts, *after)


def pick_kernel(me, w_ref, got_ref, *refs):
    out_ref = refs[-1]
    mine = w_ref[:, pl.ds(pl.multiple_of(me[2] * HALF, HALF), HALF)]
    for core in range(2):

        @pl.when(me[2] == core)
        def _():
            out_ref[core * 64 : core * 64 + 64, :] = mine
            out_ref[64 - core * 64 : 128 - core * 64, :] = got_ref[...]


def pick(me, weights, got, after):
    whole = pl.BlockSpec(memory_space=pltpu.VMEM)
    return pl.pallas_call(
        pick_kernel,
        in_specs=[pl.BlockSpec(memory_space=pltpu.SMEM), whole, whole]
        + [pl.BlockSpec(memory_space=pl.ANY)] * len(after),
        out_specs=whole,
        out_shape=jax.ShapeDtypeStruct((128, HALF), BF),
        compiler_params=pltpu.CompilerParams(vmem_limit_bytes=16 * MIB),
    )(me, weights, got, *after)


def ring(value, phase, amount):
    return lax.ppermute(value, ALL, shift(phase, -amount))


def fold_kernel(a_ref, b_ref, got_a, got_b, after, out_a, out_b):
    for ref, got, out in ((a_ref, got_a, out_a), (b_ref, got_b, out_b)):
        out[...] = (ref[...].astype(jnp.float32) + got[...].astype(jnp.float32)).astype(BF)


def fold(ahead, behind, got_a, got_b, after):
    def block(start):
        return pl.BlockSpec((1, 4, 128, HEAD_DIM), lambda i: (i + start, 0, 0, 0))

    whole = jax.ShapeDtypeStruct(ahead.shape, BF)
    return pl.pallas_call(
        fold_kernel,
        grid=(2,),
        in_specs=[block(0), block(2), block(0), block(0), pl.BlockSpec(memory_space=pl.ANY)],
        out_specs=[block(0), block(2)],
        out_shape=[whole, whole],
        input_output_aliases={0: 0, 1: 1},
        compiler_params=pltpu.CompilerParams(vmem_limit_bytes=16 * MIB),
    )(ahead, behind, got_a, got_b, after)


def scatter_ring(own, ahead, behind, far_a, far_b, after):
    got_a = lax.ppermute(far_a, ALL, shift(0, 1))
    got_b = lax.ppermute(far_b, ALL, shift(0, -1))
    ahead, behind = fold(ahead, behind, got_a, got_b, after)
    return [own, lax.ppermute(ahead, ALL, shift(0, 1)), lax.ppermute(behind, ALL, shift(0, -1))]


def body(enc_hidden, kv_weights, queries, cotangent, enc_lengths, dec_lengths, dec_partner):
    z, y, c, x = (lax.axis_index(a) for a in ALL)
    me = jnp.stack([z, y, c, x]).astype(jnp.int32)
    swapped = [swap(value) for value in (enc_hidden, queries, cotangent)]
    meta, info, leave_a, leave_b = depart(me, enc_lengths, dec_lengths, dec_partner, queries, cotangent)
    sent_a = lax.ppermute(leave_a, DP, SEND_A)
    sent_b = lax.ppermute(leave_b, DP, SEND_B)

    got = swap(jnp.where(c == 0, kv_weights[:, HALF:], kv_weights[:, :HALF]))
    own = pick(me, kv_weights, got, [info, *swapped])
    first = [own] + [ring(own, 2, n) for n in (1, 2, 3)]
    tokens, tokens_t, turned = turn(enc_hidden, swapped[0], [first[1]])
    part = join(first, [turned, sent_a, sent_b])
    part = join([part] + [ring(part, 1, n) for n in (1, 2, 3)], [])
    ahead, behind = ring(part, 0, 1), ring(part, 0, -1)
    weights = [[part, ahead, behind, ring(behind[:2], 0, -1), ring(ahead[2:], 0, 1)]]
    part = join(first, [part], slice(HEAD_DIM, HALF))
    part = join([part] + [ring(part, 1, n) for n in (1, 2, 3)], [ahead, behind])
    weights.append([part, ring(part, 0, 1), ring(part, 0, -1), ring(part, 0, 2)])

    shared = (meta, me, tokens, tokens_t)
    inputs = (queries, cotangent, *swapped[1:], sent_a, sent_b)
    home = [back(SEND_A), back(SEND_B)]

    *results, d0, d1, d3, d2 = run_main(0, *shared, weights[0], *inputs)
    returned = [lax.ppermute(part, DP, pairs) for part, pairs in zip(results[2:], home)]
    parts = exchange([d0, d1, d2, d3], 0)
    *results, d0, d1, d3, far_a, far_b = run_main(1, *shared, weights[1], *inputs, before=results[:2])
    mine, other = results[:2]
    late = [lax.ppermute(part, DP, pairs) for part, pairs in zip(results[2:], home)]

    first = add_parts(parts, [far_a, *returned])
    parts = scatter_ring(d0, d1, d3, far_a, far_b, first[0])
    first = exchange(first, 1)
    second = exchange(add_parts(parts, first[1:]), 1)
    context, grad_queries, finished = finish(info, [mine, swap(other), *returned, *late])
    kept, given = add_last(me, exchange(add_both(first, second, [finished]), 2), [])
    got = swap(given)
    grad = jnp.concatenate([jnp.where(c == 0, kept, got), jnp.where(c == 0, got, kept)], axis=1)
    return context, grad_queries, grad


def solution(mesh):
    fine = Mesh(mesh.devices.reshape(4, 4, 2, 4), ALL)
    rows = P(ALL, None)
    cut = P(DP, "x")
    return jax.shard_map(
        body,
        mesh=fine,
        in_specs=(rows, cut, rows, rows, P(), P(), P()),
        out_specs=(rows, rows, cut),
        check_vma=False,
    )
```

```python
import functools

import jax
import jax.numpy as jnp
from jax import lax
from jax.experimental import pallas as pl
from jax.experimental.pallas import tpu as pltpu
from jax.sharding import Mesh, PartitionSpec as P

HEAD_DIM = 256
SEGS = 4
TOK = 512
PAIR = 2 * TOK
WIN = 176
POOL = PAIR + 2 * WIN
D = 2048
HALF = 512
GROUP = 4
DP = ("z", "y", "c")
ALL = ("z", "y", "c", "x")
MIB = 1024 * 1024
BF = jnp.bfloat16


def align(start, limit):
    return jnp.minimum((start // 16) * 16, limit - WIN)


def mm(a, b, dims):
    return lax.dot_general(a, b, (dims, ((), ())), preferred_element_type=jnp.float32)


def attend(meta, k_s, v_s, q_s, ct_s, ctx_s, gq_s, gk_s, gv_s):
    scale = HEAD_DIM ** -0.5
    col = lax.broadcasted_iota(jnp.int32, (WIN, WIN), 1)
    row = lax.broadcasted_iota(jnp.int32, (WIN, WIN), 0)
    row_wide = lax.broadcasted_iota(jnp.int32, (WIN, HEAD_DIM), 0)
    for first in range(0, 2 * SEGS, GROUP):
        spots, loaded, scores = [], [], []
        for e in range(first, first + GROUP):
            es, el, ds, dl = meta[e, 0], meta[e, 1], meta[e, 2], meta[e, 3]
            ew = pl.multiple_of(align(es, PAIR), 16)
            dw = pl.multiple_of(align(ds, POOL), 16)
            spots.append((pl.ds(ew, WIN), pl.ds(dw, WIN), es - ew, el, ds - dw, dl))
        for ewin, dwin, *_ in spots:
            k, v, q, ct = k_s[ewin, :], v_s[ewin, :], q_s[dwin, :], ct_s[dwin, :]
            loaded.append((k, v, q, ct))
            scores.append((mm(q, k, ((1,), (1,))), mm(ct, v, ((1,), (1,)))))
        weights = []
        for (_, _, elo, el, dlo, dl), (s, gw) in zip(spots, scores):
            k_live = (col >= elo) & (col < elo + el)
            q_live = (row[:, :1] >= dlo) & (row[:, :1] < dlo + dl)
            s = jnp.where(k_live, s * scale, -jnp.inf)
            p = jnp.exp(s - jnp.max(s, axis=1, keepdims=True))
            share = jnp.where(q_live, 1.0 / jnp.sum(p, axis=1, keepdims=True), 0.0)
            w = p * share
            delta = jnp.sum(w * gw, axis=1, keepdims=True)
            weights.append((w.astype(BF), (w * (gw - delta) * scale).astype(BF)))
        results = []
        for (k, v, q, ct), (w_low, gs) in zip(loaded, weights):
            results.append((
                mm(w_low, v, ((1,), (0,))).astype(BF),
                mm(gs, k, ((1,), (0,))).astype(BF),
                mm(gs, q, ((0,), (0,))).astype(BF),
                mm(w_low, ct, ((0,), (0,))).astype(BF),
            ))
        for (ewin, dwin, elo, el, dlo, dl), (ctx, gq, gk, gv) in zip(spots, results):
            d_in = (row_wide >= dlo) & (row_wide < dlo + dl)
            e_in = (row_wide >= elo) & (row_wide < elo + el)
            ctx_s[dwin, :] = jnp.where(d_in, ctx, ctx_s[dwin, :])
            gq_s[dwin, :] = jnp.where(d_in, gq, gq_s[dwin, :])
            gk_s[ewin, :] = jnp.where(e_in, gk, gk_s[ewin, :])
            gv_s[ewin, :] = jnp.where(e_in, gv, gv_s[ewin, :])


def places(me):
    z, y, c, x = me[0], me[1], me[2], me[3]

    def block(ra, rb, rc):
        first = c == 0
        bx = (x + jnp.where(first, ra, rb)) & 3
        by = (y + jnp.where(first, rb, rc)) & 3
        bz = (z + jnp.where(first, rc, ra)) & 3
        return bx, bz * 4 + by

    return block


def main_kernel(weights, extra, meta, me, x_ref, xt_ref, *refs):
    qm, qo, qa, qb, cm, co, ca, cb = refs[weights : weights + 8]
    om, oo, oa, ob, d0, d1, d3, *d2 = refs[weights + 8 + extra : -10]
    k_s, v_s, gk_s, gv_s, q_s, ct_s, ctx_s, gq_s, dw_s, w_s = refs[-10:]
    step = pl.program_id(0)
    block = places(me)

    w0, w1, w3, *w2 = refs[:weights]

    @pl.when(step == 0)
    def _():
        def take(rc, carry):
            for rb in range(4):
                far = w2[rb * len(w2) // 4][rb % (4 // len(w2)), rc]
                for ra, value in enumerate((w0[rb, rc], w1[rb, rc], far, w3[rb, rc])):
                    bx, bzy = block(ra, rb, rc)
                    w_s[bx, pl.ds(pl.multiple_of(bzy * 128, 128), 128), :] = value
            return carry

        lax.fori_loop(0, 4, take, 0)

    x = x_ref[...]
    k_s[...] = jnp.dot(x, w_s[step], preferred_element_type=jnp.float32).astype(BF)
    v_s[...] = jnp.dot(x, w_s[2 + step], preferred_element_type=jnp.float32).astype(BF)
    for pool, parts in ((q_s, (qm, qo, qa, qb)), (ct_s, (cm, co, ca, cb))):
        pool[0:TOK, :] = parts[0][...]
        pool[TOK:PAIR, :] = parts[1][...]
        pool[PAIR : PAIR + WIN, :] = parts[2][...]
        pool[PAIR + WIN :, :] = parts[3][...]
    attend(meta, k_s, v_s, q_s, ct_s, ctx_s, gq_s, gk_s, gv_s)
    for kind, pool in enumerate((ctx_s, gq_s)):
        om[kind] = pool[0:TOK, :]
        oo[kind] = pool[TOK:PAIR, :]
        oa[kind] = pool[PAIR : PAIR + WIN, :]
        ob[kind] = pool[PAIR + WIN :, :]
    xt = xt_ref[...]
    dw_s[step] = jnp.dot(xt, gk_s[...], preferred_element_type=jnp.float32).astype(BF)
    dw_s[2 + step] = jnp.dot(xt, gv_s[...], preferred_element_type=jnp.float32).astype(BF)

    @pl.when(step == 1)
    def _():
        def put(rc, carry):
            for rb in range(4):
                for ra, out in ((0, d0), (1, d1), (3, d3), (2, d2[rb * len(d2) // 4])):
                    bx, bzy = block(ra, rb, rc)
                    at = rb % (4 // len(d2)) if ra == 2 else rb
                    out[at, rc] = dw_s[bx, pl.ds(pl.multiple_of(bzy * 128, 128), 128), :]
            return carry

        lax.fori_loop(0, 4, put, 0)


def run_main(chunk, meta, me, x, xt, weights, q, ct, q_other, ct_other, sent_a, sent_b, before=()):
    whole = pl.BlockSpec(memory_space=pltpu.VMEM)

    def wide():
        return pl.BlockSpec((TOK, HEAD_DIM), lambda i, m, e: (0, i * 4 + e[2] * 2 + chunk))

    def narrow(rows, kind):
        return pl.BlockSpec((rows, HEAD_DIM), lambda i, m, e: (0, kind * 4 + i * 2 + chunk))

    def out(rows):
        return pl.BlockSpec((2, rows, HEAD_DIM), lambda i, m, e: (0, 0, i * 2 + chunk))

    def out_far():
        return pl.BlockSpec((2, WIN, HEAD_DIM), lambda i, m, e: (0, 0, i))

    parts = [(4, 4, 128, HEAD_DIM)] * 4 if chunk == 0 else [(4, 4, 128, HEAD_DIM)] * 3 + [(2, 4, 128, HEAD_DIM)] * 2
    anywhere = pl.BlockSpec(memory_space=pl.ANY)
    pair = pltpu.VMEM((PAIR, HEAD_DIM), BF)
    pool = pltpu.VMEM((POOL, HEAD_DIM), BF)
    return pl.pallas_call(
        functools.partial(main_kernel, len(weights), len(before)),
        grid_spec=pltpu.PrefetchScalarGridSpec(
            num_scalar_prefetch=2,
            grid=(2,),
            in_specs=[whole, whole, *[whole for w in weights],
                      wide(), wide(), narrow(WIN, 0), narrow(WIN, 0),
                      wide(), wide(), narrow(WIN, 1), narrow(WIN, 1)]
            + [anywhere] * len(before),
            out_specs=[out(TOK), out(TOK), out_far(), out_far(), *[whole for shape in parts]],
            scratch_shapes=[pair, pair, pair, pair, pool, pool, pool, pool,
                            pltpu.VMEM((4, D, HEAD_DIM), BF), pltpu.VMEM((4, D, HEAD_DIM), BF)],
        ),
        out_shape=[jax.ShapeDtypeStruct((2, TOK, 2 * HALF), BF)] * 2
        + [jax.ShapeDtypeStruct((2, WIN, HALF), BF)] * 2
        + [jax.ShapeDtypeStruct(shape, BF) for shape in parts],
        input_output_aliases={12 + len(weights) + n: n for n in range(len(before))},
        compiler_params=pltpu.CompilerParams(vmem_limit_bytes=32 * MIB),
        cost_estimate=pl.CostEstimate(flops=12_000_000_000, bytes_accessed=24_000_000, transcendentals=500_000),
    )(meta, me, x, xt, *weights, q, q_other, sent_a, sent_b, ct, ct_other, sent_a, sent_b, *before)


def add(refs):
    return sum(ref[...].astype(jnp.float32) for ref in refs)


def add_kernel(count, *refs):
    total = add(refs[:count]).astype(BF)
    for n, out in enumerate(refs[-4:]):
        out[...] = total[n]


def add_parts(parts, after):
    return pl.pallas_call(
        functools.partial(add_kernel, len(parts)),
        grid=(4,),
        in_specs=[pl.BlockSpec((4, 1, 128, HEAD_DIM), lambda i: (0, i, 0, 0))] * len(parts)
        + [pl.BlockSpec(memory_space=pl.ANY)] * len(after),
        out_specs=[pl.BlockSpec((1, 128, HEAD_DIM), lambda i: (i, 0, 0))] * 4,
        out_shape=[jax.ShapeDtypeStruct((4, 128, HEAD_DIM), BF)] * 4,
        compiler_params=pltpu.CompilerParams(vmem_limit_bytes=16 * MIB),
    )(*parts, *after)


def add_both_kernel(*refs):
    for chunk in range(2):
        total = add(refs[chunk * 4 : chunk * 4 + 4]).astype(BF)
        for n, out in enumerate(refs[-4:]):
            out[:, chunk * HEAD_DIM : (chunk + 1) * HEAD_DIM] = total[n]


def add_both(first, second, after):
    whole = pl.BlockSpec(memory_space=pltpu.VMEM)
    return pl.pallas_call(
        add_both_kernel,
        in_specs=[whole] * 8 + [pl.BlockSpec(memory_space=pl.ANY)] * len(after),
        out_specs=[whole] * 4,
        out_shape=[jax.ShapeDtypeStruct((128, HALF), BF)] * 4,
        compiler_params=pltpu.CompilerParams(vmem_limit_bytes=16 * MIB),
    )(*first, *second, *after)


def add_last_kernel(me, *refs):
    kept, given = refs[-2:]
    for row, out in ((me[2], kept), (1 - me[2], given)):
        rows = pl.ds(pl.multiple_of(row * 64, 64), 64)
        out[...] = sum(ref[rows, :].astype(jnp.float32) for ref in refs[:4])


def add_last(me, parts, after):
    whole = pl.BlockSpec(memory_space=pltpu.VMEM)
    return pl.pallas_call(
        add_last_kernel,
        in_specs=[pl.BlockSpec(memory_space=pltpu.SMEM)] + [whole] * 4
        + [pl.BlockSpec(memory_space=pl.ANY)] * len(after),
        out_specs=[whole] * 2,
        out_shape=[jax.ShapeDtypeStruct((64, HALF), jnp.float32)] * 2,
        compiler_params=pltpu.CompilerParams(vmem_limit_bytes=16 * MIB),
    )(me, *parts, *after)


def depart_kernel(me, enc_len, dec_len, partner, q_ref, ct_ref, meta, info, a_ref, b_ref, sems):
    core, x = me[2], me[3]
    t = me[0] * 4 + me[1]

    info[0], info[1], info[2], info[3] = jnp.int32(0), core, jnp.int32(0), jnp.int32(0)
    device = (t * 2 + core) * 4 + x
    start = jnp.int32(0)
    for slot in range(SEGS):
        begin, length = start, dec_len[slot, device]

        @pl.when((partner[slot, device] >> 5) != t)
        def _():
            info[0] = align(begin, TOK)
            info[2] = begin
            info[3] = length

        start = start + length

    rows = pl.ds(pl.multiple_of(info[0], 16), WIN)
    copies = []
    for n in range(4):
        source = (q_ref, ct_ref)[n // 2]
        for side, out in ((core, a_ref), (1 - core, b_ref)):
            begin = pl.ds(pl.multiple_of((n % 2) * 1024 + side * HALF, HALF), HALF)
            copies.append((source.at[rows, begin], out.at[:, pl.ds(n * HALF, HALF)]))
    copies = [pltpu.make_async_copy(a, b, sems.at[n]) for n, (a, b) in enumerate(copies)]
    for copy in copies:
        copy.start()

    for side in range(2):
        device = (t * 2 + (core if side == 0 else 1 - core)) * 4 + x
        start = jnp.int32(side * TOK)
        for slot in range(SEGS):
            meta[side * SEGS + slot, 0] = start
            meta[side * SEGS + slot, 1] = enc_len[slot, device]
            start = start + enc_len[slot, device]
    for near in range(4):
        dp = t * 2 - 1 + near
        device = jnp.clip(dp, 0, 31) * 4 + x
        real = (dp >= 0) & (dp < 32)
        same = (dp & 1) == core
        start = jnp.int32(0)
        for slot in range(SEGS):
            begin, length = start, dec_len[slot, device]
            owner = partner[slot, device] >> 4
            if near in (1, 2):
                at = begin + jnp.where(same, 0, TOK)
            else:
                at = begin - align(begin, TOK) + PAIR + jnp.where(same, 0, WIN)

            @pl.when(real & ((owner >> 1) == t))
            def _():
                entry = jnp.where((owner & 1) == core, 0, SEGS) + (partner[slot, device] & 3)
                meta[entry, 2] = at
                meta[entry, 3] = length

            start = start + length
    for copy in copies:
        copy.wait()


def depart(me, enc_lengths, dec_lengths, dec_partner, q, ct):
    whole = pl.BlockSpec(memory_space=pl.ANY)
    scalar = pl.BlockSpec(memory_space=pltpu.SMEM)
    return pl.pallas_call(
        depart_kernel,
        in_specs=[scalar, scalar, scalar, scalar, whole, whole],
        out_specs=[scalar, scalar, pl.BlockSpec(memory_space=pltpu.VMEM), pl.BlockSpec(memory_space=pltpu.VMEM)],
        scratch_shapes=[pltpu.SemaphoreType.DMA((8,))],
        out_shape=[jax.ShapeDtypeStruct((2 * SEGS, 4), jnp.int32), jax.ShapeDtypeStruct((4,), jnp.int32)]
        + [jax.ShapeDtypeStruct((WIN, 2048), BF)] * 2,
        compiler_params=pltpu.CompilerParams(vmem_limit_bytes=59 * MIB),
    )(me, enc_lengths.T, dec_lengths.T, dec_partner.T, q, ct)


def turn_kernel(a_ref, b_ref, *refs):
    x_ref, xt_ref, mark = refs[-3:]
    mark[...] = jnp.zeros_like(mark)
    for n, ref in enumerate((a_ref, b_ref)):
        value = ref[...]
        x_ref[n * TOK : (n + 1) * TOK, :] = value
        xt_ref[:, n * TOK : (n + 1) * TOK] = value.T


def turn(a, b, after):
    part = pl.BlockSpec((TOK, 512), lambda i: (0, i))
    return pl.pallas_call(
        turn_kernel,
        grid=(D // 512,),
        in_specs=[part, part]
        + [pl.BlockSpec(memory_space=pl.ANY)] * len(after),
        out_specs=[pl.BlockSpec((PAIR, 512), lambda i: (0, i)), pl.BlockSpec((512, PAIR), lambda i: (i, 0)),
                   pl.BlockSpec((8, 128), lambda i: (0, 0))],
        out_shape=[jax.ShapeDtypeStruct((PAIR, D), BF), jax.ShapeDtypeStruct((D, PAIR), BF),
                   jax.ShapeDtypeStruct((8, 128), jnp.float32)],
        compiler_params=pltpu.CompilerParams(vmem_limit_bytes=16 * MIB),
    )(a, b, *after)


def finish_kernel(info, *refs):
    ins, outs, mark = refs[:6], refs[6:8], refs[8]
    mark[...] = jnp.zeros_like(mark)
    win = pl.multiple_of(info[0], 16)
    core, start, length = info[1], info[2] - info[0], info[3]
    rows = pl.ds(win, WIN)
    place = lax.broadcasted_iota(jnp.int32, (WIN, HEAD_DIM), 0)
    inside = (place >= start) & (place < start + length)
    mine, theirs, *returned = ins
    for side, base, first in ((core, mine, 0), (1 - core, theirs, 1)):
        for chunk in range(2):
            cols = pl.ds(pl.multiple_of(side * HALF + chunk * HEAD_DIM, HEAD_DIM), HEAD_DIM)
            for kind, out in enumerate(outs):
                out[:, cols] = base[kind, :, chunk * HEAD_DIM : (chunk + 1) * HEAD_DIM]
                out[rows, cols] = jnp.where(inside, returned[chunk * 2 + first][kind], out[rows, cols])


def finish(info, pieces):
    def source(rows, cols):
        return pl.BlockSpec((2, rows, cols), lambda i, e: (0, 0, i))

    out = pl.BlockSpec((TOK, 1024), lambda i, e: (0, i))
    return pl.pallas_call(
        finish_kernel,
        grid_spec=pltpu.PrefetchScalarGridSpec(
            num_scalar_prefetch=1,
            grid=(2,),
            in_specs=[source(TOK, HALF)] * 2 + [source(WIN, HEAD_DIM)] * 4,
            out_specs=[out, out, pl.BlockSpec((8, 128), lambda i, e: (0, 0))],
        ),
        out_shape=[jax.ShapeDtypeStruct((TOK, 2048), BF)] * 2 + [jax.ShapeDtypeStruct((8, 128), jnp.float32)],
        compiler_params=pltpu.CompilerParams(vmem_limit_bytes=24 * MIB),
    )(info, *pieces)


def swap(value):
    return lax.ppermute(value, "c", [(0, 1), (1, 0)])


SEND_A = [(2 * t, 2 * t - 2) for t in range(1, 16)] + [(2 * t + 1, 2 * t + 3) for t in range(15)]
SEND_B = [(2 * t, 2 * t - 1) for t in range(1, 16)] + [(2 * t + 1, 2 * t + 2) for t in range(15)]


def back(pairs):
    return [(b, a) for a, b in pairs]


def shift(phase, amount):
    pairs = []
    for z in range(4):
        for y in range(4):
            for c in range(2):
                for x in range(4):
                    to = {"z": z, "y": y, "x": x}
                    axis = ("xyz", "zxy")[c][phase]
                    to[axis] = (to[axis] + amount) % 4
                    pairs.append((((z * 4 + y) * 2 + c) * 4 + x, ((to["z"] * 4 + to["y"]) * 2 + c) * 4 + to["x"]))
    return pairs


def exchange(parts, phase):
    return [parts[0]] + [lax.ppermute(parts[r], ALL, shift(phase, r)) for r in (1, 3, 2)]


def join_kernel(cols, *refs):
    for n in range(4):
        refs[-1][n] = refs[n][..., cols]


def join(parts, after, cols=slice(0, HEAD_DIM)):
    whole = pl.BlockSpec(memory_space=pltpu.VMEM)
    return pl.pallas_call(
        functools.partial(join_kernel, cols),
        in_specs=[whole] * 4 + [pl.BlockSpec(memory_space=pl.ANY)] * len(after),
        out_specs=whole,
        out_shape=jax.ShapeDtypeStruct((4,) + parts[0].shape[:-1] + (HEAD_DIM,), BF),
        compiler_params=pltpu.CompilerParams(vmem_limit_bytes=16 * MIB),
    )(*parts, *after)


def pick_kernel(me, w_ref, got_ref, *refs):
    out_ref = refs[-1]
    mine = w_ref[:, pl.ds(pl.multiple_of(me[2] * HALF, HALF), HALF)]
    for core in range(2):

        @pl.when(me[2] == core)
        def _():
            out_ref[core * 64 : core * 64 + 64, :] = mine
            out_ref[64 - core * 64 : 128 - core * 64, :] = got_ref[...]


def pick(me, weights, got, after):
    whole = pl.BlockSpec(memory_space=pltpu.VMEM)
    return pl.pallas_call(
        pick_kernel,
        in_specs=[pl.BlockSpec(memory_space=pltpu.SMEM), whole, whole]
        + [pl.BlockSpec(memory_space=pl.ANY)] * len(after),
        out_specs=whole,
        out_shape=jax.ShapeDtypeStruct((128, HALF), BF),
        compiler_params=pltpu.CompilerParams(vmem_limit_bytes=16 * MIB),
    )(me, weights, got, *after)


def ring(value, phase, amount):
    return lax.ppermute(value, ALL, shift(phase, -amount))


def fold_kernel(a_ref, b_ref, got_a, got_b, after, out_a, out_b):
    for ref, got, out in ((a_ref, got_a, out_a), (b_ref, got_b, out_b)):
        out[...] = (ref[...].astype(jnp.float32) + got[...].astype(jnp.float32)).astype(BF)


def fold(ahead, behind, got_a, got_b, after):
    def block(start):
        return pl.BlockSpec((1, 4, 128, HEAD_DIM), lambda i: (i + start, 0, 0, 0))

    whole = jax.ShapeDtypeStruct(ahead.shape, BF)
    return pl.pallas_call(
        fold_kernel,
        grid=(2,),
        in_specs=[block(0), block(2), block(0), block(0), pl.BlockSpec(memory_space=pl.ANY)],
        out_specs=[block(0), block(2)],
        out_shape=[whole, whole],
        input_output_aliases={0: 0, 1: 1},
        compiler_params=pltpu.CompilerParams(vmem_limit_bytes=16 * MIB),
    )(ahead, behind, got_a, got_b, after)


def scatter_ring(own, ahead, behind, far_a, far_b, after):
    got_a = lax.ppermute(far_a, ALL, shift(0, 1))
    got_b = lax.ppermute(far_b, ALL, shift(0, -1))
    ahead, behind = fold(ahead, behind, got_a, got_b, after)
    return [own, lax.ppermute(ahead, ALL, shift(0, 1)), lax.ppermute(behind, ALL, shift(0, -1))]


def body(enc_hidden, kv_weights, queries, cotangent, enc_lengths, dec_lengths, dec_partner):
    z, y, c, x = (lax.axis_index(a) for a in ALL)
    me = jnp.stack([z, y, c, x]).astype(jnp.int32)
    swapped = [swap(value) for value in (enc_hidden, queries, cotangent)]
    meta, info, leave_a, leave_b = depart(me, enc_lengths, dec_lengths, dec_partner, queries, cotangent)
    sent_a = lax.ppermute(leave_a, DP, SEND_A)
    sent_b = lax.ppermute(leave_b, DP, SEND_B)

    got = swap(jnp.where(c == 0, kv_weights[:, HALF:], kv_weights[:, :HALF]))
    own = pick(me, kv_weights, got, [info, *swapped])
    first = [own] + [ring(own, 2, n) for n in (1, 2, 3)]
    tokens, tokens_t, turned = turn(enc_hidden, swapped[0], [first[1]])
    part = join(first, [turned, sent_a, sent_b])
    part = join([part] + [ring(part, 1, n) for n in (1, 2, 3)], [])
    ahead, behind = ring(part, 0, 1), ring(part, 0, -1)
    weights = [[part, ahead, behind, ring(behind[:2], 0, -1), ring(ahead[2:], 0, 1)]]
    part = join(first, [part], slice(HEAD_DIM, HALF))
    part = join([part] + [ring(part, 1, n) for n in (1, 2, 3)], [ahead, behind])
    weights.append([part, ring(part, 0, 1), ring(part, 0, -1), ring(part, 0, 2)])

    shared = (meta, me, tokens, tokens_t)
    inputs = (queries, cotangent, *swapped[1:], sent_a, sent_b)
    home = [back(SEND_A), back(SEND_B)]

    *results, d0, d1, d3, d2 = run_main(0, *shared, weights[0], *inputs)
    returned = [lax.ppermute(part, DP, pairs) for part, pairs in zip(results[2:], home)]
    parts = exchange([d0, d1, d2, d3], 0)
    *results, d0, d1, d3, far_a, far_b = run_main(1, *shared, weights[1], *inputs, before=results[:2])
    mine, other = results[:2]
    late = [lax.ppermute(part, DP, pairs) for part, pairs in zip(results[2:], home)]

    first = add_parts(parts, [far_a, *returned])
    parts = scatter_ring(d0, d1, d3, far_a, far_b, first[0])
    first = exchange(first, 1)
    second = exchange(add_parts(parts, first[1:]), 1)
    context, grad_queries, finished = finish(info, [mine, swap(other), *returned, *late])
    kept, given = add_last(me, exchange(add_both(first, second, late), 2), [finished])
    got = swap(given)
    grad = jnp.concatenate([jnp.where(c == 0, kept, got), jnp.where(c == 0, got, kept)], axis=1)
    return context, grad_queries, grad


def solution(mesh):
    fine = Mesh(mesh.devices.reshape(4, 4, 2, 4), ALL)
    rows = P(ALL, None)
    cut = P(DP, "x")
    return jax.shard_map(
        body,
        mesh=fine,
        in_specs=(rows, cut, rows, rows, P(), P(), P()),
        out_specs=(rows, rows, cut),
        check_vma=False,
    )
```

```python
import functools

import jax
import jax.numpy as jnp
from jax import lax
from jax.experimental import pallas as pl
from jax.experimental.pallas import tpu as pltpu
from jax.sharding import Mesh, PartitionSpec as P

HEAD_DIM = 256
SEGS = 4
TOK = 512
PAIR = 2 * TOK
WIN = 176
POOL = PAIR + 2 * WIN
D = 2048
HALF = 512
GROUP = 4
DP = ("z", "y", "c")
ALL = ("z", "y", "c", "x")
MIB = 1024 * 1024
BF = jnp.bfloat16


def align(start, limit):
    return jnp.minimum((start // 16) * 16, limit - WIN)


def mm(a, b, dims):
    return lax.dot_general(a, b, (dims, ((), ())), preferred_element_type=jnp.float32)


def attend(meta, k_s, v_s, q_s, ct_s, ctx_s, gq_s, gk_s, gv_s):
    scale = HEAD_DIM ** -0.5
    col = lax.broadcasted_iota(jnp.int32, (WIN, WIN), 1)
    row = lax.broadcasted_iota(jnp.int32, (WIN, WIN), 0)
    row_wide = lax.broadcasted_iota(jnp.int32, (WIN, HEAD_DIM), 0)
    for first in range(0, 2 * SEGS, GROUP):
        spots, loaded, scores = [], [], []
        for e in range(first, first + GROUP):
            es, el, ds, dl = meta[e, 0], meta[e, 1], meta[e, 2], meta[e, 3]
            ew = pl.multiple_of(align(es, PAIR), 16)
            dw = pl.multiple_of(align(ds, POOL), 16)
            spots.append((pl.ds(ew, WIN), pl.ds(dw, WIN), es - ew, el, ds - dw, dl))
        for ewin, dwin, *_ in spots:
            k, v, q, ct = k_s[ewin, :], v_s[ewin, :], q_s[dwin, :], ct_s[dwin, :]
            loaded.append((k, v, q, ct))
            scores.append((mm(q, k, ((1,), (1,))), mm(ct, v, ((1,), (1,)))))
        weights = []
        for (_, _, elo, el, dlo, dl), (s, gw) in zip(spots, scores):
            k_live = (col >= elo) & (col < elo + el)
            q_live = (row[:, :1] >= dlo) & (row[:, :1] < dlo + dl)
            s = jnp.where(k_live, s * scale, -jnp.inf)
            p = jnp.exp(s - jnp.max(s, axis=1, keepdims=True))
            share = jnp.where(q_live, 1.0 / jnp.sum(p, axis=1, keepdims=True), 0.0)
            w = p * share
            delta = jnp.sum(w * gw, axis=1, keepdims=True)
            weights.append((w.astype(BF), (w * (gw - delta) * scale).astype(BF)))
        results = []
        for (k, v, q, ct), (w_low, gs) in zip(loaded, weights):
            results.append((
                mm(w_low, v, ((1,), (0,))).astype(BF),
                mm(gs, k, ((1,), (0,))).astype(BF),
                mm(gs, q, ((0,), (0,))).astype(BF),
                mm(w_low, ct, ((0,), (0,))).astype(BF),
            ))
        for (ewin, dwin, elo, el, dlo, dl), (ctx, gq, gk, gv) in zip(spots, results):
            d_in = (row_wide >= dlo) & (row_wide < dlo + dl)
            e_in = (row_wide >= elo) & (row_wide < elo + el)
            ctx_s[dwin, :] = jnp.where(d_in, ctx, ctx_s[dwin, :])
            gq_s[dwin, :] = jnp.where(d_in, gq, gq_s[dwin, :])
            gk_s[ewin, :] = jnp.where(e_in, gk, gk_s[ewin, :])
            gv_s[ewin, :] = jnp.where(e_in, gv, gv_s[ewin, :])


def places(me):
    z, y, c, x = me[0], me[1], me[2], me[3]

    def block(ra, rb, rc):
        first = c == 0
        bx = (x + jnp.where(first, ra, rb)) & 3
        by = (y + jnp.where(first, rb, rc)) & 3
        bz = (z + jnp.where(first, rc, ra)) & 3
        return bx, bz * 4 + by

    return block


def main_kernel(weights, extra, meta, me, x_ref, xt_ref, *refs):
    qm, qo, qa, qb, cm, co, ca, cb = refs[weights : weights + 8]
    om, oo, oa, ob, d0, d1, d3, *d2 = refs[weights + 8 + extra : -10]
    k_s, v_s, gk_s, gv_s, q_s, ct_s, ctx_s, gq_s, dw_s, w_s = refs[-10:]
    step = pl.program_id(0)
    block = places(me)

    w0, w1, w3, *w2 = refs[:weights]

    @pl.when(step == 0)
    def _():
        def take(rc, carry):
            for rb in range(4):
                far = w2[rb * len(w2) // 4][rb % (4 // len(w2)), rc]
                for ra, value in enumerate((w0[rb, rc], w1[rb, rc], far, w3[rb, rc])):
                    bx, bzy = block(ra, rb, rc)
                    w_s[bx, pl.ds(pl.multiple_of(bzy * 128, 128), 128), :] = value
            return carry

        lax.fori_loop(0, 4, take, 0)

    x = x_ref[...]
    k_s[...] = jnp.dot(x, w_s[step], preferred_element_type=jnp.float32).astype(BF)
    v_s[...] = jnp.dot(x, w_s[2 + step], preferred_element_type=jnp.float32).astype(BF)
    for pool, parts in ((q_s, (qm, qo, qa, qb)), (ct_s, (cm, co, ca, cb))):
        pool[0:TOK, :] = parts[0][...]
        pool[TOK:PAIR, :] = parts[1][...]
        pool[PAIR : PAIR + WIN, :] = parts[2][...]
        pool[PAIR + WIN :, :] = parts[3][...]
    attend(meta, k_s, v_s, q_s, ct_s, ctx_s, gq_s, gk_s, gv_s)
    for kind, pool in enumerate((ctx_s, gq_s)):
        om[kind] = pool[0:TOK, :]
        oo[kind] = pool[TOK:PAIR, :]
        oa[kind] = pool[PAIR : PAIR + WIN, :]
        ob[kind] = pool[PAIR + WIN :, :]
    xt = xt_ref[...]
    dw_s[step] = jnp.dot(xt, gk_s[...], preferred_element_type=jnp.float32).astype(BF)
    dw_s[2 + step] = jnp.dot(xt, gv_s[...], preferred_element_type=jnp.float32).astype(BF)

    @pl.when(step == 1)
    def _():
        def put(rc, carry):
            for rb in range(4):
                for ra, out in ((0, d0), (1, d1), (3, d3), (2, d2[rb * len(d2) // 4])):
                    bx, bzy = block(ra, rb, rc)
                    at = rb % (4 // len(d2)) if ra == 2 else rb
                    out[at, rc] = dw_s[bx, pl.ds(pl.multiple_of(bzy * 128, 128), 128), :]
            return carry

        lax.fori_loop(0, 4, put, 0)


def run_main(chunk, meta, me, x, xt, weights, q, ct, q_other, ct_other, sent_a, sent_b, before=()):
    whole = pl.BlockSpec(memory_space=pltpu.VMEM)

    def wide():
        return pl.BlockSpec((TOK, HEAD_DIM), lambda i, m, e: (0, i * 4 + e[2] * 2 + chunk))

    def narrow(rows, kind):
        return pl.BlockSpec((rows, HEAD_DIM), lambda i, m, e: (0, kind * 4 + i * 2 + chunk))

    def out(rows):
        return pl.BlockSpec((2, rows, HEAD_DIM), lambda i, m, e: (0, 0, i * 2 + chunk))

    def out_far():
        return pl.BlockSpec((2, WIN, HEAD_DIM), lambda i, m, e: (0, 0, i))

    parts = [(4, 4, 128, HEAD_DIM)] * 4 if chunk == 0 else [(4, 4, 128, HEAD_DIM)] * 3 + [(2, 4, 128, HEAD_DIM)] * 2
    anywhere = pl.BlockSpec(memory_space=pl.ANY)
    pair = pltpu.VMEM((PAIR, HEAD_DIM), BF)
    pool = pltpu.VMEM((POOL, HEAD_DIM), BF)
    return pl.pallas_call(
        functools.partial(main_kernel, len(weights), len(before)),
        grid_spec=pltpu.PrefetchScalarGridSpec(
            num_scalar_prefetch=2,
            grid=(2,),
            in_specs=[whole, whole, *[whole for w in weights],
                      wide(), wide(), narrow(WIN, 0), narrow(WIN, 0),
                      wide(), wide(), narrow(WIN, 1), narrow(WIN, 1)]
            + [anywhere] * len(before),
            out_specs=[out(TOK), out(TOK), out_far(), out_far(), *[whole for shape in parts]],
            scratch_shapes=[pair, pair, pair, pair, pool, pool, pool, pool,
                            pltpu.VMEM((4, D, HEAD_DIM), BF), pltpu.VMEM((4, D, HEAD_DIM), BF)],
        ),
        out_shape=[jax.ShapeDtypeStruct((2, TOK, 2 * HALF), BF)] * 2
        + [jax.ShapeDtypeStruct((2, WIN, HALF), BF)] * 2
        + [jax.ShapeDtypeStruct(shape, BF) for shape in parts],
        input_output_aliases={12 + len(weights) + n: n for n in range(len(before))},
        compiler_params=pltpu.CompilerParams(vmem_limit_bytes=32 * MIB),
        cost_estimate=pl.CostEstimate(flops=12_000_000_000, bytes_accessed=24_000_000, transcendentals=500_000),
    )(meta, me, x, xt, *weights, q, q_other, sent_a, sent_b, ct, ct_other, sent_a, sent_b, *before)


def add(refs):
    return sum(ref[...].astype(jnp.float32) for ref in refs)


def add_kernel(count, *refs):
    total = add(refs[:count]).astype(BF)
    for n, out in enumerate(refs[-4:]):
        out[...] = total[n]


def add_parts(parts, after):
    return pl.pallas_call(
        functools.partial(add_kernel, len(parts)),
        grid=(4,),
        in_specs=[pl.BlockSpec((4, 1, 128, HEAD_DIM), lambda i: (0, i, 0, 0))] * len(parts)
        + [pl.BlockSpec(memory_space=pl.ANY)] * len(after),
        out_specs=[pl.BlockSpec((1, 128, HEAD_DIM), lambda i: (i, 0, 0))] * 4,
        out_shape=[jax.ShapeDtypeStruct((4, 128, HEAD_DIM), BF)] * 4,
        compiler_params=pltpu.CompilerParams(vmem_limit_bytes=16 * MIB),
    )(*parts, *after)


def add_both_kernel(*refs):
    for chunk in range(2):
        total = add(refs[chunk * 4 : chunk * 4 + 4]).astype(BF)
        for n, out in enumerate(refs[-4:]):
            out[:, chunk * HEAD_DIM : (chunk + 1) * HEAD_DIM] = total[n]


def add_both(first, second, after):
    whole = pl.BlockSpec(memory_space=pltpu.VMEM)
    return pl.pallas_call(
        add_both_kernel,
        in_specs=[whole] * 8 + [pl.BlockSpec(memory_space=pl.ANY)] * len(after),
        out_specs=[whole] * 4,
        out_shape=[jax.ShapeDtypeStruct((128, HALF), BF)] * 4,
        compiler_params=pltpu.CompilerParams(vmem_limit_bytes=16 * MIB),
    )(*first, *second, *after)


def add_last_kernel(me, *refs):
    kept, given = refs[-2:]
    for row, out in ((me[2], kept), (1 - me[2], given)):
        rows = pl.ds(pl.multiple_of(row * 64, 64), 64)
        out[...] = sum(ref[rows, :].astype(jnp.float32) for ref in refs[:4])


def add_last(me, parts, after):
    whole = pl.BlockSpec(memory_space=pltpu.VMEM)
    return pl.pallas_call(
        add_last_kernel,
        in_specs=[pl.BlockSpec(memory_space=pltpu.SMEM)] + [whole] * 4
        + [pl.BlockSpec(memory_space=pl.ANY)] * len(after),
        out_specs=[whole] * 2,
        out_shape=[jax.ShapeDtypeStruct((64, HALF), jnp.float32)] * 2,
        compiler_params=pltpu.CompilerParams(vmem_limit_bytes=16 * MIB),
    )(me, *parts, *after)


def depart_kernel(me, enc_len, dec_len, partner, q_ref, ct_ref, meta, info, a_ref, b_ref, sems):
    core, x = me[2], me[3]
    t = me[0] * 4 + me[1]

    info[0], info[1], info[2], info[3] = jnp.int32(0), core, jnp.int32(0), jnp.int32(0)
    device = (t * 2 + core) * 4 + x
    start = jnp.int32(0)
    for slot in range(SEGS):
        begin, length = start, dec_len[slot, device]

        @pl.when((partner[slot, device] >> 5) != t)
        def _():
            info[0] = align(begin, TOK)
            info[2] = begin
            info[3] = length

        start = start + length

    rows = pl.ds(pl.multiple_of(info[0], 16), WIN)
    copies = []
    for n in range(4):
        source = (q_ref, ct_ref)[n // 2]
        for side, out in ((core, a_ref), (1 - core, b_ref)):
            begin = pl.ds(pl.multiple_of((n % 2) * 1024 + side * HALF, HALF), HALF)
            copies.append((source.at[rows, begin], out.at[:, pl.ds(n * HALF, HALF)]))
    copies = [pltpu.make_async_copy(a, b, sems.at[n]) for n, (a, b) in enumerate(copies)]
    for copy in copies:
        copy.start()

    for side in range(2):
        device = (t * 2 + (core if side == 0 else 1 - core)) * 4 + x
        start = jnp.int32(side * TOK)
        for slot in range(SEGS):
            meta[side * SEGS + slot, 0] = start
            meta[side * SEGS + slot, 1] = enc_len[slot, device]
            start = start + enc_len[slot, device]
    for near in range(4):
        dp = t * 2 - 1 + near
        device = jnp.clip(dp, 0, 31) * 4 + x
        real = (dp >= 0) & (dp < 32)
        same = (dp & 1) == core
        start = jnp.int32(0)
        for slot in range(SEGS):
            begin, length = start, dec_len[slot, device]
            owner = partner[slot, device] >> 4
            if near in (1, 2):
                at = begin + jnp.where(same, 0, TOK)
            else:
                at = begin - align(begin, TOK) + PAIR + jnp.where(same, 0, WIN)

            @pl.when(real & ((owner >> 1) == t))
            def _():
                entry = jnp.where((owner & 1) == core, 0, SEGS) + (partner[slot, device] & 3)
                meta[entry, 2] = at
                meta[entry, 3] = length

            start = start + length
    for copy in copies:
        copy.wait()


def depart(me, enc_lengths, dec_lengths, dec_partner, q, ct):
    whole = pl.BlockSpec(memory_space=pl.ANY)
    scalar = pl.BlockSpec(memory_space=pltpu.SMEM)
    return pl.pallas_call(
        depart_kernel,
        in_specs=[scalar, scalar, scalar, scalar, whole, whole],
        out_specs=[scalar, scalar, pl.BlockSpec(memory_space=pltpu.VMEM), pl.BlockSpec(memory_space=pltpu.VMEM)],
        scratch_shapes=[pltpu.SemaphoreType.DMA((8,))],
        out_shape=[jax.ShapeDtypeStruct((2 * SEGS, 4), jnp.int32), jax.ShapeDtypeStruct((4,), jnp.int32)]
        + [jax.ShapeDtypeStruct((WIN, 2048), BF)] * 2,
        compiler_params=pltpu.CompilerParams(vmem_limit_bytes=59 * MIB),
    )(me, enc_lengths.T, dec_lengths.T, dec_partner.T, q, ct)


def turn_kernel(a_ref, b_ref, *refs):
    x_ref, xt_ref, mark = refs[-3:]
    mark[...] = jnp.zeros_like(mark)
    for n, ref in enumerate((a_ref, b_ref)):
        value = ref[...]
        x_ref[n * TOK : (n + 1) * TOK, :] = value
        xt_ref[:, n * TOK : (n + 1) * TOK] = value.T


def turn(a, b, after):
    part = pl.BlockSpec((TOK, 512), lambda i: (0, i))
    return pl.pallas_call(
        turn_kernel,
        grid=(D // 512,),
        in_specs=[part, part]
        + [pl.BlockSpec(memory_space=pl.ANY)] * len(after),
        out_specs=[pl.BlockSpec((PAIR, 512), lambda i: (0, i)), pl.BlockSpec((512, PAIR), lambda i: (i, 0)),
                   pl.BlockSpec((8, 128), lambda i: (0, 0))],
        out_shape=[jax.ShapeDtypeStruct((PAIR, D), BF), jax.ShapeDtypeStruct((D, PAIR), BF),
                   jax.ShapeDtypeStruct((8, 128), jnp.float32)],
        compiler_params=pltpu.CompilerParams(vmem_limit_bytes=16 * MIB),
    )(a, b, *after)


def finish_kernel(info, *refs):
    ins, outs, mark = refs[:6], refs[6:8], refs[8]
    mark[...] = jnp.zeros_like(mark)
    win = pl.multiple_of(info[0], 16)
    core, start, length = info[1], info[2] - info[0], info[3]
    rows = pl.ds(win, WIN)
    place = lax.broadcasted_iota(jnp.int32, (WIN, HEAD_DIM), 0)
    inside = (place >= start) & (place < start + length)
    mine, theirs, *returned = ins
    for side, base, first in ((core, mine, 0), (1 - core, theirs, 1)):
        for chunk in range(2):
            cols = pl.ds(pl.multiple_of(side * HALF + chunk * HEAD_DIM, HEAD_DIM), HEAD_DIM)
            for kind, out in enumerate(outs):
                out[:, cols] = base[kind, :, chunk * HEAD_DIM : (chunk + 1) * HEAD_DIM]
                out[rows, cols] = jnp.where(inside, returned[chunk * 2 + first][kind], out[rows, cols])


def finish(info, pieces):
    def source(rows, cols):
        return pl.BlockSpec((2, rows, cols), lambda i, e: (0, 0, i))

    out = pl.BlockSpec((TOK, 1024), lambda i, e: (0, i))
    return pl.pallas_call(
        finish_kernel,
        grid_spec=pltpu.PrefetchScalarGridSpec(
            num_scalar_prefetch=1,
            grid=(2,),
            in_specs=[source(TOK, HALF)] * 2 + [source(WIN, HEAD_DIM)] * 4,
            out_specs=[out, out, pl.BlockSpec((8, 128), lambda i, e: (0, 0))],
        ),
        out_shape=[jax.ShapeDtypeStruct((TOK, 2048), BF)] * 2 + [jax.ShapeDtypeStruct((8, 128), jnp.float32)],
        compiler_params=pltpu.CompilerParams(vmem_limit_bytes=24 * MIB),
    )(info, *pieces)


def swap(value):
    return lax.ppermute(value, "c", [(0, 1), (1, 0)])


SEND_A = [(2 * t, 2 * t - 2) for t in range(1, 16)] + [(2 * t + 1, 2 * t + 3) for t in range(15)]
SEND_B = [(2 * t, 2 * t - 1) for t in range(1, 16)] + [(2 * t + 1, 2 * t + 2) for t in range(15)]


def back(pairs):
    return [(b, a) for a, b in pairs]


def shift(phase, amount):
    pairs = []
    for z in range(4):
        for y in range(4):
            for c in range(2):
                for x in range(4):
                    to = {"z": z, "y": y, "x": x}
                    axis = ("xyz", "zxy")[c][phase]
                    to[axis] = (to[axis] + amount) % 4
                    pairs.append((((z * 4 + y) * 2 + c) * 4 + x, ((to["z"] * 4 + to["y"]) * 2 + c) * 4 + to["x"]))
    return pairs


def exchange(parts, phase):
    return [parts[0]] + [lax.ppermute(parts[r], ALL, shift(phase, r)) for r in (2, 1, 3)]


def join_kernel(cols, *refs):
    for n in range(4):
        refs[-1][n] = refs[n][..., cols]


def join(parts, after, cols=slice(0, HEAD_DIM)):
    whole = pl.BlockSpec(memory_space=pltpu.VMEM)
    return pl.pallas_call(
        functools.partial(join_kernel, cols),
        in_specs=[whole] * 4 + [pl.BlockSpec(memory_space=pl.ANY)] * len(after),
        out_specs=whole,
        out_shape=jax.ShapeDtypeStruct((4,) + parts[0].shape[:-1] + (HEAD_DIM,), BF),
        compiler_params=pltpu.CompilerParams(vmem_limit_bytes=16 * MIB),
    )(*parts, *after)


def pick_kernel(me, w_ref, got_ref, *refs):
    out_ref = refs[-1]
    mine = w_ref[:, pl.ds(pl.multiple_of(me[2] * HALF, HALF), HALF)]
    for core in range(2):

        @pl.when(me[2] == core)
        def _():
            out_ref[core * 64 : core * 64 + 64, :] = mine
            out_ref[64 - core * 64 : 128 - core * 64, :] = got_ref[...]


def pick(me, weights, got, after):
    whole = pl.BlockSpec(memory_space=pltpu.VMEM)
    return pl.pallas_call(
        pick_kernel,
        in_specs=[pl.BlockSpec(memory_space=pltpu.SMEM), whole, whole]
        + [pl.BlockSpec(memory_space=pl.ANY)] * len(after),
        out_specs=whole,
        out_shape=jax.ShapeDtypeStruct((128, HALF), BF),
        compiler_params=pltpu.CompilerParams(vmem_limit_bytes=16 * MIB),
    )(me, weights, got, *after)


def ring(value, phase, amount):
    return lax.ppermute(value, ALL, shift(phase, -amount))


def fold_kernel(a_ref, b_ref, got_a, got_b, after, out_a, out_b):
    for ref, got, out in ((a_ref, got_a, out_a), (b_ref, got_b, out_b)):
        out[...] = (ref[...].astype(jnp.float32) + got[...].astype(jnp.float32)).astype(BF)


def fold(ahead, behind, got_a, got_b, after):
    def block(start):
        return pl.BlockSpec((1, 4, 128, HEAD_DIM), lambda i: (i + start, 0, 0, 0))

    whole = jax.ShapeDtypeStruct(ahead.shape, BF)
    return pl.pallas_call(
        fold_kernel,
        grid=(2,),
        in_specs=[block(0), block(2), block(0), block(0), pl.BlockSpec(memory_space=pl.ANY)],
        out_specs=[block(0), block(2)],
        out_shape=[whole, whole],
        input_output_aliases={0: 0, 1: 1},
        compiler_params=pltpu.CompilerParams(vmem_limit_bytes=16 * MIB),
    )(ahead, behind, got_a, got_b, after)


def scatter_ring(own, ahead, behind, far_a, far_b, after):
    got_a = lax.ppermute(far_a, ALL, shift(0, 1))
    got_b = lax.ppermute(far_b, ALL, shift(0, -1))
    ahead, behind = fold(ahead, behind, got_a, got_b, after)
    return [own, lax.ppermute(ahead, ALL, shift(0, 1)), lax.ppermute(behind, ALL, shift(0, -1))]


def body(enc_hidden, kv_weights, queries, cotangent, enc_lengths, dec_lengths, dec_partner):
    z, y, c, x = (lax.axis_index(a) for a in ALL)
    me = jnp.stack([z, y, c, x]).astype(jnp.int32)
    swapped = [swap(value) for value in (enc_hidden, queries, cotangent)]
    meta, info, leave_a, leave_b = depart(me, enc_lengths, dec_lengths, dec_partner, queries, cotangent)
    sent_a = lax.ppermute(leave_a, DP, SEND_A)
    sent_b = lax.ppermute(leave_b, DP, SEND_B)

    got = swap(jnp.where(c == 0, kv_weights[:, HALF:], kv_weights[:, :HALF]))
    own = pick(me, kv_weights, got, [info, *swapped])
    first = [own] + [ring(own, 2, n) for n in (1, 2, 3)]
    tokens, tokens_t, turned = turn(enc_hidden, swapped[0], [first[1]])
    part = join(first, [turned, sent_a, sent_b])
    part = join([part] + [ring(part, 1, n) for n in (1, 2, 3)], [])
    ahead, behind = ring(part, 0, 1), ring(part, 0, -1)
    weights = [[part, ahead, behind, ring(behind[:2], 0, -1), ring(ahead[2:], 0, 1)]]
    part = join(first, [part], slice(HEAD_DIM, HALF))
    part = join([part] + [ring(part, 1, n) for n in (1, 2, 3)], [ahead, behind])
    weights.append([part, ring(part, 0, 1), ring(part, 0, -1), ring(part, 0, 2)])

    shared = (meta, me, tokens, tokens_t)
    inputs = (queries, cotangent, *swapped[1:], sent_a, sent_b)
    home = [back(SEND_A), back(SEND_B)]

    *results, d0, d1, d3, d2 = run_main(0, *shared, weights[0], *inputs)
    returned = [lax.ppermute(part, DP, pairs) for part, pairs in zip(results[2:], home)]
    parts = exchange([d0, d1, d2, d3], 0)
    *results, d0, d1, d3, far_a, far_b = run_main(1, *shared, weights[1], *inputs, before=results[:2])
    mine, other = results[:2]
    late = [lax.ppermute(part, DP, pairs) for part, pairs in zip(results[2:], home)]

    first = add_parts(parts, [far_a, *returned])
    parts = scatter_ring(d0, d1, d3, far_a, far_b, first[0])
    first = exchange(first, 1)
    second = exchange(add_parts(parts, first[1:]), 1)
    context, grad_queries, finished = finish(info, [mine, swap(other), *returned, *late])
    kept, given = add_last(me, exchange(add_both(first, second, late), 2), [finished])
    got = swap(given)
    grad = jnp.concatenate([jnp.where(c == 0, kept, got), jnp.where(c == 0, got, kept)], axis=1)
    return context, grad_queries, grad


def solution(mesh):
    fine = Mesh(mesh.devices.reshape(4, 4, 2, 4), ALL)
    rows = P(ALL, None)
    cut = P(DP, "x")
    return jax.shard_map(
        body,
        mesh=fine,
        in_specs=(rows, cut, rows, rows, P(), P(), P()),
        out_specs=(rows, rows, cut),
        check_vma=False,
    )
```

```python
import functools

import jax
import jax.numpy as jnp
from jax import lax
from jax.experimental import pallas as pl
from jax.experimental.pallas import tpu as pltpu
from jax.sharding import Mesh, PartitionSpec as P

HEAD_DIM = 256
SEGS = 4
TOK = 512
PAIR = 2 * TOK
WIN = 176
POOL = PAIR + 2 * WIN
D = 2048
HALF = 512
GROUP = 4
DP = ("z", "y", "c")
ALL = ("z", "y", "c", "x")
MIB = 1024 * 1024
BF = jnp.bfloat16


def align(start, limit):
    return jnp.minimum((start // 16) * 16, limit - WIN)


def mm(a, b, dims):
    return lax.dot_general(a, b, (dims, ((), ())), preferred_element_type=jnp.float32)


def attend(meta, k_s, v_s, q_s, ct_s, ctx_s, gq_s, gk_s, gv_s):
    scale = HEAD_DIM ** -0.5
    col = lax.broadcasted_iota(jnp.int32, (WIN, WIN), 1)
    row = lax.broadcasted_iota(jnp.int32, (WIN, WIN), 0)
    row_wide = lax.broadcasted_iota(jnp.int32, (WIN, HEAD_DIM), 0)
    for first in range(0, 2 * SEGS, GROUP):
        spots, loaded, scores = [], [], []
        for e in range(first, first + GROUP):
            es, el, ds, dl = meta[e, 0], meta[e, 1], meta[e, 2], meta[e, 3]
            ew = pl.multiple_of(align(es, PAIR), 16)
            dw = pl.multiple_of(align(ds, POOL), 16)
            spots.append((pl.ds(ew, WIN), pl.ds(dw, WIN), es - ew, el, ds - dw, dl))
        for ewin, dwin, *_ in spots:
            k, v, q, ct = k_s[ewin, :], v_s[ewin, :], q_s[dwin, :], ct_s[dwin, :]
            loaded.append((k, v, q, ct))
            scores.append((mm(q, k, ((1,), (1,))), mm(ct, v, ((1,), (1,)))))
        weights = []
        for (_, _, elo, el, dlo, dl), (s, gw) in zip(spots, scores):
            k_live = (col >= elo) & (col < elo + el)
            q_live = (row[:, :1] >= dlo) & (row[:, :1] < dlo + dl)
            s = jnp.where(k_live, s * scale, -jnp.inf)
            p = jnp.exp(s - jnp.max(s, axis=1, keepdims=True))
            share = jnp.where(q_live, 1.0 / jnp.sum(p, axis=1, keepdims=True), 0.0)
            w = p * share
            delta = jnp.sum(w * gw, axis=1, keepdims=True)
            weights.append((w.astype(BF), (w * (gw - delta) * scale).astype(BF)))
        results = []
        for (k, v, q, ct), (w_low, gs) in zip(loaded, weights):
            results.append((
                mm(w_low, v, ((1,), (0,))).astype(BF),
                mm(gs, k, ((1,), (0,))).astype(BF),
                mm(gs, q, ((0,), (0,))).astype(BF),
                mm(w_low, ct, ((0,), (0,))).astype(BF),
            ))
        for (ewin, dwin, elo, el, dlo, dl), (ctx, gq, gk, gv) in zip(spots, results):
            d_in = (row_wide >= dlo) & (row_wide < dlo + dl)
            e_in = (row_wide >= elo) & (row_wide < elo + el)
            ctx_s[dwin, :] = jnp.where(d_in, ctx, ctx_s[dwin, :])
            gq_s[dwin, :] = jnp.where(d_in, gq, gq_s[dwin, :])
            gk_s[ewin, :] = jnp.where(e_in, gk, gk_s[ewin, :])
            gv_s[ewin, :] = jnp.where(e_in, gv, gv_s[ewin, :])


def places(me):
    z, y, c, x = me[0], me[1], me[2], me[3]

    def block(ra, rb, rc):
        first = c == 0
        bx = (x + jnp.where(first, ra, rb)) & 3
        by = (y + jnp.where(first, rb, rc)) & 3
        bz = (z + jnp.where(first, rc, ra)) & 3
        return bx, bz * 4 + by

    return block


def main_kernel(weights, extra, meta, me, x_ref, xt_ref, *refs):
    qm, qo, qa, qb, cm, co, ca, cb = refs[weights : weights + 8]
    om, oo, oa, ob, d0, d1, d3, *d2 = refs[weights + 8 + extra : -10]
    k_s, v_s, gk_s, gv_s, q_s, ct_s, ctx_s, gq_s, dw_s, w_s = refs[-10:]
    step = pl.program_id(0)
    block = places(me)

    w0, w1, w3, *w2 = refs[:weights]

    @pl.when(step == 0)
    def _():
        def take(rc, carry):
            for rb in range(4):
                far = w2[rb * len(w2) // 4][rb % (4 // len(w2)), rc]
                for ra, value in enumerate((w0[rb, rc], w1[rb, rc], far, w3[rb, rc])):
                    bx, bzy = block(ra, rb, rc)
                    w_s[bx, pl.ds(pl.multiple_of(bzy * 128, 128), 128), :] = value
            return carry

        lax.fori_loop(0, 4, take, 0)

    x = x_ref[...]
    k_s[...] = jnp.dot(x, w_s[step], preferred_element_type=jnp.float32).astype(BF)
    v_s[...] = jnp.dot(x, w_s[2 + step], preferred_element_type=jnp.float32).astype(BF)
    for pool, parts in ((q_s, (qm, qo, qa, qb)), (ct_s, (cm, co, ca, cb))):
        pool[0:TOK, :] = parts[0][...]
        pool[TOK:PAIR, :] = parts[1][...]
        pool[PAIR : PAIR + WIN, :] = parts[2][...]
        pool[PAIR + WIN :, :] = parts[3][...]
    attend(meta, k_s, v_s, q_s, ct_s, ctx_s, gq_s, gk_s, gv_s)
    for kind, pool in enumerate((ctx_s, gq_s)):
        om[kind] = pool[0:TOK, :]
        oo[kind] = pool[TOK:PAIR, :]
        oa[kind] = pool[PAIR : PAIR + WIN, :]
        ob[kind] = pool[PAIR + WIN :, :]
    xt = xt_ref[...]
    dw_s[step] = jnp.dot(xt, gk_s[...], preferred_element_type=jnp.float32).astype(BF)
    dw_s[2 + step] = jnp.dot(xt, gv_s[...], preferred_element_type=jnp.float32).astype(BF)

    @pl.when(step == 1)
    def _():
        def put(rc, carry):
            for rb in range(4):
                for ra, out in ((0, d0), (1, d1), (3, d3), (2, d2[rb * len(d2) // 4])):
                    bx, bzy = block(ra, rb, rc)
                    at = rb % (4 // len(d2)) if ra == 2 else rb
                    out[at, rc] = dw_s[bx, pl.ds(pl.multiple_of(bzy * 128, 128), 128), :]
            return carry

        lax.fori_loop(0, 4, put, 0)


def run_main(chunk, meta, me, x, xt, weights, q, ct, q_other, ct_other, sent_a, sent_b, before=()):
    whole = pl.BlockSpec(memory_space=pltpu.VMEM)

    def wide():
        return pl.BlockSpec((TOK, HEAD_DIM), lambda i, m, e: (0, i * 4 + e[2] * 2 + chunk))

    def narrow(rows, kind):
        return pl.BlockSpec((rows, HEAD_DIM), lambda i, m, e: (0, kind * 4 + i * 2 + chunk))

    def out(rows):
        return pl.BlockSpec((2, rows, HEAD_DIM), lambda i, m, e: (0, 0, i * 2 + chunk))

    def out_far():
        return pl.BlockSpec((2, WIN, HEAD_DIM), lambda i, m, e: (0, 0, i))

    parts = [(4, 4, 128, HEAD_DIM)] * 4 if chunk == 0 else [(4, 4, 128, HEAD_DIM)] * 3 + [(2, 4, 128, HEAD_DIM)] * 2
    anywhere = pl.BlockSpec(memory_space=pl.ANY)
    pair = pltpu.VMEM((PAIR, HEAD_DIM), BF)
    pool = pltpu.VMEM((POOL, HEAD_DIM), BF)
    return pl.pallas_call(
        functools.partial(main_kernel, len(weights), len(before)),
        grid_spec=pltpu.PrefetchScalarGridSpec(
            num_scalar_prefetch=2,
            grid=(2,),
            in_specs=[whole, whole, *[whole for w in weights],
                      wide(), wide(), narrow(WIN, 0), narrow(WIN, 0),
                      wide(), wide(), narrow(WIN, 1), narrow(WIN, 1)]
            + [anywhere] * len(before),
            out_specs=[out(TOK), out(TOK), out_far(), out_far(), *[whole for shape in parts]],
            scratch_shapes=[pair, pair, pair, pair, pool, pool, pool, pool,
                            pltpu.VMEM((4, D, HEAD_DIM), BF), pltpu.VMEM((4, D, HEAD_DIM), BF)],
        ),
        out_shape=[jax.ShapeDtypeStruct((2, TOK, 2 * HALF), BF)] * 2
        + [jax.ShapeDtypeStruct((2, WIN, HALF), BF)] * 2
        + [jax.ShapeDtypeStruct(shape, BF) for shape in parts],
        input_output_aliases={12 + len(weights) + n: n for n in range(len(before))},
        compiler_params=pltpu.CompilerParams(vmem_limit_bytes=32 * MIB),
        cost_estimate=pl.CostEstimate(flops=12_000_000_000, bytes_accessed=24_000_000, transcendentals=500_000),
    )(meta, me, x, xt, *weights, q, q_other, sent_a, sent_b, ct, ct_other, sent_a, sent_b, *before)


def add(refs):
    return sum(ref[...].astype(jnp.float32) for ref in refs)


def add_kernel(count, *refs):
    total = add(refs[:count]).astype(BF)
    for n, out in enumerate(refs[-4:]):
        out[...] = total[n]


def add_parts(parts, after):
    return pl.pallas_call(
        functools.partial(add_kernel, len(parts)),
        grid=(4,),
        in_specs=[pl.BlockSpec((4, 1, 128, HEAD_DIM), lambda i: (0, i, 0, 0))] * len(parts)
        + [pl.BlockSpec(memory_space=pl.ANY)] * len(after),
        out_specs=[pl.BlockSpec((1, 128, HEAD_DIM), lambda i: (i, 0, 0))] * 4,
        out_shape=[jax.ShapeDtypeStruct((4, 128, HEAD_DIM), BF)] * 4,
        compiler_params=pltpu.CompilerParams(vmem_limit_bytes=16 * MIB),
    )(*parts, *after)


def add_both_kernel(*refs):
    for chunk in range(2):
        total = add(refs[chunk * 4 : chunk * 4 + 4]).astype(BF)
        for n, out in enumerate(refs[-4:]):
            out[:, chunk * HEAD_DIM : (chunk + 1) * HEAD_DIM] = total[n]


def add_both(first, second, after):
    whole = pl.BlockSpec(memory_space=pltpu.VMEM)
    return pl.pallas_call(
        add_both_kernel,
        in_specs=[whole] * 8 + [pl.BlockSpec(memory_space=pl.ANY)] * len(after),
        out_specs=[whole] * 4,
        out_shape=[jax.ShapeDtypeStruct((128, HALF), BF)] * 4,
        compiler_params=pltpu.CompilerParams(vmem_limit_bytes=16 * MIB),
    )(*first, *second, *after)


def add_last_kernel(me, *refs):
    kept, given = refs[-2:]
    for row, out in ((me[2], kept), (1 - me[2], given)):
        rows = pl.ds(pl.multiple_of(row * 64, 64), 64)
        out[...] = sum(ref[rows, :].astype(jnp.float32) for ref in refs[:4])


def add_last(me, parts, after):
    whole = pl.BlockSpec(memory_space=pltpu.VMEM)
    return pl.pallas_call(
        add_last_kernel,
        in_specs=[pl.BlockSpec(memory_space=pltpu.SMEM)] + [whole] * 4
        + [pl.BlockSpec(memory_space=pl.ANY)] * len(after),
        out_specs=[whole] * 2,
        out_shape=[jax.ShapeDtypeStruct((64, HALF), jnp.float32)] * 2,
        compiler_params=pltpu.CompilerParams(vmem_limit_bytes=16 * MIB),
    )(me, *parts, *after)


def depart_kernel(me, enc_len, dec_len, partner, q_ref, ct_ref, meta, info, a_ref, b_ref, sems):
    core, x = me[2], me[3]
    t = me[0] * 4 + me[1]

    info[0], info[1], info[2], info[3] = jnp.int32(0), core, jnp.int32(0), jnp.int32(0)
    device = (t * 2 + core) * 4 + x
    start = jnp.int32(0)
    for slot in range(SEGS):
        begin, length = start, dec_len[slot, device]

        @pl.when((partner[slot, device] >> 5) != t)
        def _():
            info[0] = align(begin, TOK)
            info[2] = begin
            info[3] = length

        start = start + length

    rows = pl.ds(pl.multiple_of(info[0], 16), WIN)
    copies = []
    for n in range(4):
        source = (q_ref, ct_ref)[n // 2]
        for side, out in ((core, a_ref), (1 - core, b_ref)):
            begin = pl.ds(pl.multiple_of((n % 2) * 1024 + side * HALF, HALF), HALF)
            copies.append((source.at[rows, begin], out.at[:, pl.ds(n * HALF, HALF)]))
    copies = [pltpu.make_async_copy(a, b, sems.at[n]) for n, (a, b) in enumerate(copies)]
    for copy in copies:
        copy.start()

    for side in range(2):
        device = (t * 2 + (core if side == 0 else 1 - core)) * 4 + x
        start = jnp.int32(side * TOK)
        for slot in range(SEGS):
            meta[side * SEGS + slot, 0] = start
            meta[side * SEGS + slot, 1] = enc_len[slot, device]
            start = start + enc_len[slot, device]
    for near in range(4):
        dp = t * 2 - 1 + near
        device = jnp.clip(dp, 0, 31) * 4 + x
        real = (dp >= 0) & (dp < 32)
        same = (dp & 1) == core
        start = jnp.int32(0)
        for slot in range(SEGS):
            begin, length = start, dec_len[slot, device]
            owner = partner[slot, device] >> 4
            if near in (1, 2):
                at = begin + jnp.where(same, 0, TOK)
            else:
                at = begin - align(begin, TOK) + PAIR + jnp.where(same, 0, WIN)

            @pl.when(real & ((owner >> 1) == t))
            def _():
                entry = jnp.where((owner & 1) == core, 0, SEGS) + (partner[slot, device] & 3)
                meta[entry, 2] = at
                meta[entry, 3] = length

            start = start + length
    for copy in copies:
        copy.wait()


def depart(me, enc_lengths, dec_lengths, dec_partner, q, ct):
    whole = pl.BlockSpec(memory_space=pl.ANY)
    scalar = pl.BlockSpec(memory_space=pltpu.SMEM)
    return pl.pallas_call(
        depart_kernel,
        in_specs=[scalar, scalar, scalar, scalar, whole, whole],
        out_specs=[scalar, scalar, pl.BlockSpec(memory_space=pltpu.VMEM), pl.BlockSpec(memory_space=pltpu.VMEM)],
        scratch_shapes=[pltpu.SemaphoreType.DMA((8,))],
        out_shape=[jax.ShapeDtypeStruct((2 * SEGS, 4), jnp.int32), jax.ShapeDtypeStruct((4,), jnp.int32)]
        + [jax.ShapeDtypeStruct((WIN, 2048), BF)] * 2,
        compiler_params=pltpu.CompilerParams(vmem_limit_bytes=59 * MIB),
    )(me, enc_lengths.T, dec_lengths.T, dec_partner.T, q, ct)


def turn_kernel(a_ref, b_ref, *refs):
    x_ref, xt_ref, mark = refs[-3:]
    mark[...] = jnp.zeros_like(mark)
    for n, ref in enumerate((a_ref, b_ref)):
        value = ref[...]
        x_ref[n * TOK : (n + 1) * TOK, :] = value
        xt_ref[:, n * TOK : (n + 1) * TOK] = value.T


def turn(a, b, after):
    part = pl.BlockSpec((TOK, 512), lambda i: (0, i))
    return pl.pallas_call(
        turn_kernel,
        grid=(D // 512,),
        in_specs=[part, part]
        + [pl.BlockSpec(memory_space=pl.ANY)] * len(after),
        out_specs=[pl.BlockSpec((PAIR, 512), lambda i: (0, i)), pl.BlockSpec((512, PAIR), lambda i: (i, 0)),
                   pl.BlockSpec((8, 128), lambda i: (0, 0))],
        out_shape=[jax.ShapeDtypeStruct((PAIR, D), BF), jax.ShapeDtypeStruct((D, PAIR), BF),
                   jax.ShapeDtypeStruct((8, 128), jnp.float32)],
        compiler_params=pltpu.CompilerParams(vmem_limit_bytes=16 * MIB),
    )(a, b, *after)


def finish_kernel(info, *refs):
    ins, outs, mark = refs[:6], refs[6:8], refs[8]
    mark[...] = jnp.zeros_like(mark)
    win = pl.multiple_of(info[0], 16)
    core, start, length = info[1], info[2] - info[0], info[3]
    rows = pl.ds(win, WIN)
    place = lax.broadcasted_iota(jnp.int32, (WIN, HEAD_DIM), 0)
    inside = (place >= start) & (place < start + length)
    mine, theirs, *returned = ins
    for side, base, first in ((core, mine, 0), (1 - core, theirs, 1)):
        for chunk in range(2):
            cols = pl.ds(pl.multiple_of(side * HALF + chunk * HEAD_DIM, HEAD_DIM), HEAD_DIM)
            for kind, out in enumerate(outs):
                out[:, cols] = base[kind, :, chunk * HEAD_DIM : (chunk + 1) * HEAD_DIM]
                out[rows, cols] = jnp.where(inside, returned[chunk * 2 + first][kind], out[rows, cols])


def finish(info, pieces):
    def source(rows, cols):
        return pl.BlockSpec((2, rows, cols), lambda i, e: (0, 0, i))

    out = pl.BlockSpec((TOK, 1024), lambda i, e: (0, i))
    return pl.pallas_call(
        finish_kernel,
        grid_spec=pltpu.PrefetchScalarGridSpec(
            num_scalar_prefetch=1,
            grid=(2,),
            in_specs=[source(TOK, HALF)] * 2 + [source(WIN, HEAD_DIM)] * 4,
            out_specs=[out, out, pl.BlockSpec((8, 128), lambda i, e: (0, 0))],
        ),
        out_shape=[jax.ShapeDtypeStruct((TOK, 2048), BF)] * 2 + [jax.ShapeDtypeStruct((8, 128), jnp.float32)],
        compiler_params=pltpu.CompilerParams(vmem_limit_bytes=24 * MIB),
    )(info, *pieces)


def swap(value):
    return lax.ppermute(value, "c", [(0, 1), (1, 0)])


SEND_A = [(2 * t, 2 * t - 2) for t in range(1, 16)] + [(2 * t + 1, 2 * t + 3) for t in range(15)]
SEND_B = [(2 * t, 2 * t - 1) for t in range(1, 16)] + [(2 * t + 1, 2 * t + 2) for t in range(15)]


def back(pairs):
    return [(b, a) for a, b in pairs]


def shift(phase, amount):
    pairs = []
    for z in range(4):
        for y in range(4):
            for c in range(2):
                for x in range(4):
                    to = {"z": z, "y": y, "x": x}
                    axis = ("xyz", "zxy")[c][phase]
                    to[axis] = (to[axis] + amount) % 4
                    pairs.append((((z * 4 + y) * 2 + c) * 4 + x, ((to["z"] * 4 + to["y"]) * 2 + c) * 4 + to["x"]))
    return pairs


def exchange(parts, phase):
    return [parts[0]] + [lax.ppermute(parts[r], ALL, shift(phase, r)) for r in (2, 1, 3)]


def join_kernel(cols, *refs):
    for n, place in enumerate((0, 1, 3, 2)):
        refs[-1][place] = refs[n][..., cols]


def join(parts, after, cols=slice(0, HEAD_DIM)):
    whole = pl.BlockSpec(memory_space=pltpu.VMEM)
    return pl.pallas_call(
        functools.partial(join_kernel, cols),
        in_specs=[whole] * 4 + [pl.BlockSpec(memory_space=pl.ANY)] * len(after),
        out_specs=whole,
        out_shape=jax.ShapeDtypeStruct((4,) + parts[0].shape[:-1] + (HEAD_DIM,), BF),
        compiler_params=pltpu.CompilerParams(vmem_limit_bytes=16 * MIB),
    )(*parts, *after)


def pick_kernel(me, w_ref, got_ref, *refs):
    out_ref = refs[-1]
    mine = w_ref[:, pl.ds(pl.multiple_of(me[2] * HALF, HALF), HALF)]
    for core in range(2):

        @pl.when(me[2] == core)
        def _():
            out_ref[core * 64 : core * 64 + 64, :] = mine
            out_ref[64 - core * 64 : 128 - core * 64, :] = got_ref[...]


def pick(me, weights, got, after):
    whole = pl.BlockSpec(memory_space=pltpu.VMEM)
    return pl.pallas_call(
        pick_kernel,
        in_specs=[pl.BlockSpec(memory_space=pltpu.SMEM), whole, whole]
        + [pl.BlockSpec(memory_space=pl.ANY)] * len(after),
        out_specs=whole,
        out_shape=jax.ShapeDtypeStruct((128, HALF), BF),
        compiler_params=pltpu.CompilerParams(vmem_limit_bytes=16 * MIB),
    )(me, weights, got, *after)


def ring(value, phase, amount):
    return lax.ppermute(value, ALL, shift(phase, -amount))


def fold_kernel(a_ref, b_ref, got_a, got_b, after, out_a, out_b):
    for ref, got, out in ((a_ref, got_a, out_a), (b_ref, got_b, out_b)):
        out[...] = (ref[...].astype(jnp.float32) + got[...].astype(jnp.float32)).astype(BF)


def fold(ahead, behind, got_a, got_b, after):
    def block(start):
        return pl.BlockSpec((1, 4, 128, HEAD_DIM), lambda i: (i + start, 0, 0, 0))

    whole = jax.ShapeDtypeStruct(ahead.shape, BF)
    return pl.pallas_call(
        fold_kernel,
        grid=(2,),
        in_specs=[block(0), block(2), block(0), block(0), pl.BlockSpec(memory_space=pl.ANY)],
        out_specs=[block(0), block(2)],
        out_shape=[whole, whole],
        input_output_aliases={0: 0, 1: 1},
        compiler_params=pltpu.CompilerParams(vmem_limit_bytes=16 * MIB),
    )(ahead, behind, got_a, got_b, after)


def scatter_ring(own, ahead, behind, far_a, far_b, after):
    got_a = lax.ppermute(far_a, ALL, shift(0, 1))
    got_b = lax.ppermute(far_b, ALL, shift(0, -1))
    ahead, behind = fold(ahead, behind, got_a, got_b, after)
    return [own, lax.ppermute(ahead, ALL, shift(0, 1)), lax.ppermute(behind, ALL, shift(0, -1))]


def body(enc_hidden, kv_weights, queries, cotangent, enc_lengths, dec_lengths, dec_partner):
    z, y, c, x = (lax.axis_index(a) for a in ALL)
    me = jnp.stack([z, y, c, x]).astype(jnp.int32)
    swapped = [swap(value) for value in (enc_hidden, queries, cotangent)]
    meta, info, leave_a, leave_b = depart(me, enc_lengths, dec_lengths, dec_partner, queries, cotangent)
    sent_a = lax.ppermute(leave_a, DP, SEND_A)
    sent_b = lax.ppermute(leave_b, DP, SEND_B)

    got = swap(jnp.where(c == 0, kv_weights[:, HALF:], kv_weights[:, :HALF]))
    own = pick(me, kv_weights, got, [info, *swapped])
    first = [own] + [ring(own, 2, n) for n in (1, 3, 2)]
    tokens, tokens_t, turned = turn(enc_hidden, swapped[0], [first[3]])
    part = join(first, [turned, sent_a, sent_b])
    part = join([part] + [ring(part, 1, n) for n in (1, 3, 2)], [])
    ahead, behind = ring(part, 0, 1), ring(part, 0, -1)
    weights = [[part, ahead, behind, ring(behind[:2], 0, -1), ring(ahead[2:], 0, 1)]]
    part = join(first, [part], slice(HEAD_DIM, HALF))
    part = join([part] + [ring(part, 1, n) for n in (1, 3, 2)], [ahead, behind])
    weights.append([part, ring(part, 0, 1), ring(part, 0, -1), ring(part, 0, 2)])

    shared = (meta, me, tokens, tokens_t)
    inputs = (queries, cotangent, *swapped[1:], sent_a, sent_b)
    home = [back(SEND_A), back(SEND_B)]

    *results, d0, d1, d3, d2 = run_main(0, *shared, weights[0], *inputs)
    returned = [lax.ppermute(part, DP, pairs) for part, pairs in zip(results[2:], home)]
    parts = exchange([d0, d1, d2, d3], 0)
    *results, d0, d1, d3, far_a, far_b = run_main(1, *shared, weights[1], *inputs, before=results[:2])
    mine, other = results[:2]
    late = [lax.ppermute(part, DP, pairs) for part, pairs in zip(results[2:], home)]

    first = add_parts(parts, [far_a, *returned])
    parts = scatter_ring(d0, d1, d3, far_a, far_b, first[0])
    first = exchange(first, 1)
    second = exchange(add_parts(parts, first[1:]), 1)
    context, grad_queries, finished = finish(info, [mine, swap(other), *returned, *late])
    kept, given = add_last(me, exchange(add_both(first, second, late), 2), [finished])
    got = swap(given)
    grad = jnp.concatenate([jnp.where(c == 0, kept, got), jnp.where(c == 0, got, kept)], axis=1)
    return context, grad_queries, grad


def solution(mesh):
    fine = Mesh(mesh.devices.reshape(4, 4, 2, 4), ALL)
    rows = P(ALL, None)
    cut = P(DP, "x")
    return jax.shard_map(
        body,
        mesh=fine,
        in_specs=(rows, cut, rows, rows, P(), P(), P()),
        out_specs=(rows, rows, cut),
        check_vma=False,
    )
```
